32 devices in a mesh: dp: 8 (over y, x, core), seq: 4 (over z).
Axes of the slice: x: 2, y: 2, z: 4, core: 2. Of those that a mesh axis runs over, the one named last changes fastest.
Arguments:
- tokens: bfloat16 [15360, 768], P(('dp', 'seq')), may hold values from -6 to 6
- cotangent: bfloat16 [15360, 768], P(('dp', 'seq')), may hold values from -6 to 6
- doc_lengths: int32 [8, 8], P('dp'), may hold values from 1 to 960, 1920 in all within a row
- pad_counts: int32 [8], P('dp'), may hold values from 0 to 479
- w_in: float32 [2, 2304, 768], P(None, ('dp', 'seq')), may hold values from -0.21875 to 0.21875
- w_ao: float32 [768, 768], P(('dp', 'seq')), may hold values from -3.5 to 3.5
- w_fo: float32 [768, 1152], P(('dp', 'seq')), may hold values from -0.1875 to 0.1875
- norm_gains: float32 [2, 768], P(None, ('dp', 'seq')), may hold values from 0.5 to 1.5
- gain_moment: float32 [2, 768], P(None, ('dp', 'seq'))
- gain_second: float32 [2, 768], P(None, ('dp', 'seq')), as said below
- stat_l_in: float32 [2, 2304, 2304], P(None, ('dp', 'seq')), as said below
- stat_r_in: float32 [2, 768, 768], P(None, ('dp', 'seq')), as said below
- stat_l_ao: float32 [768, 768], P(('dp', 'seq')), as said below
- stat_r_ao: float32 [768, 768], P(('dp', 'seq')), as said below
- stat_l_fo: float32 [768, 768], P(('dp', 'seq')), as said below
- stat_r_fo: float32 [1152, 1152], P(('dp', 'seq')), as said below
- root_l_in: float32 [2, 2304, 2304], P(None, ('dp', 'seq')), as said below
- root_r_in: float32 [2, 768, 768], P(None, ('dp', 'seq')), as said below
- root_l_ao: float32 [768, 768], P(('dp', 'seq')), as said below
- root_r_ao: float32 [768, 768], P(('dp', 'seq')), as said below
- root_l_fo: float32 [768, 768], P(('dp', 'seq')), as said below
- root_r_fo: float32 [1152, 1152], P(('dp', 'seq')), as said below
Outputs:
- layer_out: bfloat16 [15360, 768], P(('dp', 'seq'))
- grad_input: float32 [15360, 768], P(('dp', 'seq'))
- grad_w_in: float32 [2, 2304, 768], P(None, ('dp', 'seq'))
- grad_w_ao: float32 [768, 768], P(('dp', 'seq'))
- grad_w_fo: float32 [768, 1152], P(('dp', 'seq'))
- grad_gains: float32 [2, 768], P(None, ('dp', 'seq'))
- new_gain_moment: float32 [2, 768], P(None, ('dp', 'seq'))
- new_gain_second: float32 [2, 768], P(None, ('dp', 'seq'))
- new_gains: float32 [2, 768], P(None, ('dp', 'seq'))
- new_stat_l_in: float32 [2, 2304, 2304], P(None, ('dp', 'seq'))
- new_stat_r_in: float32 [2, 768, 768], P(None, ('dp', 'seq'))
- new_stat_l_ao: float32 [768, 768], P(('dp', 'seq'))
- new_stat_r_ao: float32 [768, 768], P(('dp', 'seq'))
- new_stat_l_fo: float32 [768, 768], P(('dp', 'seq'))
- new_stat_r_fo: float32 [1152, 1152], P(('dp', 'seq'))
- new_w_in: float32 [2, 2304, 768], P(None, ('dp', 'seq'))
- new_w_ao: float32 [768, 768], P(('dp', 'seq'))
- new_w_fo: float32 [768, 1152], P(('dp', 'seq'))
The draws below stay inside these ranges and needn't reach their ends.
Inputs may be any that keep to these rules, and one draw needn't show every extreme that they name: `doc_lengths`: each row's 8 lengths sum to 1920; the longest of each row is exactly 960. `gain_second`: positive. `stat_l_in`: symmetric in its last two dimensions. `stat_r_in`: symmetric in its last two dimensions. `stat_l_ao`: symmetric. `stat_r_ao`: symmetric. `stat_l_fo`: symmetric. `stat_r_fo`: symmetric. `root_l_in`: symmetric in its last two dimensions. `root_r_in`: symmetric in its last two dimensions. `root_l_ao`: symmetric. `root_r_ao`: symmetric. `root_l_fo`: symmetric. `root_r_fo`: symmetric.
All inputs are finite; a program needn't handle non-finite values.
Results may differ from the reference program's by a relative error of at most 0.013.
The reference program's roundings to bfloat16 on the way count: a program that leaves them out, or rounds other values in their place, can miss the bound.
Values may be sent and summed in bfloat16 or wider, within the bound.
No kernel may reach another device: no remote copies, remote signals or barrier semaphores. Data moves between devices by JAX's collectives and lax.ppermute only.
A program may use at most 256 MiB of HBM per device.

```python
import math
import jax
import jax.numpy as jnp
import numpy as np
from jax import lax

D = 768
FF = 1152
HEAD_DIM = 64
TOK_DEV = 480
NDOC = 8
ROW = 1920
ROWS = 8
TOKENS = 15360
N_SEQ = 4


def grad_size(factor):
    return factor * math.sqrt(TOKENS)


def attend_factor():
    return 1.5 * math.sqrt(NDOC / ROW)


def out_spread():
    return 1.0 / math.sqrt(max(1, D * NDOC // ROW))


def symmetric_draw(key, lead_shape, order, base):
    key_off, key_diag = jax.random.split(key)
    noise = jax.random.normal(key_off, lead_shape + (order, order), jnp.float32)
    paired = (noise + jnp.swapaxes(noise, -1, -2)) * 0.7071
    rows_at = jnp.arange(order)[:, None]
    cols_at = jnp.arange(order)[None, :]
    identity_mask = (rows_at == cols_at).astype(jnp.float32)
    diag_scale = jax.random.uniform(key_diag, lead_shape + (order, 1), jnp.float32, 1.0, 2.0)
    return base * (identity_mask * diag_scale + (1.0 - identity_mask) * paired * (0.4 / math.sqrt(order)))


def root_base(weight_spread, factor):
    return math.sqrt(weight_spread / grad_size(factor))


def gain_rows():
    return jnp.array([[1.0], [1.7]], jnp.float32) * grad_size(1.0)


def draw_stat_l_in(key, part):
    scale_g = grad_size(0.5)
    return symmetric_draw(jax.random.fold_in(key, 101), (2,), 3 * D, scale_g * scale_g * D)


def draw_stat_r_in(key, part):
    scale_g = grad_size(0.5)
    return symmetric_draw(jax.random.fold_in(key, 102), (2,), D, scale_g * scale_g * 3 * D)


def draw_stat_l_ao(key, part):
    scale_g = grad_size(attend_factor())
    return symmetric_draw(jax.random.fold_in(key, 103), (), D, scale_g * scale_g * D)


def draw_stat_r_ao(key, part):
    scale_g = grad_size(attend_factor())
    return symmetric_draw(jax.random.fold_in(key, 104), (), D, scale_g * scale_g * D)


def draw_stat_l_fo(key, part):
    scale_g = grad_size(0.5)
    return symmetric_draw(jax.random.fold_in(key, 105), (), D, scale_g * scale_g * FF)


def draw_stat_r_fo(key, part):
    scale_g = grad_size(0.5)
    return symmetric_draw(jax.random.fold_in(key, 106), (), FF, scale_g * scale_g * D)


def draw_root_l_in(key, part):
    return symmetric_draw(jax.random.fold_in(key, 107), (2,), 3 * D, root_base(1.0 / math.sqrt(D), 0.5))


def draw_root_r_in(key, part):
    return symmetric_draw(jax.random.fold_in(key, 108), (2,), D, root_base(1.0 / math.sqrt(D), 0.5))


def draw_root_l_ao(key, part):
    return symmetric_draw(jax.random.fold_in(key, 109), (), D, root_base(out_spread(), attend_factor()))


def draw_root_r_ao(key, part):
    return symmetric_draw(jax.random.fold_in(key, 110), (), D, root_base(out_spread(), attend_factor()))


def draw_root_l_fo(key, part):
    return symmetric_draw(jax.random.fold_in(key, 111), (), D, root_base(1.0 / math.sqrt(FF), 0.5))


def draw_root_r_fo(key, part):
    return symmetric_draw(jax.random.fold_in(key, 112), (), FF, root_base(1.0 / math.sqrt(FF), 0.5))


def draw_gain_moment(key, part):
    noise = jax.random.normal(jax.random.fold_in(key, 113), (2, D), jnp.float32)
    return 0.11 * gain_rows() * noise


def draw_gain_second(key, part):
    factor_draw = jax.random.uniform(jax.random.fold_in(key, 114), (2, D), jnp.float32, 1.0, 4.0)
    scale_g = gain_rows()
    return 0.001 * scale_g * scale_g * factor_draw


def place_ends(values, stream_key, least, high):
    shape = values.shape
    index_at = [jax.random.randint(jax.random.fold_in(stream_key, axis), (), 0, shape[axis]) for axis in range(len(shape))]
    values = values.at[tuple(index_at)].set(least)
    longest = shape.index(max(shape))
    index_at[longest] = (index_at[longest] + 1) % shape[longest]
    return values.at[tuple(index_at)].set(high)


def shard_levels(stream_key, extent, shards, smallest, largest):
    def one(axis_at, shards_of):
        steps = jax.random.uniform(jax.random.fold_in(jax.random.fold_in(stream_key, 6), axis_at), (shards_of,), jnp.float32, smallest / len(shards), largest / len(shards))
        return jnp.repeat(jnp.exp(steps), extent[axis_at] // shards_of).reshape((-1,) + (1,) * (len(extent) - axis_at - 1))

    loudness = one(*shards[0])
    for cut in shards[1:]:
        loudness = loudness * one(*cut)
    return loudness


def split_up(count, total, bound, slope):
    portions = [(1 << 20) // math.isqrt(rank ** slope) + 1 for rank in range(2, count + 1)]
    surplus, holding = total - bound - (count - 1), [1] * (count - 1)
    while surplus > 0:
        movable = [i for i in range(count - 1) if holding[i] < bound]
        pool, left = sum([portions[i] for i in movable]), surplus
        for i in movable:
            extra = min(bound - holding[i], max(1, left * portions[i] // pool), surplus)
            holding[i] = holding[i] + extra
            surplus = surplus - extra
    return np.array([bound] + holding)


def ragged(key, amount, total, reach, slope):
    if amount == 2:
        one = jax.random.randint(key, (), max(1, total - reach), min(reach, total - 1) + 1)
        return jnp.stack([one, total - one])
    sizes = jnp.asarray(split_up(amount, total, reach, slope), jnp.int32)
    pairs = (amount - 1) // 2
    giver, receiver = sizes[1:1 + 2 * pairs:2], sizes[2:2 + 2 * pairs:2]
    room = jnp.minimum(giver - 1, reach - receiver)
    moved = jax.random.randint(jax.random.fold_in(key, 1), (pairs,), 0, 1 << 20) % (room + 1)
    sizes = sizes.at[1:1 + 2 * pairs:2].set(giver - moved).at[2:2 + 2 * pairs:2].set(receiver + moved)
    return sizes[jax.random.permutation(jax.random.fold_in(key, 2), amount)]


def scatter_about(stream_key, extent, scale, reach, cuts=(), held_as=jnp.bfloat16):
    level = shard_levels(stream_key, extent, cuts, -0.22, 0.18) if cuts else 1.0
    values = jax.random.normal(stream_key, extent, jnp.float32) * scale * level
    return jnp.minimum(jnp.maximum(values, -reach), reach).astype(held_as)


def setup_inputs(seed: int = 0) -> dict:
    splits = jax.random.split(jax.random.key(seed), 23)
    return {
        "tokens": scatter_about(splits[0], (TOKENS, D), 1.0, 6.0, ((0, 32),)),
        "cotangent": scatter_about(splits[1], (TOKENS, D), 1.0, 6.0, ((0, 32),)),
        "doc_lengths": jax.vmap(lambda own: ragged(own, NDOC, ROW, ROW // 2, 2))(jax.random.split(splits[2], ROWS)).reshape((ROWS, NDOC)).astype(jnp.int32),
        "pad_counts": place_ends(jax.random.randint(splits[3], (ROWS,), 0, TOK_DEV), jax.random.fold_in(splits[3], 1), 0, TOK_DEV - 1).astype(jnp.int32),
        "w_in": scatter_about(splits[4], (2, 3 * D, D), D ** -0.5, 0.21875, ((1, 32),), jnp.float32),
        "w_ao": scatter_about(splits[5], (D, D), (max(1, D * NDOC // ROW)) ** -0.5, 3.5, ((0, 32),), jnp.float32),
        "w_fo": scatter_about(splits[6], (D, FF), FF ** -0.5, 0.1875, ((0, 32),), jnp.float32),
        "norm_gains": jnp.clip(1.0 + 0.1 * jax.random.normal(splits[7], (2, D), jnp.float32), 0.5, 1.5),
        "gain_moment": draw_gain_moment(jax.random.fold_in(splits[22], 71), 0),
        "gain_second": draw_gain_second(jax.random.fold_in(splits[22], 71), 0),
        "stat_l_in": draw_stat_l_in(jax.random.fold_in(splits[22], 71), 0),
        "stat_r_in": draw_stat_r_in(jax.random.fold_in(splits[22], 71), 0),
        "stat_l_ao": draw_stat_l_ao(jax.random.fold_in(splits[22], 71), 0),
        "stat_r_ao": draw_stat_r_ao(jax.random.fold_in(splits[22], 71), 0),
        "stat_l_fo": draw_stat_l_fo(jax.random.fold_in(splits[22], 71), 0),
        "stat_r_fo": draw_stat_r_fo(jax.random.fold_in(splits[22], 71), 0),
        "root_l_in": draw_root_l_in(jax.random.fold_in(splits[22], 71), 0),
        "root_r_in": draw_root_r_in(jax.random.fold_in(splits[22], 71), 0),
        "root_l_ao": draw_root_l_ao(jax.random.fold_in(splits[22], 71), 0),
        "root_r_ao": draw_root_r_ao(jax.random.fold_in(splits[22], 71), 0),
        "root_l_fo": draw_root_l_fo(jax.random.fold_in(splits[22], 71), 0),
        "root_r_fo": draw_root_r_fo(jax.random.fold_in(splits[22], 71), 0),
    }


@jax.custom_vjp
def low(v):
    return lax.optimization_barrier(v.astype(jnp.bfloat16)).astype(jnp.float32)

@jax.custom_vjp
def low_back(v):
    return v

def low_keep(v):
    return (low(v), None)

def low_pass(kept, grad):
    return (grad,)

def back_keep(v):
    return (v, None)

def back_low(kept, grad):
    return (low(grad),)
low.defvjp(low_keep, low_pass)
low_back.defvjp(back_keep, back_low)
NORM_EPS = 1e-05
ROPE_THETA = 160000.0
SCORE_SCALE = 0.125
MASK_FILL = -1e+30
ADAM_RATE = 0.2
SHAMPOO_RATE = 1.0
HIGHEST = lax.Precision.HIGHEST

def layer_norm(values, gain_row):
    center = values - lax.optimization_barrier(jnp.mean(values, axis=-1, keepdims=True))
    spread = lax.optimization_barrier(jnp.mean(center * center, axis=-1, keepdims=True))
    return center * lax.rsqrt(spread + NORM_EPS) * gain_row

def gelu_value(inputs):
    return 0.5 * inputs * (1.0 + lax.erf(inputs * (1.0 / math.sqrt(2.0))))

def rotate(values, cos_table, sin_table):
    half_dim = values.shape[-1] // 2
    turned = jnp.concatenate([-values[..., half_dim:], values[..., :half_dim]], axis=-1)
    return values * cos_table + turned * sin_table

def rope_tables(within):
    freq_index = jnp.arange(0, HEAD_DIM, 2, dtype=jnp.float32)
    inverse = 1.0 / jnp.power(ROPE_THETA, freq_index / HEAD_DIM)
    angles = within.astype(jnp.float32)[:, None] * inverse[None, :]
    angles = jnp.concatenate([angles, angles], axis=-1)
    return (jnp.cos(angles), jnp.sin(angles))

def doc_tables(lengths_row, pad_count, row_length):
    doc_ends = jnp.cumsum(lengths_row).astype(jnp.int32)
    starts = doc_ends - lengths_row
    places = jnp.arange(row_length, dtype=jnp.int32)
    segment = lax.optimization_barrier(jnp.sum((places[:, None] >= doc_ends[None, :]).astype(jnp.int32), axis=1))
    doc_ids = jnp.arange(lengths_row.shape[0], dtype=jnp.int32)
    doc_begin = lax.optimization_barrier(jnp.sum(jnp.where(segment[:, None] == doc_ids[None, :], starts[None, :], 0), axis=1))
    is_valid = places < row_length - pad_count
    return (segment, places - doc_begin, is_valid)

def head_attention(query_head, key_head, value_head, allowed):
    scores = jnp.dot(query_head, key_head.T, precision=HIGHEST, preferred_element_type=jnp.float32) * SCORE_SCALE
    scores = low_back(jnp.where(allowed, scores, MASK_FILL))
    row_max = lax.optimization_barrier(jnp.max(scores, axis=-1, keepdims=True))
    exponent = jnp.exp(scores - row_max)
    softmax_out = exponent / lax.optimization_barrier(jnp.sum(exponent, axis=-1, keepdims=True))
    return jnp.dot(low(softmax_out), value_head, precision=HIGHEST, preferred_element_type=jnp.float32)

def row_attention(packed):
    query_row, key_row, value_row, segment, is_valid = packed
    places = jnp.arange(segment.shape[0], dtype=jnp.int32)
    allowed = (segment[:, None] == segment[None, :]) & (is_valid[None, :] | (places[:, None] == places[None, :]))
    checked_head = jax.checkpoint(head_attention)

    def one_head(head_parts):
        return checked_head(head_parts[0], head_parts[1], head_parts[2], allowed)
    return lax.map(one_head, (query_row, key_row, value_row))

def forward(inputs, w_in, w_ao, w_fo, norm_gains, segments, withins, valid_rows):
    token_count, model_width = inputs.shape
    head_count = model_width // HEAD_DIM
    row_count, row_length = segments.shape
    gains_low = low(norm_gains)
    attn_in = low(layer_norm(inputs, gains_low[0]))
    qkv_raw = low_back(jnp.dot(attn_in, low(w_in[0]).T, precision=HIGHEST, preferred_element_type=jnp.float32))
    cos_table, sin_table = rope_tables(withins.reshape(-1))
    cos_table = cos_table[:, None, :]
    sin_table = sin_table[:, None, :]
    query_all = low(rotate(qkv_raw[:, :model_width].reshape(token_count, head_count, HEAD_DIM), cos_table, sin_table))
    key_all = low(rotate(qkv_raw[:, model_width:2 * model_width].reshape(token_count, head_count, HEAD_DIM), cos_table, sin_table))
    value_all = low(qkv_raw[:, 2 * model_width:].reshape(token_count, head_count, HEAD_DIM))

    def by_rows(tensor):
        return jnp.transpose(tensor.reshape(row_count, row_length, head_count, HEAD_DIM), (0, 2, 1, 3))
    attended = lax.map(row_attention, (by_rows(query_all), by_rows(key_all), by_rows(value_all), segments, valid_rows))
    attended = jnp.transpose(attended, (0, 2, 1, 3)).reshape(token_count, model_width)
    attn_low = low_back(low(attended))
    residual = inputs + low_back(jnp.dot(attn_low, low(w_ao).T, precision=HIGHEST, preferred_element_type=jnp.float32))
    ffn_in = low(layer_norm(residual, gains_low[1]))
    projected = low_back(jnp.dot(ffn_in, low(w_in[1]).T, precision=HIGHEST, preferred_element_type=jnp.float32))
    hidden_width = projected.shape[1] // 2
    mid_low = low(gelu_value(projected[:, :hidden_width]) * projected[:, hidden_width:])
    return residual + low_back(jnp.dot(mid_low, low(w_fo).T, precision=HIGHEST, preferred_element_type=jnp.float32))

def shampoo(weight, gradient, stat_left, stat_right, root_left, root_right):
    new_left = 0.5 * stat_left + 0.5 * jnp.dot(gradient, gradient.T, precision=HIGHEST)
    new_right = 0.5 * stat_right + 0.5 * jnp.dot(gradient.T, gradient, precision=HIGHEST)
    update = jnp.dot(jnp.dot(root_left, gradient, precision=HIGHEST), root_right, precision=HIGHEST)
    return (new_left, new_right, weight - SHAMPOO_RATE * update)

def reference(tokens, cotangent, doc_lengths, pad_counts, w_in, w_ao, w_fo, norm_gains, gain_moment, gain_second, stat_l_in, stat_r_in, stat_l_ao, stat_r_ao, stat_l_fo, stat_r_fo, root_l_in, root_r_in, root_l_ao, root_r_ao, root_l_fo, root_r_fo):
    row_length = TOK_DEV * N_SEQ
    segments, withins, valid_rows = jax.vmap(lambda lengths_row, pad_count: doc_tables(lengths_row, pad_count, row_length))(doc_lengths, pad_counts)

    def closed(inputs, weight_in, weight_ao, weight_fo, gain_arg):
        return forward(inputs, weight_in, weight_ao, weight_fo, gain_arg, segments, withins, valid_rows)
    result, pullback = jax.vjp(closed, tokens.astype(jnp.float32), w_in, w_ao, w_fo, norm_gains)
    grad_input, grad_w_in, grad_w_ao, grad_w_fo, grad_gains = pullback(cotangent.astype(jnp.float32))
    new_moment = 0.9 * gain_moment + 0.1 * grad_gains
    new_second = 0.999 * gain_second + 0.001 * grad_gains * grad_gains
    new_gains = norm_gains - ADAM_RATE * new_moment / (jnp.sqrt(new_second) + 1e-08)
    parts_in = [shampoo(w_in[matrix_index], grad_w_in[matrix_index], stat_l_in[matrix_index], stat_r_in[matrix_index], root_l_in[matrix_index], root_r_in[matrix_index]) for matrix_index in range(2)]
    new_l_in = jnp.stack([parts_in[0][0], parts_in[1][0]])
    new_r_in = jnp.stack([parts_in[0][1], parts_in[1][1]])
    new_w_in = jnp.stack([parts_in[0][2], parts_in[1][2]])
    new_l_ao, new_r_ao, new_w_ao = shampoo(w_ao, grad_w_ao, stat_l_ao, stat_r_ao, root_l_ao, root_r_ao)
    new_l_fo, new_r_fo, new_w_fo = shampoo(w_fo, grad_w_fo, stat_l_fo, stat_r_fo, root_l_fo, root_r_fo)
    return (result.astype(jnp.bfloat16), grad_input, grad_w_in, grad_w_ao, grad_w_fo, grad_gains, new_moment, new_second, new_gains, new_l_in, new_r_in, new_l_ao, new_r_ao, new_l_fo, new_r_fo, new_w_in, new_w_ao, new_w_fo)
```

```python
import math

import jax
import jax.numpy as jnp
from jax import lax
from jax.sharding import PartitionSpec as P

HEAD_DIM = 64


NORM_EPS = 1e-05
ROPE_THETA = 160000.0
SCORE_SCALE = 0.125
MASK_FILL = -1e30
ADAM_RATE = 0.2
SHAMPOO_RATE = 1.0
HIGHEST = lax.Precision.HIGHEST


def norm_forward(values):
    center = values - jnp.mean(values, axis=-1, keepdims=True)
    inv_spread = lax.rsqrt(jnp.mean(center * center, axis=-1, keepdims=True) + NORM_EPS)
    return (center * inv_spread, inv_spread)


def norm_backward(grad_out, normed, inv_spread, gain_row):
    scaled = grad_out * gain_row
    inner_term = (
        scaled
        - jnp.mean(scaled, axis=-1, keepdims=True)
        - normed * jnp.mean(scaled * normed, axis=-1, keepdims=True)
    )
    return (inner_term * inv_spread, jnp.sum(grad_out * normed, axis=0))


def gelu_value(inputs):
    return 0.5 * inputs * (1.0 + lax.erf(inputs * (1.0 / math.sqrt(2.0))))


def gelu_slope(inputs):
    cumulative = 0.5 * (1.0 + lax.erf(inputs * (1.0 / math.sqrt(2.0))))
    return cumulative + inputs * jnp.exp(-0.5 * inputs * inputs) * (1.0 / math.sqrt(2.0 * math.pi))


def rotate(values, cos_table, sin_table):
    half_dim = values.shape[-1] // 2
    turned = jnp.concatenate([-values[..., half_dim:], values[..., :half_dim]], axis=-1)
    return values * cos_table + turned * sin_table


def unrotate(gradient, cos_table, sin_table):
    half_dim = gradient.shape[-1] // 2
    shifted = gradient * sin_table
    back_turn = jnp.concatenate([shifted[..., half_dim:], -shifted[..., :half_dim]], axis=-1)
    return gradient * cos_table + back_turn


def rope_tables(within):
    freq_index = jnp.arange(0, HEAD_DIM, 2, dtype=jnp.float32)
    inverse = 1.0 / jnp.power(ROPE_THETA, freq_index / HEAD_DIM)
    angles = within.astype(jnp.float32)[:, None] * inverse[None, :]
    angles = jnp.concatenate([angles, angles], axis=-1)
    return (jnp.cos(angles), jnp.sin(angles))


def doc_tables(lengths_row, pad_count, row_length):
    doc_order = jnp.arange(lengths_row.shape[0], dtype=jnp.int32)
    doc_ends = jnp.sum(
        jnp.where(doc_order[:, None] >= doc_order[None, :], lengths_row[None, :], 0), axis=1
    )
    starts = doc_ends - lengths_row
    places = jnp.arange(row_length, dtype=jnp.int32)
    segment = jnp.sum((places[:, None] >= doc_ends[None, :]).astype(jnp.int32), axis=1)
    doc_ids = jnp.arange(lengths_row.shape[0], dtype=jnp.int32)
    doc_begin = jnp.sum(jnp.where(segment[:, None] == doc_ids[None, :], starts[None, :], 0), axis=1)
    is_valid = places < row_length - pad_count
    return (segment, places - doc_begin, is_valid)


def apply_rows(activations, weight):
    return lax.dot_general(
        activations, weight, (((1,), (1,)), ((), ())), preferred_element_type=jnp.float32
    )


def outer_sum(grad_rows, act_rows):
    return lax.dot_general(
        grad_rows, act_rows, (((0,), (0,)), ((), ())), preferred_element_type=jnp.float32
    )


def body(
    tokens,
    cotangent,
    doc_lengths,
    pad_counts,
    w_in,
    w_ao,
    w_fo,
    norm_gains,
    gain_moment,
    gain_second,
    stat_l_in,
    stat_r_in,
    stat_l_ao,
    stat_r_ao,
    stat_l_fo,
    stat_r_fo,
    root_l_in,
    root_r_in,
    root_l_ao,
    root_r_ao,
    root_l_fo,
    root_r_fo,
):
    token_count, model_width = tokens.shape
    head_count = model_width // HEAD_DIM
    pair_count = head_count // 2
    pair_width = 2 * HEAD_DIM
    hidden_width = w_fo.shape[1]
    seq_count = lax.axis_size("seq")
    row_length = token_count * seq_count
    first_place = lax.axis_index("seq") * token_count
    segment, within, is_valid = doc_tables(doc_lengths[0], pad_counts[0], row_length)
    own_places = first_place + jnp.arange(token_count, dtype=jnp.int32)
    all_places = jnp.arange(row_length, dtype=jnp.int32)
    own_segment = lax.dynamic_slice_in_dim(segment, first_place, token_count)
    own_within = lax.dynamic_slice_in_dim(within, first_place, token_count)
    allowed = (own_segment[:, None] == segment[None, :]) & (
        is_valid[None, :] | (own_places[:, None] == all_places[None, :])
    )
    cos_table, sin_table = rope_tables(own_within)
    cos_table = cos_table[:, None, :]
    sin_table = sin_table[:, None, :]
    low_weights = (
        w_in.astype(jnp.bfloat16),
        w_ao.astype(jnp.bfloat16),
        w_fo.astype(jnp.bfloat16),
        norm_gains.astype(jnp.bfloat16),
    )
    full_in, full_ao, full_fo, full_gains = (
        lax.all_gather(low_weights[0], ("dp", "seq"), axis=1, tiled=True),
        lax.all_gather(low_weights[1], ("dp", "seq"), axis=0, tiled=True),
        lax.all_gather(low_weights[2], ("dp", "seq"), axis=0, tiled=True),
        lax.all_gather(low_weights[3], ("dp", "seq"), axis=1, tiled=True),
    )
    gain_rows = full_gains.astype(jnp.float32)
    inputs = tokens.astype(jnp.float32)
    normed_one, spread_one = norm_forward(inputs)
    attn_in = (normed_one * gain_rows[0]).astype(jnp.bfloat16)
    qkv_raw = apply_rows(attn_in, full_in[0])
    query_low = (
        rotate(
            qkv_raw[:, :model_width].reshape(token_count, head_count, HEAD_DIM),
            cos_table,
            sin_table,
        )
        .reshape(token_count, model_width)
        .astype(jnp.bfloat16)
    )
    key_low = (
        rotate(
            qkv_raw[:, model_width : 2 * model_width].reshape(token_count, head_count, HEAD_DIM),
            cos_table,
            sin_table,
        )
        .reshape(token_count, model_width)
        .astype(jnp.bfloat16)
    )
    value_low = qkv_raw[:, 2 * model_width :].astype(jnp.bfloat16)
    keys_all, values_all = (
        lax.all_gather(key_low, "seq", axis=0, tiled=True),
        lax.all_gather(value_low, "seq", axis=0, tiled=True),
    )

    def pair_slice(matrix, pair_index):
        return lax.dynamic_slice_in_dim(matrix, pair_index * pair_width, pair_width, 1).reshape(
            matrix.shape[0], 2, HEAD_DIM
        )

    def pair_scores(query_pair, key_pair, allow_mask):
        raw_scores = (
            jnp.einsum("thd,khd->htk", query_pair, key_pair, preferred_element_type=jnp.float32)
            * SCORE_SCALE
        )
        return jnp.where(allow_mask[None], raw_scores, MASK_FILL)

    def forward_pair(loop_carry, pair_index):
        scores = pair_scores(
            pair_slice(query_low, pair_index), pair_slice(keys_all, pair_index), allowed
        )
        row_max = jnp.max(scores, axis=-1, keepdims=True)
        exponent = jnp.exp(scores - row_max)
        row_sum = jnp.sum(exponent, axis=-1, keepdims=True)
        weights_low = (exponent / row_sum).astype(jnp.bfloat16)
        attended = jnp.einsum(
            "htk,khd->thd",
            weights_low,
            pair_slice(values_all, pair_index),
            preferred_element_type=jnp.float32,
        )
        return (
            loop_carry,
            (attended.reshape(token_count, pair_width), (row_max + jnp.log(row_sum))[..., 0]),
        )

    unused, (attended_pairs, log_norms) = lax.scan(forward_pair, 0, jnp.arange(pair_count))
    attn_low = (
        jnp.transpose(attended_pairs, (1, 0, 2))
        .reshape(token_count, model_width)
        .astype(jnp.bfloat16)
    )
    residual = inputs + apply_rows(attn_low, full_ao)
    normed_two, spread_two = norm_forward(residual)
    ffn_in = (normed_two * gain_rows[1]).astype(jnp.bfloat16)
    projected = apply_rows(ffn_in, full_in[1])
    inner_part = projected[:, :hidden_width]
    gate_part = projected[:, hidden_width:]
    activated = gelu_value(inner_part)
    mid_low = (activated * gate_part).astype(jnp.bfloat16)
    layer_out = (residual + apply_rows(mid_low, full_fo)).astype(jnp.bfloat16)
    back_in, back_ao, back_fo, back_gains = (
        lax.all_gather(low_weights[0], ("dp", "seq"), axis=1, tiled=True),
        lax.all_gather(low_weights[1], ("dp", "seq"), axis=0, tiled=True),
        lax.all_gather(low_weights[2], ("dp", "seq"), axis=0, tiled=True),
        lax.all_gather(low_weights[3], ("dp", "seq"), axis=1, tiled=True),
    )
    back_rows = back_gains.astype(jnp.float32)
    grad_fo_w = outer_sum(cotangent, mid_low)
    grad_mid = jnp.dot(cotangent, back_fo, preferred_element_type=jnp.float32)
    grad_proj = jnp.concatenate(
        [grad_mid * gate_part * gelu_slope(inner_part), grad_mid * activated], axis=1
    ).astype(jnp.bfloat16)
    grad_ffn_w = outer_sum(grad_proj, ffn_in)
    grad_ffn_in = jnp.dot(grad_proj, back_in[1], preferred_element_type=jnp.float32)
    grad_norm_two, grad_gain_two = norm_backward(grad_ffn_in, normed_two, spread_two, back_rows[1])
    grad_resid = cotangent.astype(jnp.float32) + grad_norm_two
    grad_out_attn = grad_resid.astype(jnp.bfloat16)
    grad_ao_w = outer_sum(grad_out_attn, attn_low)
    grad_attn = jnp.dot(grad_out_attn, back_ao, preferred_element_type=jnp.float32).astype(
        jnp.bfloat16
    )

    def query_side_grads(pair_index):
        query_pair = pair_slice(query_low, pair_index)
        key_pair = pair_slice(keys_all, pair_index)
        value_pair = pair_slice(values_all, pair_index)
        grad_pair = pair_slice(grad_attn, pair_index)
        scores = pair_scores(query_pair, key_pair, allowed)
        softmax_out = jnp.exp(scores - log_norms[pair_index][..., None])
        grad_weights = jnp.einsum(
            "thd,khd->htk", grad_pair, value_pair, preferred_element_type=jnp.float32
        )
        delta_row = jnp.sum(softmax_out * grad_weights, axis=-1, keepdims=True)
        grad_scores = (softmax_out * (grad_weights - delta_row)).astype(jnp.bfloat16)
        grad_query = (
            jnp.einsum("htk,khd->thd", grad_scores, key_pair, preferred_element_type=jnp.float32)
            * SCORE_SCALE
        )
        return (query_pair, grad_pair, softmax_out, grad_scores, grad_query, delta_row)

    def backward_pair(loop_carry, pair_index):
        query_pair, grad_pair, softmax_out, grad_scores, grad_query, delta_row = query_side_grads(
            pair_index
        )
        grad_key = (
            jnp.einsum("htk,thd->khd", grad_scores, query_pair, preferred_element_type=jnp.float32)
            * SCORE_SCALE
        )
        grad_value = jnp.einsum(
            "htk,thd->khd",
            softmax_out.astype(jnp.bfloat16),
            grad_pair,
            preferred_element_type=jnp.float32,
        )
        return (
            loop_carry,
            (
                grad_query.reshape(token_count, pair_width),
                grad_key.reshape(row_length, pair_width),
                grad_value.reshape(row_length, pair_width),
            ),
        )

    unused, (grad_query_pairs, grad_key_parts, grad_value_parts) = lax.scan(
        backward_pair, 0, jnp.arange(pair_count)
    )
    grad_key_pairs, grad_value_pairs = (
        lax.psum_scatter(
            grad_key_parts.astype(jnp.bfloat16), "seq", scatter_dimension=1, tiled=True
        ).astype(jnp.float32),
        lax.psum_scatter(
            grad_value_parts.astype(jnp.bfloat16), "seq", scatter_dimension=1, tiled=True
        ).astype(jnp.float32),
    )

    def heads_of(pairs_array):
        return jnp.transpose(pairs_array, (1, 0, 2)).reshape(token_count, head_count, HEAD_DIM)

    grad_qkv = jnp.concatenate(
        [
            unrotate(heads_of(grad_query_pairs), cos_table, sin_table).reshape(
                token_count, model_width
            ),
            unrotate(heads_of(grad_key_pairs), cos_table, sin_table).reshape(
                token_count, model_width
            ),
            heads_of(grad_value_pairs).reshape(token_count, model_width),
        ],
        axis=1,
    ).astype(jnp.bfloat16)
    grad_qkv_w = outer_sum(grad_qkv, attn_in)
    grad_attn_in = jnp.dot(grad_qkv, back_in[0], preferred_element_type=jnp.float32)
    grad_norm_one, grad_gain_one = norm_backward(grad_attn_in, normed_one, spread_one, back_rows[0])
    grad_input = grad_resid + grad_norm_one
    w_terms = jnp.stack([grad_qkv_w, grad_ffn_w])
    gain_terms = jnp.stack([grad_gain_one, grad_gain_two])
    summed_in, summed_ao, summed_fo, summed_gains = (
        lax.psum_scatter(w_terms, ("dp", "seq"), scatter_dimension=1, tiled=True),
        lax.psum_scatter(grad_ao_w, ("dp", "seq"), scatter_dimension=0, tiled=True),
        lax.psum_scatter(grad_fo_w, ("dp", "seq"), scatter_dimension=0, tiled=True),
        lax.psum_scatter(gain_terms, ("dp", "seq"), scatter_dimension=1, tiled=True),
    )
    new_moment = 0.9 * gain_moment + 0.1 * summed_gains
    new_second = 0.999 * gain_second + 0.001 * summed_gains * summed_gains
    new_gains = norm_gains - ADAM_RATE * new_moment / (jnp.sqrt(new_second) + 1e-08)
    whole_in, whole_ao, whole_fo = (
        lax.all_gather(summed_in.astype(jnp.bfloat16), ("dp", "seq"), axis=1, tiled=True).astype(
            summed_in.dtype
        ),
        lax.all_gather(summed_ao.astype(jnp.bfloat16), ("dp", "seq"), axis=0, tiled=True).astype(
            summed_ao.dtype
        ),
        lax.all_gather(summed_fo.astype(jnp.bfloat16), ("dp", "seq"), axis=0, tiled=True).astype(
            summed_fo.dtype
        ),
    )
    dev_index = lax.axis_index(("dp", "seq"))

    def refresh(grad_shard, grad_full, stat_left, stat_right, root_right):
        col_count = stat_right.shape[1]
        new_left = 0.5 * stat_left + 0.5 * jnp.einsum(
            "arn,amn->arm", grad_shard, grad_full, precision=HIGHEST
        )
        full_cols = lax.dynamic_slice_in_dim(grad_full, dev_index * col_count, col_count, 2)
        new_right = 0.5 * stat_right + 0.5 * jnp.einsum(
            "amc,amn->acn", full_cols, grad_full, precision=HIGHEST
        )
        applied = jnp.einsum("amn,acn->amc", grad_full, root_right, precision=HIGHEST)
        return (new_left, new_right, applied)

    left_in, right_in, applied_in = refresh(summed_in, whole_in, stat_l_in, stat_r_in, root_r_in)
    left_ao, right_ao, applied_ao = refresh(
        summed_ao[None], whole_ao[None], stat_l_ao[None], stat_r_ao[None], root_r_ao[None]
    )
    left_fo, right_fo, applied_fo = refresh(
        summed_fo[None], whole_fo[None], stat_l_fo[None], stat_r_fo[None], root_r_fo[None]
    )
    product_in, product_ao, product_fo = (
        lax.all_gather(applied_in.astype(jnp.bfloat16), ("dp", "seq"), axis=2, tiled=True).astype(
            applied_in.dtype
        ),
        lax.all_gather(applied_ao.astype(jnp.bfloat16), ("dp", "seq"), axis=2, tiled=True).astype(
            applied_ao.dtype
        ),
        lax.all_gather(applied_fo.astype(jnp.bfloat16), ("dp", "seq"), axis=2, tiled=True).astype(
            applied_fo.dtype
        ),
    )
    new_w_in = w_in - SHAMPOO_RATE * jnp.einsum(
        "arm,amn->arn", root_l_in, product_in, precision=HIGHEST
    )
    new_w_ao = (
        w_ao
        - SHAMPOO_RATE
        * jnp.einsum("arm,amn->arn", root_l_ao[None], product_ao, precision=HIGHEST)[0]
    )
    new_w_fo = (
        w_fo
        - SHAMPOO_RATE
        * jnp.einsum("arm,amn->arn", root_l_fo[None], product_fo, precision=HIGHEST)[0]
    )
    return (
        layer_out,
        grad_input,
        summed_in,
        summed_ao,
        summed_fo,
        summed_gains,
        new_moment,
        new_second,
        new_gains,
        left_in,
        right_in,
        left_ao[0],
        right_ao[0],
        left_fo[0],
        right_fo[0],
        new_w_in,
        new_w_ao,
        new_w_fo,
    )


def solution(mesh):
    in_specs = (
        P(("dp", "seq"), None),
        P(("dp", "seq"), None),
        P("dp", None),
        P("dp"),
        P(None, ("dp", "seq"), None),
        P(("dp", "seq"), None),
        P(("dp", "seq"), None),
        P(None, ("dp", "seq")),
        P(None, ("dp", "seq")),
        P(None, ("dp", "seq")),
        P(None, ("dp", "seq"), None),
        P(None, ("dp", "seq"), None),
        P(("dp", "seq"), None),
        P(("dp", "seq"), None),
        P(("dp", "seq"), None),
        P(("dp", "seq"), None),
        P(None, ("dp", "seq"), None),
        P(None, ("dp", "seq"), None),
        P(("dp", "seq"), None),
        P(("dp", "seq"), None),
        P(("dp", "seq"), None),
        P(("dp", "seq"), None),
    )
    out_specs = (
        P(("dp", "seq"), None),
        P(("dp", "seq"), None),
        P(None, ("dp", "seq"), None),
        P(("dp", "seq"), None),
        P(("dp", "seq"), None),
        P(None, ("dp", "seq")),
        P(None, ("dp", "seq")),
        P(None, ("dp", "seq")),
        P(None, ("dp", "seq")),
        P(None, ("dp", "seq"), None),
        P(None, ("dp", "seq"), None),
        P(("dp", "seq"), None),
        P(("dp", "seq"), None),
        P(("dp", "seq"), None),
        P(("dp", "seq"), None),
        P(None, ("dp", "seq"), None),
        P(("dp", "seq"), None),
        P(("dp", "seq"), None),
    )
    return jax.shard_map(body, mesh=mesh, in_specs=in_specs, out_specs=out_specs, check_vma=False)
```

```python
import math

import jax
import jax.numpy as jnp
from jax import lax
from jax.experimental import pallas as pl
from jax.experimental.pallas import tpu as pltpu
from jax.sharding import PartitionSpec as P

HEAD_DIM = 64


NORM_EPS = 1e-05
ROPE_THETA = 160000.0
SCORE_SCALE = 0.125
MASK_FILL = -1e30
ADAM_RATE = 0.2
SHAMPOO_RATE = 1.0
HIGHEST = lax.Precision.HIGHEST


def norm_forward(values):
    center = values - jnp.mean(values, axis=-1, keepdims=True)
    inv_spread = lax.rsqrt(jnp.mean(center * center, axis=-1, keepdims=True) + NORM_EPS)
    return (center * inv_spread, inv_spread)


def norm_backward(grad_out, normed, inv_spread, gain_row):
    scaled = grad_out * gain_row
    inner_term = (
        scaled
        - jnp.mean(scaled, axis=-1, keepdims=True)
        - normed * jnp.mean(scaled * normed, axis=-1, keepdims=True)
    )
    return (inner_term * inv_spread, jnp.sum(grad_out * normed, axis=0))


def gelu_value(inputs):
    return 0.5 * inputs * (1.0 + lax.erf(inputs * (1.0 / math.sqrt(2.0))))


def gelu_slope(inputs):
    cumulative = 0.5 * (1.0 + lax.erf(inputs * (1.0 / math.sqrt(2.0))))
    return cumulative + inputs * jnp.exp(-0.5 * inputs * inputs) * (1.0 / math.sqrt(2.0 * math.pi))


def rotate(values, cos_table, sin_table):
    half_dim = values.shape[-1] // 2
    turned = jnp.concatenate([-values[..., half_dim:], values[..., :half_dim]], axis=-1)
    return values * cos_table + turned * sin_table


def unrotate(gradient, cos_table, sin_table):
    half_dim = gradient.shape[-1] // 2
    shifted = gradient * sin_table
    back_turn = jnp.concatenate([shifted[..., half_dim:], -shifted[..., :half_dim]], axis=-1)
    return gradient * cos_table + back_turn


def rope_tables(within):
    freq_index = jnp.arange(0, HEAD_DIM, 2, dtype=jnp.float32)
    inverse = 1.0 / jnp.power(ROPE_THETA, freq_index / HEAD_DIM)
    angles = within.astype(jnp.float32)[:, None] * inverse[None, :]
    angles = jnp.concatenate([angles, angles], axis=-1)
    return (jnp.cos(angles), jnp.sin(angles))


def doc_tables(lengths_row, pad_count, row_length):
    doc_order = jnp.arange(lengths_row.shape[0], dtype=jnp.int32)
    doc_ends = jnp.sum(
        jnp.where(doc_order[:, None] >= doc_order[None, :], lengths_row[None, :], 0), axis=1
    )
    starts = doc_ends - lengths_row
    places = jnp.arange(row_length, dtype=jnp.int32)
    segment = jnp.sum((places[:, None] >= doc_ends[None, :]).astype(jnp.int32), axis=1)
    doc_ids = jnp.arange(lengths_row.shape[0], dtype=jnp.int32)
    doc_begin = jnp.sum(jnp.where(segment[:, None] == doc_ids[None, :], starts[None, :], 0), axis=1)
    is_valid = places < row_length - pad_count
    return (segment, places - doc_begin, is_valid)


def apply_rows(activations, weight):
    return lax.dot_general(
        activations, weight, (((1,), (1,)), ((), ())), preferred_element_type=jnp.float32
    )


def outer_sum(grad_rows, act_rows):
    return lax.dot_general(
        grad_rows, act_rows, (((0,), (0,)), ((), ())), preferred_element_type=jnp.float32
    )


def sequence_body(
    tokens,
    cotangent,
    doc_lengths,
    pad_counts,
    w_in,
    w_ao,
    w_fo,
    norm_gains,
    gain_moment,
    gain_second,
    stat_l_in,
    stat_r_in,
    stat_l_ao,
    stat_r_ao,
    stat_l_fo,
    stat_r_fo,
    root_l_in,
    root_r_in,
    root_l_ao,
    root_r_ao,
    root_l_fo,
    root_r_fo,
):
    token_count, model_width = tokens.shape
    head_count = model_width // HEAD_DIM
    pair_count = head_count // 2
    pair_width = 2 * HEAD_DIM
    hidden_width = w_fo.shape[1]
    seq_count = lax.axis_size("seq")
    row_length = token_count * seq_count
    first_place = lax.axis_index("seq") * token_count
    segment, within, is_valid = doc_tables(doc_lengths[0], pad_counts[0], row_length)
    own_places = first_place + jnp.arange(token_count, dtype=jnp.int32)
    all_places = jnp.arange(row_length, dtype=jnp.int32)
    own_segment = lax.dynamic_slice_in_dim(segment, first_place, token_count)
    own_within = lax.dynamic_slice_in_dim(within, first_place, token_count)
    allowed = (own_segment[:, None] == segment[None, :]) & (
        is_valid[None, :] | (own_places[:, None] == all_places[None, :])
    )
    cos_table, sin_table = rope_tables(own_within)
    cos_table = cos_table[:, None, :]
    sin_table = sin_table[:, None, :]
    low_weights = (
        w_in.astype(jnp.bfloat16),
        w_ao.astype(jnp.bfloat16),
        w_fo.astype(jnp.bfloat16),
        norm_gains.astype(jnp.bfloat16),
    )
    full_in, full_ao, full_fo, full_gains = (
        lax.all_gather(low_weights[0], ("dp", "seq"), axis=1, tiled=True),
        lax.all_gather(low_weights[1], ("dp", "seq"), axis=0, tiled=True),
        lax.all_gather(low_weights[2], ("dp", "seq"), axis=0, tiled=True),
        lax.all_gather(low_weights[3], ("dp", "seq"), axis=1, tiled=True),
    )
    gain_rows = full_gains.astype(jnp.float32)
    inputs = tokens.astype(jnp.float32)
    normed_one, spread_one = norm_forward(inputs)
    attn_in = (normed_one * gain_rows[0]).astype(jnp.bfloat16)
    qkv_raw = apply_rows(attn_in, full_in[0])
    query_low = (
        rotate(
            qkv_raw[:, :model_width].reshape(token_count, head_count, HEAD_DIM),
            cos_table,
            sin_table,
        )
        .reshape(token_count, model_width)
        .astype(jnp.bfloat16)
    )
    key_low = (
        rotate(
            qkv_raw[:, model_width : 2 * model_width].reshape(token_count, head_count, HEAD_DIM),
            cos_table,
            sin_table,
        )
        .reshape(token_count, model_width)
        .astype(jnp.bfloat16)
    )
    value_low = qkv_raw[:, 2 * model_width :].astype(jnp.bfloat16)
    keys_all, values_all = (
        lax.all_gather(key_low, "seq", axis=0, tiled=True),
        lax.all_gather(value_low, "seq", axis=0, tiled=True),
    )

    def pair_slice(matrix, pair_index):
        return lax.dynamic_slice_in_dim(matrix, pair_index * pair_width, pair_width, 1).reshape(
            matrix.shape[0], 2, HEAD_DIM
        )

    def pair_scores(query_pair, key_pair, allow_mask):
        raw_scores = (
            jnp.einsum("thd,khd->htk", query_pair, key_pair, preferred_element_type=jnp.float32)
            * SCORE_SCALE
        )
        return jnp.where(allow_mask[None], raw_scores, MASK_FILL)

    def forward_pair(loop_carry, pair_index):
        scores = pair_scores(
            pair_slice(query_low, pair_index), pair_slice(keys_all, pair_index), allowed
        )
        row_max = jnp.max(scores, axis=-1, keepdims=True)
        exponent = jnp.exp(scores - row_max)
        row_sum = jnp.sum(exponent, axis=-1, keepdims=True)
        weights_low = (exponent / row_sum).astype(jnp.bfloat16)
        attended = jnp.einsum(
            "htk,khd->thd",
            weights_low,
            pair_slice(values_all, pair_index),
            preferred_element_type=jnp.float32,
        )
        return (
            loop_carry,
            (attended.reshape(token_count, pair_width), (row_max + jnp.log(row_sum))[..., 0]),
        )

    unused, (attended_pairs, log_norms) = lax.scan(forward_pair, 0, jnp.arange(pair_count))
    attn_low = (
        jnp.transpose(attended_pairs, (1, 0, 2))
        .reshape(token_count, model_width)
        .astype(jnp.bfloat16)
    )
    residual = inputs + apply_rows(attn_low, full_ao)
    normed_two, spread_two = norm_forward(residual)
    ffn_in = (normed_two * gain_rows[1]).astype(jnp.bfloat16)
    projected = apply_rows(ffn_in, full_in[1])
    inner_part = projected[:, :hidden_width]
    gate_part = projected[:, hidden_width:]
    activated = gelu_value(inner_part)
    mid_low = (activated * gate_part).astype(jnp.bfloat16)
    layer_out = (residual + apply_rows(mid_low, full_fo)).astype(jnp.bfloat16)
    back_in, back_ao, back_fo, back_gains = (
        lax.all_gather(low_weights[0], ("dp", "seq"), axis=1, tiled=True),
        lax.all_gather(low_weights[1], ("dp", "seq"), axis=0, tiled=True),
        lax.all_gather(low_weights[2], ("dp", "seq"), axis=0, tiled=True),
        lax.all_gather(low_weights[3], ("dp", "seq"), axis=1, tiled=True),
    )
    back_rows = back_gains.astype(jnp.float32)
    grad_fo_w = outer_sum(cotangent, mid_low)
    grad_mid = jnp.dot(cotangent, back_fo, preferred_element_type=jnp.float32)
    grad_proj = jnp.concatenate(
        [grad_mid * gate_part * gelu_slope(inner_part), grad_mid * activated], axis=1
    ).astype(jnp.bfloat16)
    grad_ffn_w = outer_sum(grad_proj, ffn_in)
    grad_ffn_in = jnp.dot(grad_proj, back_in[1], preferred_element_type=jnp.float32)
    grad_norm_two, grad_gain_two = norm_backward(grad_ffn_in, normed_two, spread_two, back_rows[1])
    grad_resid = cotangent.astype(jnp.float32) + grad_norm_two
    grad_out_attn = grad_resid.astype(jnp.bfloat16)
    grad_ao_w = outer_sum(grad_out_attn, attn_low)
    grad_attn = jnp.dot(grad_out_attn, back_ao, preferred_element_type=jnp.float32).astype(
        jnp.bfloat16
    )

    def query_side_grads(pair_index):
        query_pair = pair_slice(query_low, pair_index)
        key_pair = pair_slice(keys_all, pair_index)
        value_pair = pair_slice(values_all, pair_index)
        grad_pair = pair_slice(grad_attn, pair_index)
        scores = pair_scores(query_pair, key_pair, allowed)
        softmax_out = jnp.exp(scores - log_norms[pair_index][..., None])
        grad_weights = jnp.einsum(
            "thd,khd->htk", grad_pair, value_pair, preferred_element_type=jnp.float32
        )
        delta_row = jnp.sum(softmax_out * grad_weights, axis=-1, keepdims=True)
        grad_scores = (softmax_out * (grad_weights - delta_row)).astype(jnp.bfloat16)
        grad_query = (
            jnp.einsum("htk,khd->thd", grad_scores, key_pair, preferred_element_type=jnp.float32)
            * SCORE_SCALE
        )
        return (query_pair, grad_pair, softmax_out, grad_scores, grad_query, delta_row)

    def backward_pair(loop_carry, pair_index):
        query_pair, grad_pair, softmax_out, grad_scores, grad_query, delta_row = query_side_grads(
            pair_index
        )
        grad_key = (
            jnp.einsum("htk,thd->khd", grad_scores, query_pair, preferred_element_type=jnp.float32)
            * SCORE_SCALE
        )
        grad_value = jnp.einsum(
            "htk,thd->khd",
            softmax_out.astype(jnp.bfloat16),
            grad_pair,
            preferred_element_type=jnp.float32,
        )
        return (
            loop_carry,
            (
                grad_query.reshape(token_count, pair_width),
                grad_key.reshape(row_length, pair_width),
                grad_value.reshape(row_length, pair_width),
            ),
        )

    unused, (grad_query_pairs, grad_key_parts, grad_value_parts) = lax.scan(
        backward_pair, 0, jnp.arange(pair_count)
    )
    grad_key_pairs, grad_value_pairs = (
        lax.psum_scatter(
            grad_key_parts.astype(jnp.bfloat16), "seq", scatter_dimension=1, tiled=True
        ).astype(jnp.float32),
        lax.psum_scatter(
            grad_value_parts.astype(jnp.bfloat16), "seq", scatter_dimension=1, tiled=True
        ).astype(jnp.float32),
    )

    def heads_of(pairs_array):
        return jnp.transpose(pairs_array, (1, 0, 2)).reshape(token_count, head_count, HEAD_DIM)

    grad_qkv = jnp.concatenate(
        [
            unrotate(heads_of(grad_query_pairs), cos_table, sin_table).reshape(
                token_count, model_width
            ),
            unrotate(heads_of(grad_key_pairs), cos_table, sin_table).reshape(
                token_count, model_width
            ),
            heads_of(grad_value_pairs).reshape(token_count, model_width),
        ],
        axis=1,
    ).astype(jnp.bfloat16)
    grad_qkv_w = outer_sum(grad_qkv, attn_in)
    grad_attn_in = jnp.dot(grad_qkv, back_in[0], preferred_element_type=jnp.float32)
    grad_norm_one, grad_gain_one = norm_backward(grad_attn_in, normed_one, spread_one, back_rows[0])
    grad_input = grad_resid + grad_norm_one
    w_terms = jnp.stack([grad_qkv_w, grad_ffn_w])
    gain_terms = jnp.stack([grad_gain_one, grad_gain_two])
    summed_in, summed_ao, summed_fo, summed_gains = (
        lax.psum_scatter(w_terms, ("dp", "seq"), scatter_dimension=1, tiled=True),
        lax.psum_scatter(grad_ao_w, ("dp", "seq"), scatter_dimension=0, tiled=True),
        lax.psum_scatter(grad_fo_w, ("dp", "seq"), scatter_dimension=0, tiled=True),
        lax.psum_scatter(gain_terms, ("dp", "seq"), scatter_dimension=1, tiled=True),
    )
    new_moment = 0.9 * gain_moment + 0.1 * summed_gains
    new_second = 0.999 * gain_second + 0.001 * summed_gains * summed_gains
    new_gains = norm_gains - ADAM_RATE * new_moment / (jnp.sqrt(new_second) + 1e-08)
    whole_in, whole_ao, whole_fo = (
        lax.all_gather(summed_in.astype(jnp.bfloat16), ("dp", "seq"), axis=1, tiled=True).astype(
            summed_in.dtype
        ),
        lax.all_gather(summed_ao.astype(jnp.bfloat16), ("dp", "seq"), axis=0, tiled=True).astype(
            summed_ao.dtype
        ),
        lax.all_gather(summed_fo.astype(jnp.bfloat16), ("dp", "seq"), axis=0, tiled=True).astype(
            summed_fo.dtype
        ),
    )
    dev_index = lax.axis_index(("dp", "seq"))

    def refresh(grad_shard, grad_full, stat_left, stat_right, root_right):
        col_count = stat_right.shape[1]
        new_left = 0.5 * stat_left + 0.5 * jnp.einsum(
            "arn,amn->arm", grad_shard, grad_full, precision=HIGHEST
        )
        full_cols = lax.dynamic_slice_in_dim(grad_full, dev_index * col_count, col_count, 2)
        new_right = 0.5 * stat_right + 0.5 * jnp.einsum(
            "amc,amn->acn", full_cols, grad_full, precision=HIGHEST
        )
        applied = jnp.einsum("amn,acn->amc", grad_full, root_right, precision=HIGHEST)
        return (new_left, new_right, applied)

    left_in, right_in, applied_in = refresh(summed_in, whole_in, stat_l_in, stat_r_in, root_r_in)
    left_ao, right_ao, applied_ao = refresh(
        summed_ao[None], whole_ao[None], stat_l_ao[None], stat_r_ao[None], root_r_ao[None]
    )
    left_fo, right_fo, applied_fo = refresh(
        summed_fo[None], whole_fo[None], stat_l_fo[None], stat_r_fo[None], root_r_fo[None]
    )
    product_in, product_ao, product_fo = (
        lax.all_gather(applied_in.astype(jnp.bfloat16), ("dp", "seq"), axis=2, tiled=True).astype(
            applied_in.dtype
        ),
        lax.all_gather(applied_ao.astype(jnp.bfloat16), ("dp", "seq"), axis=2, tiled=True).astype(
            applied_ao.dtype
        ),
        lax.all_gather(applied_fo.astype(jnp.bfloat16), ("dp", "seq"), axis=2, tiled=True).astype(
            applied_fo.dtype
        ),
    )
    new_w_in = w_in - SHAMPOO_RATE * jnp.einsum(
        "arm,amn->arn", root_l_in, product_in, precision=HIGHEST
    )
    new_w_ao = (
        w_ao
        - SHAMPOO_RATE
        * jnp.einsum("arm,amn->arn", root_l_ao[None], product_ao, precision=HIGHEST)[0]
    )
    new_w_fo = (
        w_fo
        - SHAMPOO_RATE
        * jnp.einsum("arm,amn->arn", root_l_fo[None], product_fo, precision=HIGHEST)[0]
    )
    return (
        layer_out,
        grad_input,
        summed_in,
        summed_ao,
        summed_fo,
        summed_gains,
        new_moment,
        new_second,
        new_gains,
        left_in,
        right_in,
        left_ao[0],
        right_ao[0],
        left_fo[0],
        right_fo[0],
        new_w_in,
        new_w_ao,
        new_w_fo,
    )


QUERY_TILE = 384
KEY_STEP = 256
KEY_ALIGN = 128
PREP_TILE = 480
LANES = 128
MASK_BIT = -(2.0**100)
NO_MAX = -3e38
BF16 = jnp.bfloat16
F32 = jnp.float32
VMEM_BYTES = 56 * 2**20


def dot_rows(left, right):
    return lax.dot_general(left, right, (((1,), (1,)), ((), ())), preferred_element_type=F32)


def dot_plain(left, right):
    return lax.dot_general(left, right, (((1,), (0,)), ((), ())), preferred_element_type=F32)


def dot_first(left, right):
    return lax.dot_general(left, right, (((0,), (0,)), ((), ())), preferred_element_type=F32)


def lane_index(rows):
    return lax.broadcasted_iota(jnp.int32, (rows, LANES), 1)


def three_pieces(column):
    first = column.astype(BF16).astype(F32)
    second = (column - first).astype(BF16).astype(F32)
    return first, second, column - first - second


def project_kernel(
    tokens, weight, gain, cosine, sine, query_mask, key_mask, attn_in, query, key, value
):
    step = pl.program_id(0)
    last = pl.num_programs(0) - 1
    own_heads = query.shape[0]
    rows = tokens.shape[0]
    lane = lane_index(rows)
    low_lanes = lane < HEAD_DIM

    @pl.when(step < last)
    def compute():
        normed = norm_forward(tokens[...].astype(F32))[0]
        low = (normed * gain[...]).astype(BF16)
        attn_in[...] = low
        raw = dot_rows(low, weight[...])
        first_half = lane % HEAD_DIM < HEAD_DIM // 2
        ones = jnp.where(lane < HEAD_DIM + 3, 1.0, 0.0)
        for head in range(own_heads):
            both = raw[:, head * LANES : (head + 1) * LANES]
            turned = jnp.where(
                first_half,
                -pltpu.roll(both, LANES - HEAD_DIM // 2, 1),
                pltpu.roll(both, HEAD_DIM // 2, 1),
            )
            both = both * cosine[...] + turned * sine[...]
            query[head] = jnp.where(
                low_lanes, both * SCORE_SCALE, query_mask[...].astype(F32)
            ).astype(BF16)
            key[head] = jnp.where(
                low_lanes, pltpu.roll(both, HEAD_DIM, 1), key_mask[...].astype(F32)
            ).astype(BF16)
            at = own_heads + head // 2
            pair = raw[:, at * LANES : (at + 1) * LANES]
            if head % 2:
                pair = pltpu.roll(pair, HEAD_DIM, 1)
            value[head] = jnp.where(low_lanes, pair, ones).astype(BF16)

    @pl.when(step == last)
    def pad():
        blocked = jnp.where(
            low_lanes,
            0.0,
            jnp.where(lane < HEAD_DIM + 8, MASK_BIT, jnp.where(lane < HEAD_DIM + 11, 1.0, 0.0)),
        ).astype(BF16)
        for head in range(own_heads):
            key[head] = blocked
            value[head] = jnp.zeros((rows, LANES), BF16)


def attend_kernel(
    start_at, step_count, pad_from, query, key, value, pair_out, extra_out, wide_out, query_out
):
    tile = pl.program_id(0)
    own_heads, rows, _ = query.shape
    lane = lane_index(rows)
    low_lanes = lane < HEAD_DIM
    place = tile * rows + lax.broadcasted_iota(jnp.int32, (rows, 1), 0)
    padded = place >= pad_from[0]
    own_rows = pl.ds(pl.multiple_of(tile * rows, KEY_ALIGN), rows)
    maxima, totals = [], []
    for head in range(own_heads):
        products = query[head].astype(F32) * key[head, own_rows, :].astype(F32)
        self_score = jnp.sum(jnp.where(low_lanes, products, 0.0), axis=1, keepdims=True)
        maxima.append(jnp.where(padded, self_score, NO_MAX))
        totals.append(jnp.where(padded, value[head, own_rows, :].astype(F32), 0.0))
    first = start_at[tile] * KEY_ALIGN

    def step(index, carry):
        maxima, totals = carry
        at = pl.ds(pl.multiple_of(first + index * KEY_STEP, KEY_ALIGN), KEY_STEP)
        new_maxima, new_totals = [], []
        for head in range(own_heads):
            scores = dot_rows(query[head], key[head, at, :])
            row_max = jnp.maximum(maxima[head], jnp.max(scores, axis=1, keepdims=True))
            weights = jnp.exp(scores - row_max).astype(BF16)
            new_totals.append(
                totals[head] * jnp.exp(maxima[head] - row_max)
                + dot_plain(weights, value[head, at, :])
            )
            new_maxima.append(row_max)
        return new_maxima, new_totals

    maxima, totals = lax.fori_loop(0, step_count[tile], step, (maxima, totals))
    outs = []
    for head in range(own_heads):
        row_sum = totals[head][:, HEAD_DIM : HEAD_DIM + 1]
        attended = jnp.where(low_lanes, totals[head] / row_sum, 0.0)
        wide_out[head] = attended
        outs.append(attended)
        one, two, three = three_pieces(-(maxima[head] + jnp.log(row_sum)))
        at = HEAD_DIM + 8
        query_out[head] = jnp.where(
            lane == at,
            one,
            jnp.where(
                lane == at + 1, two, jnp.where(lane == at + 2, three, query[head].astype(F32))
            ),
        ).astype(BF16)
    pair_out[...] = (outs[0] + pltpu.roll(outs[1], HEAD_DIM, 1)).astype(BF16)
    extra_out[...] = outs[2].astype(BF16)


def attend_back_kernel(
    start_at,
    step_count,
    pad_from,
    query,
    wide,
    grad_pair,
    grad_extra,
    key,
    value,
    cosine,
    sine,
    grads,
    grad_query,
    grad_key,
    grad_value,
):
    tile = pl.program_id(0)
    own_heads, rows, _ = query.shape
    tile_count = grad_query.shape[1] // rows

    @pl.when(tile == 0)
    def clear():
        grad_key[...] = jnp.zeros_like(grad_key)
        grad_value[...] = jnp.zeros_like(grad_value)

    @pl.when(tile < tile_count)
    def accumulate():
        lane = lane_index(rows)
        low_lanes = lane < HEAD_DIM
        own_rows = pl.ds(pl.multiple_of(tile * rows, KEY_ALIGN), rows)
        first = start_at[tile] * KEY_ALIGN
        pair = grad_pair[...].astype(F32)
        incoming = [pair, pltpu.roll(pair, HEAD_DIM, 1), grad_extra[...].astype(F32)]
        grads_out = []
        for head in range(own_heads):
            own = jnp.where(low_lanes, incoming[head], 0.0)
            one, two, three = three_pieces(-jnp.sum(own * wide[head], axis=1, keepdims=True))
            grads_out.append(
                jnp.where(
                    lane == HEAD_DIM,
                    one,
                    jnp.where(
                        lane == HEAD_DIM + 1, two, jnp.where(lane == HEAD_DIM + 2, three, own)
                    ),
                ).astype(BF16)
            )

        def step(index, carry):
            at = pl.ds(pl.multiple_of(first + index * KEY_STEP, KEY_ALIGN), KEY_STEP)
            sums = []
            for head in range(own_heads):
                keys = key[head, at, :]
                probs = jnp.exp(dot_rows(keys, query[head]))
                grad_scores = (probs * dot_rows(value[head, at, :], grads_out[head])).astype(BF16)
                grad_value[head, at, :] += dot_plain(probs.astype(BF16), grads_out[head])
                grad_key[head, at, :] += dot_plain(grad_scores, query[head])
                sums.append(carry[head] + dot_first(grad_scores, keys))
            return sums

        zeros = [jnp.zeros((rows, LANES), F32) for _ in range(own_heads)]
        sums = lax.fori_loop(0, step_count[tile], step, zeros)
        for head in range(own_heads):
            grad_query[head, own_rows, :] = sums[head]

        @pl.when((tile + 1) * rows > pad_from[0])
        def self_terms():
            place = tile * rows + lax.broadcasted_iota(jnp.int32, (rows, 1), 0)
            padded = place >= pad_from[0]
            for head in range(own_heads):
                keys = key[head, own_rows, :].astype(F32)
                queries = query[head].astype(F32)
                outs = grads_out[head].astype(F32)
                counted = low_lanes | (lane >= HEAD_DIM + 8)
                score = jnp.sum(jnp.where(counted, queries * keys, 0.0), axis=1, keepdims=True)
                prob = jnp.where(padded, jnp.exp(jnp.where(padded, score, 0.0)), 0.0)
                grad_prob = jnp.sum(
                    outs * value[head, own_rows, :].astype(F32), axis=1, keepdims=True
                )
                grad_score = (prob * grad_prob).astype(BF16).astype(F32)
                low_prob = prob.astype(BF16).astype(F32)
                grad_query[head, own_rows, :] += grad_score * jnp.where(low_lanes, keys, 0.0)
                grad_key[head, own_rows, :] += grad_score * queries
                grad_value[head, own_rows, :] += low_prob * outs

    @pl.when(tile >= tile_count)
    def finish():
        size = grads.shape[0]
        at = pl.ds(pl.multiple_of((tile - tile_count) * size, 16), size)
        lane = lane_index(size)
        low_lanes = lane < HEAD_DIM
        first_half = lane % HEAD_DIM < HEAD_DIM // 2
        values = []
        for head in range(own_heads):
            both = jnp.where(
                low_lanes,
                grad_query[head, at, :] * SCORE_SCALE,
                pltpu.roll(grad_key[head, at, :], HEAD_DIM, 1),
            )
            shifted = both * sine[...]
            turned = jnp.where(
                first_half,
                pltpu.roll(shifted, LANES - HEAD_DIM // 2, 1),
                -pltpu.roll(shifted, HEAD_DIM // 2, 1),
            )
            grads[:, head * LANES : (head + 1) * LANES] = (both * cosine[...] + turned).astype(BF16)
            values.append(jnp.where(low_lanes, grad_value[head, at, :], 0.0))
        base = own_heads * LANES
        grads[:, base : base + LANES] = (values[0] + pltpu.roll(values[1], HEAD_DIM, 1)).astype(
            BF16
        )
        grads[:, base + LANES : base + 2 * LANES] = values[2].astype(BF16)


def exchange(values, axis, offset):
    size = lax.axis_size(axis)
    return lax.ppermute(values, axis, [(i, i ^ offset) for i in range(size)])


def bit_count(size):
    return size.bit_length() - 1


def gather_blocks(values):
    seq_count, dp_count = lax.axis_size("seq"), lax.axis_size("dp")
    seq_at, dp_at = lax.axis_index("seq"), lax.axis_index("dp")
    parts = jnp.stack([values] + [exchange(values, "seq", k) for k in range(1, seq_count)])
    for bit in range(bit_count(seq_count)):
        split = parts.reshape((seq_count >> (bit + 1), 2, 1 << bit) + values.shape)
        split = jnp.where(((seq_at >> bit) & 1) == 1, split[:, ::-1], split)
        parts = split.reshape((seq_count,) + values.shape)
    bits = bit_count(dp_count)
    half = values.shape[1] // 2

    def spread(block, order):
        block = block.reshape((1,) * bits + block.shape)
        for bit in order:
            other = exchange(block, "dp", 1 << bit)
            upper = ((dp_at >> bit) & 1) == 1
            block = jnp.concatenate(
                [jnp.where(upper, other, block), jnp.where(upper, block, other)], bits - 1 - bit
            )
        return block

    ahead = list(range(1, bits))
    left = spread(parts[..., :half], ahead + [0])
    right = spread(parts[..., half:], ahead[::-1] + [0])
    return jnp.concatenate([left, right], -1).reshape((dp_count, seq_count) + values.shape)


def sum_to_owner(values):
    seq_count, dp_count = lax.axis_size("seq"), lax.axis_size("dp")
    part = sum_over_dp(values)
    pieces = lax.all_to_all(part, "seq", 0, 0, tiled=True)
    return jnp.sum(pieces.astype(F32), axis=0)


def sum_over_dp(values):
    dp_count = lax.axis_size("dp")
    dp_at = lax.axis_index("dp")
    bits = bit_count(dp_count)

    def halve(block, bit):
        at = bits - 1 - bit
        upper = (dp_at >> bit) & 1
        send = lax.dynamic_index_in_dim(block, 1 - upper, at, keepdims=True)
        keep = lax.dynamic_index_in_dim(block, upper, at, keepdims=True)
        other = exchange(send, "dp", 1 << bit)
        return (keep.astype(F32) + other.astype(F32)).astype(BF16)

    block = halve(values.reshape((2,) * bits + values.shape[1:]), 0)
    half = values.shape[-1] // 2
    left, right = block[..., :half], block[..., half:]
    for bit in range(1, bits):
        left = halve(left, bit)
        right = halve(right, bits - bit)
    return jnp.concatenate([left, right], -1).reshape(values.shape[1:])


def head_body(
    tokens,
    cotangent,
    doc_lengths,
    pad_counts,
    w_in,
    w_ao,
    w_fo,
    norm_gains,
    gain_moment,
    gain_second,
    stat_l_in,
    stat_r_in,
    stat_l_ao,
    stat_r_ao,
    stat_l_fo,
    stat_r_fo,
    root_l_in,
    root_r_in,
    root_l_ao,
    root_r_ao,
    root_l_fo,
    root_r_fo,
):
    token_count, width = tokens.shape
    hidden = w_fo.shape[1]
    seq_count, dp_count = lax.axis_size("seq"), lax.axis_size("dp")
    all_count = seq_count * dp_count
    row_length = token_count * seq_count
    seq_at = lax.axis_index("seq")
    dev_at = lax.axis_index(("dp", "seq"))
    head_count = width // HEAD_DIM
    own_heads = head_count // seq_count
    own_width = own_heads * HEAD_DIM
    in_rows = w_in.shape[1]
    ao_rows, fo_rows = w_ao.shape[0], w_fo.shape[0]
    out_rows = fo_rows * hidden // width
    gain_cols = norm_gains.shape[1]

    row_tokens = lax.all_gather(tokens, "seq", axis=0, tiled=True)
    gain_tile = jnp.zeros((8, width), F32).at[:2, :gain_cols].set(norm_gains)
    first_pack = gather_blocks(jnp.concatenate([w_in[0].astype(BF16), gain_tile.astype(BF16)]))
    full_qkv = first_pack[:, :, :in_rows].reshape(all_count * in_rows, width)
    gain_rows = (
        jnp.transpose(first_pack[:, :, in_rows : in_rows + 2, :gain_cols], (2, 0, 1, 3))
        .reshape(2, width)
        .astype(F32)
    )
    rest = jnp.concatenate(
        [
            w_in[1].astype(BF16),
            w_ao.astype(BF16),
            w_fo.astype(BF16).reshape(out_rows, width),
        ]
    )
    rest = lax.all_gather(rest, ("dp", "seq"), axis=0, tiled=False)
    full_up = rest[:, :in_rows].reshape(all_count * in_rows, width)
    full_ao = rest[:, in_rows : in_rows + ao_rows].reshape(width, width)
    full_fo = rest[:, in_rows + ao_rows :].reshape(width, hidden)
    root_rows = stat_r_in.shape[1]
    fo_root_rows = root_r_fo.shape[0] * hidden // width
    roots = jnp.concatenate(
        [
            root_r_in.astype(BF16).reshape(2 * root_rows, width),
            root_r_ao.astype(BF16),
            root_r_fo.astype(BF16).reshape(fo_root_rows, width),
        ]
    )
    roots = lax.all_gather(roots, ("dp", "seq"), axis=0, tiled=False)
    right_qkv = roots[:, :root_rows].reshape(width, width)
    right_up = roots[:, root_rows : 2 * root_rows].reshape(width, width)
    right_ao = roots[:, 2 * root_rows : 3 * root_rows].reshape(width, width)
    right_fo = roots[:, 3 * root_rows :].reshape(hidden, hidden)

    lengths = doc_lengths[0]
    segment, within, is_valid = doc_tables(lengths, pad_counts[0], row_length)
    pad_from = row_length - pad_counts[0]
    doc_ids = jnp.arange(lengths.shape[0], dtype=jnp.int32)
    places = jnp.arange(row_length, dtype=jnp.int32)
    doc_begin = places - within
    doc_end = doc_begin + jnp.sum(
        jnp.where(segment[:, None] == doc_ids[None, :], lengths[None, :], 0), axis=1
    )
    freq_index = jnp.arange(0, HEAD_DIM, 2, dtype=F32)
    inverse = 1.0 / jnp.power(ROPE_THETA, freq_index / HEAD_DIM)
    angles = within.astype(F32)[:, None] * inverse[None, :]
    copies = LANES // (HEAD_DIM // 2)
    cos_table = jnp.concatenate([jnp.cos(angles)] * copies, axis=1)
    sin_table = jnp.concatenate([jnp.sin(angles)] * copies, axis=1)
    lane = jnp.arange(LANES, dtype=jnp.int32)
    in_doc = lane[None, :] - HEAD_DIM == segment[:, None]
    mask_lanes = (lane >= HEAD_DIM) & (lane < HEAD_DIM + 8)
    one_lanes = (lane >= HEAD_DIM + 8) & (lane < HEAD_DIM + 11)
    query_mask = in_doc.astype(BF16)
    key_mask = jnp.where(
        mask_lanes[None, :] & ~(in_doc & is_valid[:, None]),
        MASK_BIT,
        jnp.where(one_lanes[None, :], 1.0, 0.0),
    ).astype(BF16)
    tile_starts = doc_begin[::QUERY_TILE] // KEY_ALIGN
    tile_ends = jnp.minimum(doc_end[QUERY_TILE - 1 :: QUERY_TILE], pad_from)
    tile_steps = jnp.maximum(-((tile_starts * KEY_ALIGN - tile_ends) // KEY_STEP), 0)
    tile_count = row_length // QUERY_TILE
    pad_at = pad_from[None]

    qkv_heads = lax.dynamic_slice_in_dim(
        full_qkv.reshape(3, head_count, HEAD_DIM, width), seq_at * own_heads, own_heads, 1
    )
    own_weight = jnp.concatenate(
        [
            jnp.transpose(qkv_heads[:2], (1, 0, 2, 3)).reshape(2 * own_width, width),
            qkv_heads[2].reshape(own_width, width),
            jnp.zeros((HEAD_DIM, width), BF16),
        ]
    )
    own_columns = own_weight.shape[0]
    prep_count = row_length // PREP_TILE
    key_length = row_length + PREP_TILE

    def row_block(columns):
        return pl.BlockSpec(
            (PREP_TILE, columns), lambda i: (jnp.minimum(i, prep_count - 1), 0)
        )

    def fixed_block(*shape):
        return pl.BlockSpec(shape, lambda i, *_: (0,) * len(shape))

    head_block = pl.BlockSpec((own_heads, PREP_TILE, LANES), lambda i: (0, i, 0))
    attn_in, query_ext, key_ext, value_ext = pl.pallas_call(
        project_kernel,
        grid=(prep_count + 1,),
        in_specs=[
            row_block(width),
            fixed_block(own_columns, width),
            fixed_block(1, width),
            row_block(LANES),
            row_block(LANES),
            row_block(LANES),
            row_block(LANES),
        ],
        out_specs=[
            row_block(width),
            pl.BlockSpec(
                (own_heads, PREP_TILE, LANES), lambda i: (0, jnp.minimum(i, prep_count - 1), 0)
            ),
            head_block,
            head_block,
        ],
        out_shape=[
            jax.ShapeDtypeStruct((row_length, width), BF16),
            jax.ShapeDtypeStruct((own_heads, row_length, LANES), BF16),
            jax.ShapeDtypeStruct((own_heads, key_length, LANES), BF16),
            jax.ShapeDtypeStruct((own_heads, key_length, LANES), BF16),
        ],
        compiler_params=pltpu.CompilerParams(vmem_limit_bytes=VMEM_BYTES),
        cost_estimate=pl.CostEstimate(
            flops=2 * row_length * own_columns * width,
            bytes_accessed=14_000_000,
            transcendentals=0,
        ),
        name="project",
    )(
        row_tokens,
        own_weight,
        gain_rows[:1],
        cos_table,
        sin_table,
        query_mask,
        key_mask,
    )

    def tile_block(columns):
        return pl.BlockSpec(
            (QUERY_TILE, columns), lambda i, *_: (jnp.minimum(i, tile_count - 1), 0)
        )

    head_tile = pl.BlockSpec(
        (own_heads, QUERY_TILE, LANES), lambda i, *_: (0, jnp.minimum(i, tile_count - 1), 0)
    )
    whole_keys = fixed_block(own_heads, key_length, LANES)
    pair_out, extra_out, wide_out, query_low = pl.pallas_call(
        attend_kernel,
        grid_spec=pltpu.PrefetchScalarGridSpec(
            num_scalar_prefetch=3,
            grid=(tile_count,),
            in_specs=[head_tile, whole_keys, whole_keys],
            out_specs=[tile_block(LANES), tile_block(LANES), head_tile, head_tile],
        ),
        out_shape=[
            jax.ShapeDtypeStruct((row_length, LANES), BF16),
            jax.ShapeDtypeStruct((row_length, LANES), BF16),
            jax.ShapeDtypeStruct((own_heads, row_length, LANES), F32),
            jax.ShapeDtypeStruct((own_heads, row_length, LANES), BF16),
        ],
        compiler_params=pltpu.CompilerParams(vmem_limit_bytes=VMEM_BYTES),
        cost_estimate=pl.CostEstimate(
            flops=2 * own_heads * row_length * row_length * LANES,
            bytes_accessed=12_000_000,
            transcendentals=0,
        ),
        name="attend",
    )(tile_starts, tile_steps, pad_at, query_ext, key_ext, value_ext)

    half_tokens = token_count // 2

    def fold(extra):
        blocks = extra[:, :HEAD_DIM].reshape(seq_count, 2, half_tokens, HEAD_DIM)
        return jnp.concatenate([blocks[:, 0], blocks[:, 1]], axis=-1)

    def unfold(folded):
        return jnp.concatenate([folded[:, :, :HEAD_DIM], folded[:, :, HEAD_DIM:]], axis=1)

    packed = jnp.concatenate(
        [pair_out.reshape(seq_count, token_count, LANES), fold(extra_out)], axis=1
    )
    packed = lax.all_to_all(packed, "seq", 0, 0, tiled=True)
    attn_low = jnp.concatenate([packed[:, :token_count], unfold(packed[:, token_count:])], axis=-1)
    attn_low = jnp.transpose(attn_low, (1, 0, 2)).reshape(token_count, width)

    inputs = tokens.astype(F32)
    residual = inputs + apply_rows(attn_low, full_ao)
    normed_two, spread_two = norm_forward(residual)
    ffn_in = (normed_two * gain_rows[1]).astype(BF16)
    projected = apply_rows(ffn_in, full_up)
    inner_part = projected[:, :hidden]
    gate_part = projected[:, hidden:]
    activated = gelu_value(inner_part)
    mid_low = (activated * gate_part).astype(BF16)
    layer_out = (residual + apply_rows(mid_low, full_fo)).astype(BF16)
    grad_mid = jnp.dot(cotangent, full_fo, preferred_element_type=F32)
    grad_proj = jnp.concatenate(
        [grad_mid * gate_part * gelu_slope(inner_part), grad_mid * activated], axis=1
    ).astype(BF16)
    grad_ffn_in = jnp.dot(grad_proj, full_up, preferred_element_type=F32)
    grad_norm_two, _ = norm_backward(grad_ffn_in, normed_two, spread_two, gain_rows[1])
    grad_resid = cotangent.astype(F32) + grad_norm_two
    grad_out_attn = grad_resid.astype(BF16)
    grad_attn = jnp.dot(grad_out_attn, full_ao, preferred_element_type=F32).astype(BF16)

    grad_blocks = jnp.transpose(
        grad_attn.reshape(token_count, seq_count, own_width), (1, 0, 2)
    )
    folded = grad_blocks[:, :, LANES:].reshape(seq_count, 2, half_tokens, HEAD_DIM)
    packed_back = jnp.concatenate(
        [grad_blocks[:, :, :LANES], jnp.concatenate([folded[:, 0], folded[:, 1]], axis=-1)], axis=1
    )
    packed_back = lax.all_to_all(packed_back, "seq", 0, 0, tiled=True)
    grad_pair = packed_back[:, :token_count].reshape(row_length, LANES)
    grad_extra = unfold(packed_back[:, token_count:]).reshape(row_length, HEAD_DIM)
    grad_extra = jnp.pad(grad_extra, ((0, 0), (0, LANES - HEAD_DIM)))

    grad_up_term = outer_sum(grad_proj, ffn_in).astype(BF16).reshape(all_count, in_rows, width)
    grad_ao_term = outer_sum(grad_out_attn, attn_low).astype(BF16)
    grad_fo_term = outer_sum(cotangent, mid_low).astype(BF16)
    terms = jnp.concatenate(
        [
            grad_up_term,
            grad_ao_term.reshape(all_count, ao_rows, width),
            grad_fo_term.reshape(all_count, out_rows, width),
        ],
        axis=1,
    )
    summed = sum_to_owner(terms.reshape((dp_count, seq_count) + terms.shape[1:]))
    summed_up = summed[:in_rows]
    summed_ao = summed[in_rows : in_rows + ao_rows]
    summed_fo = summed[in_rows + ao_rows :].reshape(fo_rows, hidden)
    whole = gather_blocks(summed.astype(BF16)).reshape(all_count, summed.shape[0], width)
    whole_up = whole[:, :in_rows].reshape(all_count * in_rows, width)
    whole_ao = whole[:, in_rows : in_rows + ao_rows].reshape(width, width)
    whole_fo = whole[:, in_rows + ao_rows :].reshape(width, hidden)

    finish_count = prep_count

    def finish_block(columns):
        return pl.BlockSpec(
            (PREP_TILE, columns), lambda i, *_: (jnp.maximum(i - tile_count, 0), 0)
        )

    grad_qkv = pl.pallas_call(
        attend_back_kernel,
        grid_spec=pltpu.PrefetchScalarGridSpec(
            num_scalar_prefetch=3,
            grid=(tile_count + finish_count,),
            in_specs=[
                head_tile,
                head_tile,
                tile_block(LANES),
                tile_block(LANES),
                whole_keys,
                whole_keys,
                finish_block(LANES),
                finish_block(LANES),
            ],
            out_specs=finish_block(own_columns),
            scratch_shapes=[
                pltpu.VMEM((own_heads, row_length, LANES), F32),
                pltpu.VMEM((own_heads, key_length, LANES), F32),
                pltpu.VMEM((own_heads, key_length, LANES), F32),
            ],
        ),
        out_shape=jax.ShapeDtypeStruct((row_length, own_columns), BF16),
        compiler_params=pltpu.CompilerParams(vmem_limit_bytes=VMEM_BYTES),
        cost_estimate=pl.CostEstimate(
            flops=5 * own_heads * row_length * row_length * LANES,
            bytes_accessed=15_000_000,
            transcendentals=0,
        ),
        name="attend_back",
    )(
        tile_starts,
        tile_steps,
        pad_at,
        query_low,
        wide_out,
        grad_pair,
        grad_extra,
        key_ext,
        value_ext,
        cos_table,
        sin_table,
    )
    qkv_term = outer_sum(grad_qkv, attn_in)[: 3 * own_width].astype(BF16)
    qkv_sum = sum_over_dp(qkv_term.reshape(dp_count, 3 * own_width // dp_count, width))
    qkv_parts = jnp.transpose(gather_blocks(qkv_sum), (1, 0, 2, 3)).reshape(
        seq_count, 3 * own_width, width
    )
    whole_query_key = qkv_parts[:, : 2 * own_width].reshape(
        seq_count, own_heads, 2, HEAD_DIM, width
    )
    whole_qkv = jnp.concatenate(
        [
            jnp.transpose(whole_query_key, (2, 0, 1, 3, 4)),
            qkv_parts[:, 2 * own_width :].reshape(1, seq_count, own_heads, HEAD_DIM, width),
        ]
    ).reshape(3 * width, width)
    summed_qkv = lax.dynamic_slice_in_dim(whole_qkv, dev_at * in_rows, in_rows, 0).astype(F32)

    input_term = jnp.dot(grad_qkv, own_weight, preferred_element_type=F32).astype(BF16)
    grad_attn_in = lax.psum_scatter(input_term, "seq", scatter_dimension=0, tiled=True).astype(F32)
    normed_one, spread_one = norm_forward(inputs)
    grad_norm_one, _ = norm_backward(grad_attn_in, normed_one, spread_one, gain_rows[0])
    grad_input = grad_resid + grad_norm_one

    def own_columns_of(matrix, count):
        return lax.dynamic_slice_in_dim(matrix, dev_at * count, count, 1)

    def gain_gradient(weight, gradient, gain):
        own_weight_columns = own_columns_of(weight, gain_cols).astype(F32)
        products = own_weight_columns * own_columns_of(gradient, gain_cols).astype(F32)
        own_gain = lax.dynamic_slice_in_dim(gain, dev_at * gain_cols, gain_cols)
        return jnp.sum(products, axis=0) / own_gain

    summed_gains = jnp.stack(
        [
            gain_gradient(full_qkv, whole_qkv, gain_rows[0]),
            gain_gradient(full_up, whole_up, gain_rows[1]),
        ]
    )
    new_moment = 0.9 * gain_moment + 0.1 * summed_gains
    new_second = 0.999 * gain_second + 0.001 * summed_gains * summed_gains
    new_gains = norm_gains - ADAM_RATE * new_moment / (jnp.sqrt(new_second) + 1e-08)

    def refresh(weight, own, full, stat_left, stat_right, root_left, right):
        new_left = 0.5 * stat_left + 0.5 * apply_rows(own.astype(BF16), full)
        columns = own_columns_of(full, stat_right.shape[0])
        new_right = 0.5 * stat_right + 0.5 * outer_sum(columns, full)
        left_product = jnp.dot(root_left.astype(BF16), full, preferred_element_type=F32)
        update = jnp.dot(left_product.astype(BF16), right, preferred_element_type=F32)
        return new_left, new_right, weight - SHAMPOO_RATE * update

    left_up, right_stat_up, new_up = refresh(
        w_in[1], summed_up, whole_up, stat_l_in[1], stat_r_in[1], root_l_in[1], right_up
    )
    left_ao, right_stat_ao, new_ao = refresh(
        w_ao, summed_ao, whole_ao, stat_l_ao, stat_r_ao, root_l_ao, right_ao
    )
    left_fo, right_stat_fo, new_fo = refresh(
        w_fo, summed_fo, whole_fo, stat_l_fo, stat_r_fo, root_l_fo, right_fo
    )
    left_qkv, right_stat_qkv, new_qkv = refresh(
        w_in[0], summed_qkv, whole_qkv, stat_l_in[0], stat_r_in[0], root_l_in[0], right_qkv
    )
    return (
        layer_out,
        grad_input,
        jnp.stack([summed_qkv, summed_up]),
        summed_ao,
        summed_fo,
        summed_gains,
        new_moment,
        new_second,
        new_gains,
        jnp.stack([left_qkv, left_up]),
        jnp.stack([right_stat_qkv, right_stat_up]),
        left_ao,
        right_stat_ao,
        left_fo,
        right_stat_fo,
        jnp.stack([new_qkv, new_up]),
        new_ao,
        new_fo,
    )


def body(tokens, *others):
    seq_count, dp_count = lax.axis_size("seq"), lax.axis_size("dp")
    token_count, width = tokens.shape
    row_length = token_count * seq_count
    by_heads = (
        width // HEAD_DIM == 3 * seq_count
        and dp_count & (dp_count - 1) == 0
        and seq_count & (seq_count - 1) == 0
        and row_length % QUERY_TILE == 0
        and row_length % PREP_TILE == 0
        and others[1].shape[1] == 8
    )
    return head_body(tokens, *others) if by_heads else sequence_body(tokens, *others)


def solution(mesh):
    in_specs = (
        P(("dp", "seq"), None),
        P(("dp", "seq"), None),
        P("dp", None),
        P("dp"),
        P(None, ("dp", "seq"), None),
        P(("dp", "seq"), None),
        P(("dp", "seq"), None),
        P(None, ("dp", "seq")),
        P(None, ("dp", "seq")),
        P(None, ("dp", "seq")),
        P(None, ("dp", "seq"), None),
        P(None, ("dp", "seq"), None),
        P(("dp", "seq"), None),
        P(("dp", "seq"), None),
        P(("dp", "seq"), None),
        P(("dp", "seq"), None),
        P(None, ("dp", "seq"), None),
        P(None, ("dp", "seq"), None),
        P(("dp", "seq"), None),
        P(("dp", "seq"), None),
        P(("dp", "seq"), None),
        P(("dp", "seq"), None),
    )
    out_specs = (
        P(("dp", "seq"), None),
        P(("dp", "seq"), None),
        P(None, ("dp", "seq"), None),
        P(("dp", "seq"), None),
        P(("dp", "seq"), None),
        P(None, ("dp", "seq")),
        P(None, ("dp", "seq")),
        P(None, ("dp", "seq")),
        P(None, ("dp", "seq")),
        P(None, ("dp", "seq"), None),
        P(None, ("dp", "seq"), None),
        P(("dp", "seq"), None),
        P(("dp", "seq"), None),
        P(("dp", "seq"), None),
        P(("dp", "seq"), None),
        P(None, ("dp", "seq"), None),
        P(("dp", "seq"), None),
        P(("dp", "seq"), None),
    )
    return jax.shard_map(body, mesh=mesh, in_specs=in_specs, out_specs=out_specs, check_vma=False)
```

```python
import functools
import math

import jax
import jax.numpy as jnp
from jax import lax
from jax.experimental import pallas as pl
from jax.experimental.pallas import tpu as pltpu
from jax.sharding import PartitionSpec as P

HEAD_DIM = 64


NORM_EPS = 1e-05
ROPE_THETA = 160000.0
SCORE_SCALE = 0.125
MASK_FILL = -1e30
ADAM_RATE = 0.2
SHAMPOO_RATE = 1.0
HIGHEST = lax.Precision.HIGHEST


def norm_forward(values):
    center = values - jnp.mean(values, axis=-1, keepdims=True)
    inv_spread = lax.rsqrt(jnp.mean(center * center, axis=-1, keepdims=True) + NORM_EPS)
    return (center * inv_spread, inv_spread)


def norm_backward(grad_out, normed, inv_spread, gain_row):
    scaled = grad_out * gain_row
    inner_term = (
        scaled
        - jnp.mean(scaled, axis=-1, keepdims=True)
        - normed * jnp.mean(scaled * normed, axis=-1, keepdims=True)
    )
    return (inner_term * inv_spread, jnp.sum(grad_out * normed, axis=0))


def gelu_value(inputs):
    return 0.5 * inputs * (1.0 + lax.erf(inputs * (1.0 / math.sqrt(2.0))))


def gelu_slope(inputs):
    cumulative = 0.5 * (1.0 + lax.erf(inputs * (1.0 / math.sqrt(2.0))))
    return cumulative + inputs * jnp.exp(-0.5 * inputs * inputs) * (1.0 / math.sqrt(2.0 * math.pi))


def rotate(values, cos_table, sin_table):
    half_dim = values.shape[-1] // 2
    turned = jnp.concatenate([-values[..., half_dim:], values[..., :half_dim]], axis=-1)
    return values * cos_table + turned * sin_table


def unrotate(gradient, cos_table, sin_table):
    half_dim = gradient.shape[-1] // 2
    shifted = gradient * sin_table
    back_turn = jnp.concatenate([shifted[..., half_dim:], -shifted[..., :half_dim]], axis=-1)
    return gradient * cos_table + back_turn


def rope_tables(within):
    freq_index = jnp.arange(0, HEAD_DIM, 2, dtype=jnp.float32)
    inverse = 1.0 / jnp.power(ROPE_THETA, freq_index / HEAD_DIM)
    angles = within.astype(jnp.float32)[:, None] * inverse[None, :]
    angles = jnp.concatenate([angles, angles], axis=-1)
    return (jnp.cos(angles), jnp.sin(angles))


def doc_tables(lengths_row, pad_count, row_length):
    doc_order = jnp.arange(lengths_row.shape[0], dtype=jnp.int32)
    doc_ends = jnp.sum(
        jnp.where(doc_order[:, None] >= doc_order[None, :], lengths_row[None, :], 0), axis=1
    )
    starts = doc_ends - lengths_row
    places = jnp.arange(row_length, dtype=jnp.int32)
    segment = jnp.sum((places[:, None] >= doc_ends[None, :]).astype(jnp.int32), axis=1)
    doc_ids = jnp.arange(lengths_row.shape[0], dtype=jnp.int32)
    doc_begin = jnp.sum(jnp.where(segment[:, None] == doc_ids[None, :], starts[None, :], 0), axis=1)
    is_valid = places < row_length - pad_count
    return (segment, places - doc_begin, is_valid)


def apply_rows(activations, weight):
    return lax.dot_general(
        activations, weight, (((1,), (1,)), ((), ())), preferred_element_type=jnp.float32
    )


def outer_sum(grad_rows, act_rows):
    return lax.dot_general(
        grad_rows, act_rows, (((0,), (0,)), ((), ())), preferred_element_type=jnp.float32
    )


def sequence_body(
    tokens,
    cotangent,
    doc_lengths,
    pad_counts,
    w_in,
    w_ao,
    w_fo,
    norm_gains,
    gain_moment,
    gain_second,
    stat_l_in,
    stat_r_in,
    stat_l_ao,
    stat_r_ao,
    stat_l_fo,
    stat_r_fo,
    root_l_in,
    root_r_in,
    root_l_ao,
    root_r_ao,
    root_l_fo,
    root_r_fo,
):
    token_count, model_width = tokens.shape
    head_count = model_width // HEAD_DIM
    pair_count = head_count // 2
    pair_width = 2 * HEAD_DIM
    hidden_width = w_fo.shape[1]
    seq_count = lax.axis_size("seq")
    row_length = token_count * seq_count
    first_place = lax.axis_index("seq") * token_count
    segment, within, is_valid = doc_tables(doc_lengths[0], pad_counts[0], row_length)
    own_places = first_place + jnp.arange(token_count, dtype=jnp.int32)
    all_places = jnp.arange(row_length, dtype=jnp.int32)
    own_segment = lax.dynamic_slice_in_dim(segment, first_place, token_count)
    own_within = lax.dynamic_slice_in_dim(within, first_place, token_count)
    allowed = (own_segment[:, None] == segment[None, :]) & (
        is_valid[None, :] | (own_places[:, None] == all_places[None, :])
    )
    cos_table, sin_table = rope_tables(own_within)
    cos_table = cos_table[:, None, :]
    sin_table = sin_table[:, None, :]
    low_weights = (
        w_in.astype(jnp.bfloat16),
        w_ao.astype(jnp.bfloat16),
        w_fo.astype(jnp.bfloat16),
        norm_gains.astype(jnp.bfloat16),
    )
    full_in, full_ao, full_fo, full_gains = (
        lax.all_gather(low_weights[0], ("dp", "seq"), axis=1, tiled=True),
        lax.all_gather(low_weights[1], ("dp", "seq"), axis=0, tiled=True),
        lax.all_gather(low_weights[2], ("dp", "seq"), axis=0, tiled=True),
        lax.all_gather(low_weights[3], ("dp", "seq"), axis=1, tiled=True),
    )
    gain_rows = full_gains.astype(jnp.float32)
    inputs = tokens.astype(jnp.float32)
    normed_one, spread_one = norm_forward(inputs)
    attn_in = (normed_one * gain_rows[0]).astype(jnp.bfloat16)
    qkv_raw = apply_rows(attn_in, full_in[0])
    query_low = (
        rotate(
            qkv_raw[:, :model_width].reshape(token_count, head_count, HEAD_DIM),
            cos_table,
            sin_table,
        )
        .reshape(token_count, model_width)
        .astype(jnp.bfloat16)
    )
    key_low = (
        rotate(
            qkv_raw[:, model_width : 2 * model_width].reshape(token_count, head_count, HEAD_DIM),
            cos_table,
            sin_table,
        )
        .reshape(token_count, model_width)
        .astype(jnp.bfloat16)
    )
    value_low = qkv_raw[:, 2 * model_width :].astype(jnp.bfloat16)
    keys_all, values_all = (
        lax.all_gather(key_low, "seq", axis=0, tiled=True),
        lax.all_gather(value_low, "seq", axis=0, tiled=True),
    )

    def pair_slice(matrix, pair_index):
        return lax.dynamic_slice_in_dim(matrix, pair_index * pair_width, pair_width, 1).reshape(
            matrix.shape[0], 2, HEAD_DIM
        )

    def pair_scores(query_pair, key_pair, allow_mask):
        raw_scores = (
            jnp.einsum("thd,khd->htk", query_pair, key_pair, preferred_element_type=jnp.float32)
            * SCORE_SCALE
        )
        return jnp.where(allow_mask[None], raw_scores, MASK_FILL)

    def forward_pair(loop_carry, pair_index):
        scores = pair_scores(
            pair_slice(query_low, pair_index), pair_slice(keys_all, pair_index), allowed
        )
        row_max = jnp.max(scores, axis=-1, keepdims=True)
        exponent = jnp.exp(scores - row_max)
        row_sum = jnp.sum(exponent, axis=-1, keepdims=True)
        weights_low = (exponent / row_sum).astype(jnp.bfloat16)
        attended = jnp.einsum(
            "htk,khd->thd",
            weights_low,
            pair_slice(values_all, pair_index),
            preferred_element_type=jnp.float32,
        )
        return (
            loop_carry,
            (attended.reshape(token_count, pair_width), (row_max + jnp.log(row_sum))[..., 0]),
        )

    unused, (attended_pairs, log_norms) = lax.scan(forward_pair, 0, jnp.arange(pair_count))
    attn_low = (
        jnp.transpose(attended_pairs, (1, 0, 2))
        .reshape(token_count, model_width)
        .astype(jnp.bfloat16)
    )
    residual = inputs + apply_rows(attn_low, full_ao)
    normed_two, spread_two = norm_forward(residual)
    ffn_in = (normed_two * gain_rows[1]).astype(jnp.bfloat16)
    projected = apply_rows(ffn_in, full_in[1])
    inner_part = projected[:, :hidden_width]
    gate_part = projected[:, hidden_width:]
    activated = gelu_value(inner_part)
    mid_low = (activated * gate_part).astype(jnp.bfloat16)
    layer_out = (residual + apply_rows(mid_low, full_fo)).astype(jnp.bfloat16)
    back_in, back_ao, back_fo, back_gains = (
        lax.all_gather(low_weights[0], ("dp", "seq"), axis=1, tiled=True),
        lax.all_gather(low_weights[1], ("dp", "seq"), axis=0, tiled=True),
        lax.all_gather(low_weights[2], ("dp", "seq"), axis=0, tiled=True),
        lax.all_gather(low_weights[3], ("dp", "seq"), axis=1, tiled=True),
    )
    back_rows = back_gains.astype(jnp.float32)
    grad_fo_w = outer_sum(cotangent, mid_low)
    grad_mid = jnp.dot(cotangent, back_fo, preferred_element_type=jnp.float32)
    grad_proj = jnp.concatenate(
        [grad_mid * gate_part * gelu_slope(inner_part), grad_mid * activated], axis=1
    ).astype(jnp.bfloat16)
    grad_ffn_w = outer_sum(grad_proj, ffn_in)
    grad_ffn_in = jnp.dot(grad_proj, back_in[1], preferred_element_type=jnp.float32)
    grad_norm_two, grad_gain_two = norm_backward(grad_ffn_in, normed_two, spread_two, back_rows[1])
    grad_resid = cotangent.astype(jnp.float32) + grad_norm_two
    grad_out_attn = grad_resid.astype(jnp.bfloat16)
    grad_ao_w = outer_sum(grad_out_attn, attn_low)
    grad_attn = jnp.dot(grad_out_attn, back_ao, preferred_element_type=jnp.float32).astype(
        jnp.bfloat16
    )

    def query_side_grads(pair_index):
        query_pair = pair_slice(query_low, pair_index)
        key_pair = pair_slice(keys_all, pair_index)
        value_pair = pair_slice(values_all, pair_index)
        grad_pair = pair_slice(grad_attn, pair_index)
        scores = pair_scores(query_pair, key_pair, allowed)
        softmax_out = jnp.exp(scores - log_norms[pair_index][..., None])
        grad_weights = jnp.einsum(
            "thd,khd->htk", grad_pair, value_pair, preferred_element_type=jnp.float32
        )
        delta_row = jnp.sum(softmax_out * grad_weights, axis=-1, keepdims=True)
        grad_scores = (softmax_out * (grad_weights - delta_row)).astype(jnp.bfloat16)
        grad_query = (
            jnp.einsum("htk,khd->thd", grad_scores, key_pair, preferred_element_type=jnp.float32)
            * SCORE_SCALE
        )
        return (query_pair, grad_pair, softmax_out, grad_scores, grad_query, delta_row)

    def backward_pair(loop_carry, pair_index):
        query_pair, grad_pair, softmax_out, grad_scores, grad_query, delta_row = query_side_grads(
            pair_index
        )
        grad_key = (
            jnp.einsum("htk,thd->khd", grad_scores, query_pair, preferred_element_type=jnp.float32)
            * SCORE_SCALE
        )
        grad_value = jnp.einsum(
            "htk,thd->khd",
            softmax_out.astype(jnp.bfloat16),
            grad_pair,
            preferred_element_type=jnp.float32,
        )
        return (
            loop_carry,
            (
                grad_query.reshape(token_count, pair_width),
                grad_key.reshape(row_length, pair_width),
                grad_value.reshape(row_length, pair_width),
            ),
        )

    unused, (grad_query_pairs, grad_key_parts, grad_value_parts) = lax.scan(
        backward_pair, 0, jnp.arange(pair_count)
    )
    grad_key_pairs, grad_value_pairs = (
        lax.psum_scatter(
            grad_key_parts.astype(jnp.bfloat16), "seq", scatter_dimension=1, tiled=True
        ).astype(jnp.float32),
        lax.psum_scatter(
            grad_value_parts.astype(jnp.bfloat16), "seq", scatter_dimension=1, tiled=True
        ).astype(jnp.float32),
    )

    def heads_of(pairs_array):
        return jnp.transpose(pairs_array, (1, 0, 2)).reshape(token_count, head_count, HEAD_DIM)

    grad_qkv = jnp.concatenate(
        [
            unrotate(heads_of(grad_query_pairs), cos_table, sin_table).reshape(
                token_count, model_width
            ),
            unrotate(heads_of(grad_key_pairs), cos_table, sin_table).reshape(
                token_count, model_width
            ),
            heads_of(grad_value_pairs).reshape(token_count, model_width),
        ],
        axis=1,
    ).astype(jnp.bfloat16)
    grad_qkv_w = outer_sum(grad_qkv, attn_in)
    grad_attn_in = jnp.dot(grad_qkv, back_in[0], preferred_element_type=jnp.float32)
    grad_norm_one, grad_gain_one = norm_backward(grad_attn_in, normed_one, spread_one, back_rows[0])
    grad_input = grad_resid + grad_norm_one
    w_terms = jnp.stack([grad_qkv_w, grad_ffn_w])
    gain_terms = jnp.stack([grad_gain_one, grad_gain_two])
    summed_in, summed_ao, summed_fo, summed_gains = (
        lax.psum_scatter(w_terms, ("dp", "seq"), scatter_dimension=1, tiled=True),
        lax.psum_scatter(grad_ao_w, ("dp", "seq"), scatter_dimension=0, tiled=True),
        lax.psum_scatter(grad_fo_w, ("dp", "seq"), scatter_dimension=0, tiled=True),
        lax.psum_scatter(gain_terms, ("dp", "seq"), scatter_dimension=1, tiled=True),
    )
    new_moment = 0.9 * gain_moment + 0.1 * summed_gains
    new_second = 0.999 * gain_second + 0.001 * summed_gains * summed_gains
    new_gains = norm_gains - ADAM_RATE * new_moment / (jnp.sqrt(new_second) + 1e-08)
    whole_in, whole_ao, whole_fo = (
        lax.all_gather(summed_in.astype(jnp.bfloat16), ("dp", "seq"), axis=1, tiled=True).astype(
            summed_in.dtype
        ),
        lax.all_gather(summed_ao.astype(jnp.bfloat16), ("dp", "seq"), axis=0, tiled=True).astype(
            summed_ao.dtype
        ),
        lax.all_gather(summed_fo.astype(jnp.bfloat16), ("dp", "seq"), axis=0, tiled=True).astype(
            summed_fo.dtype
        ),
    )
    dev_index = lax.axis_index(("dp", "seq"))

    def refresh(grad_shard, grad_full, stat_left, stat_right, root_right):
        col_count = stat_right.shape[1]
        new_left = 0.5 * stat_left + 0.5 * jnp.einsum(
            "arn,amn->arm", grad_shard, grad_full, precision=HIGHEST
        )
        full_cols = lax.dynamic_slice_in_dim(grad_full, dev_index * col_count, col_count, 2)
        new_right = 0.5 * stat_right + 0.5 * jnp.einsum(
            "amc,amn->acn", full_cols, grad_full, precision=HIGHEST
        )
        applied = jnp.einsum("amn,acn->amc", grad_full, root_right, precision=HIGHEST)
        return (new_left, new_right, applied)

    left_in, right_in, applied_in = refresh(summed_in, whole_in, stat_l_in, stat_r_in, root_r_in)
    left_ao, right_ao, applied_ao = refresh(
        summed_ao[None], whole_ao[None], stat_l_ao[None], stat_r_ao[None], root_r_ao[None]
    )
    left_fo, right_fo, applied_fo = refresh(
        summed_fo[None], whole_fo[None], stat_l_fo[None], stat_r_fo[None], root_r_fo[None]
    )
    product_in, product_ao, product_fo = (
        lax.all_gather(applied_in.astype(jnp.bfloat16), ("dp", "seq"), axis=2, tiled=True).astype(
            applied_in.dtype
        ),
        lax.all_gather(applied_ao.astype(jnp.bfloat16), ("dp", "seq"), axis=2, tiled=True).astype(
            applied_ao.dtype
        ),
        lax.all_gather(applied_fo.astype(jnp.bfloat16), ("dp", "seq"), axis=2, tiled=True).astype(
            applied_fo.dtype
        ),
    )
    new_w_in = w_in - SHAMPOO_RATE * jnp.einsum(
        "arm,amn->arn", root_l_in, product_in, precision=HIGHEST
    )
    new_w_ao = (
        w_ao
        - SHAMPOO_RATE
        * jnp.einsum("arm,amn->arn", root_l_ao[None], product_ao, precision=HIGHEST)[0]
    )
    new_w_fo = (
        w_fo
        - SHAMPOO_RATE
        * jnp.einsum("arm,amn->arn", root_l_fo[None], product_fo, precision=HIGHEST)[0]
    )
    return (
        layer_out,
        grad_input,
        summed_in,
        summed_ao,
        summed_fo,
        summed_gains,
        new_moment,
        new_second,
        new_gains,
        left_in,
        right_in,
        left_ao[0],
        right_ao[0],
        left_fo[0],
        right_fo[0],
        new_w_in,
        new_w_ao,
        new_w_fo,
    )


QUERY_TILE = 480
ROW_ALIGN = 16
KEY_STEP = 512
KEY_ALIGN = 128
PREP_TILE = 480
LANES = 128
REFRESH_ROWS = 384
MASK_BIT = -(2.0**100)
NO_MAX = -3e38
BF16 = jnp.bfloat16
F32 = jnp.float32
VMEM_BYTES = 56 * 2**20


def dot_rows(left, right):
    return lax.dot_general(left, right, (((1,), (1,)), ((), ())), preferred_element_type=F32)


def dot_plain(left, right):
    return lax.dot_general(left, right, (((1,), (0,)), ((), ())), preferred_element_type=F32)


def dot_first(left, right):
    return lax.dot_general(left, right, (((0,), (0,)), ((), ())), preferred_element_type=F32)


def lane_index(rows):
    return lax.broadcasted_iota(jnp.int32, (rows, LANES), 1)


def three_pieces(column):
    first = column.astype(BF16).astype(F32)
    second = (column - first).astype(BF16).astype(F32)
    return first, second, column - first - second


def with_pieces(values, column, lane, at):
    one, two, three = three_pieces(column)
    return jnp.where(
        lane == at, one, jnp.where(lane == at + 1, two, jnp.where(lane == at + 2, three, values))
    ).astype(BF16)


def project_kernel(
    tokens, weight, gain, cosine, sine, query_mask, key_mask, attn_in, query, key, value
):
    step = pl.program_id(0)
    last = pl.num_programs(0) - 1
    own_heads = query.shape[0]
    rows = tokens.shape[0]
    lane = lane_index(rows)
    low_lanes = lane < HEAD_DIM

    @pl.when(step < last)
    def compute():
        normed = norm_forward(tokens[...].astype(F32))[0]
        low = (normed * gain[...]).astype(BF16)
        attn_in[...] = low
        raw = dot_rows(low, weight[...])
        first_half = lane % HEAD_DIM < HEAD_DIM // 2
        ones = jnp.where(lane < HEAD_DIM + 3, 1.0, 0.0)
        for head in range(own_heads):
            both = raw[:, head * LANES : (head + 1) * LANES]
            turned = jnp.where(
                first_half,
                -pltpu.roll(both, LANES - HEAD_DIM // 2, 1),
                pltpu.roll(both, HEAD_DIM // 2, 1),
            )
            both = both * cosine[...] + turned * sine[...]
            query[head] = jnp.where(
                low_lanes, both * SCORE_SCALE, query_mask[...].astype(F32)
            ).astype(BF16)
            key[head] = jnp.where(
                low_lanes, pltpu.roll(both, HEAD_DIM, 1), key_mask[...].astype(F32)
            ).astype(BF16)
            at = own_heads + head // 2
            pair = raw[:, at * LANES : (at + 1) * LANES]
            if head % 2:
                pair = pltpu.roll(pair, HEAD_DIM, 1)
            value[head] = jnp.where(low_lanes, pair, ones).astype(BF16)

    @pl.when(step == last)
    def pad():
        blocked = jnp.where(
            low_lanes,
            0.0,
            jnp.where(lane < HEAD_DIM + 8, MASK_BIT, jnp.where(lane < HEAD_DIM + 11, 1.0, 0.0)),
        ).astype(BF16)
        for head in range(own_heads):
            key[head] = blocked
            value[head] = jnp.zeros((rows, LANES), BF16)


def attend_kernel(
    start_at, step_count, pad_from, query, key, value, pair_out, extra_out, query_out
):
    tile = pl.program_id(0)
    own_heads, rows, _ = query.shape
    lane = lane_index(rows)
    low_lanes = lane < HEAD_DIM
    place = tile * rows + lax.broadcasted_iota(jnp.int32, (rows, 1), 0)
    padded = place >= pad_from[0]
    own_rows = pl.ds(pl.multiple_of(tile * rows, ROW_ALIGN), rows)
    maxima, totals = [], []
    for head in range(own_heads):
        products = query[head].astype(F32) * key[head, own_rows, :].astype(F32)
        self_score = jnp.sum(jnp.where(low_lanes, products, 0.0), axis=1, keepdims=True)
        maxima.append(jnp.where(padded, self_score, NO_MAX))
        totals.append(jnp.where(padded, value[head, own_rows, :].astype(F32), 0.0))
    first = start_at[tile] * KEY_ALIGN

    def step(index, carry):
        maxima, totals = carry
        at = pl.ds(pl.multiple_of(first + index * KEY_STEP, KEY_ALIGN), KEY_STEP)
        new_maxima, new_totals = [], []
        for head in range(own_heads):
            scores = dot_rows(query[head], key[head, at, :])
            row_max = jnp.maximum(maxima[head], jnp.max(scores, axis=1, keepdims=True))
            weights = jnp.exp(scores - row_max).astype(BF16)
            new_totals.append(
                totals[head] * jnp.exp(maxima[head] - row_max)
                + dot_plain(weights, value[head, at, :])
            )
            new_maxima.append(row_max)
        return new_maxima, new_totals

    maxima, totals = lax.fori_loop(0, step_count[tile], step, (maxima, totals))
    outs = []
    for head in range(own_heads):
        row_sum = totals[head][:, HEAD_DIM : HEAD_DIM + 1]
        outs.append(jnp.where(low_lanes, totals[head] * (1.0 / row_sum), 0.0))
        query_out[head] = with_pieces(
            query[head].astype(F32), -(maxima[head] + jnp.log(row_sum)), lane, HEAD_DIM + 8
        )
    pair_out[...] = (outs[0] + pltpu.roll(outs[1], HEAD_DIM, 1)).astype(BF16)
    extra_out[...] = outs[2].astype(BF16)


def attend_back_kernel(
    start_at,
    step_count,
    pad_from,
    query,
    pair_out,
    extra_out,
    grad_pair,
    grad_extra,
    key,
    value,
    cosine,
    sine,
    grads,
    grad_query,
    grad_key,
    grad_value,
):
    tile = pl.program_id(0)
    own_heads, rows, _ = query.shape
    tile_count = grad_query.shape[1] // rows

    @pl.when(tile == 0)
    def clear():
        grad_key[...] = jnp.zeros_like(grad_key)
        grad_value[...] = jnp.zeros_like(grad_value)

    @pl.when(tile < tile_count)
    def accumulate():
        lane = lane_index(rows)
        low_lanes = lane < HEAD_DIM
        own_rows = pl.ds(pl.multiple_of(tile * rows, ROW_ALIGN), rows)
        first = start_at[tile] * KEY_ALIGN
        pair = grad_pair[...].astype(F32)
        extra = grad_extra[...].astype(F32)
        pair_product = pair * pair_out[...].astype(F32)
        products = [
            jnp.where(low_lanes, pair_product, 0.0),
            jnp.where(low_lanes, 0.0, pair_product),
            extra * extra_out[...].astype(F32),
        ]
        incoming = [pair, pltpu.roll(pair, HEAD_DIM, 1), extra]
        grads_out = []
        for head in range(own_heads):
            own = jnp.where(low_lanes, incoming[head], 0.0)
            delta = jnp.sum(products[head], axis=1, keepdims=True)
            grads_out.append(with_pieces(own, -delta, lane, HEAD_DIM))

        def step(index, carry):
            at = pl.ds(pl.multiple_of(first + index * KEY_STEP, KEY_ALIGN), KEY_STEP)
            sums = []
            for head in range(own_heads):
                keys = key[head, at, :]
                probs = jnp.exp(dot_rows(keys, query[head]))
                grad_scores = (probs * dot_rows(value[head, at, :], grads_out[head])).astype(BF16)
                grad_value[head, at, :] += dot_plain(probs.astype(BF16), grads_out[head])
                grad_key[head, at, :] += dot_plain(grad_scores, query[head])
                sums.append(carry[head] + dot_first(grad_scores, keys))
            return sums

        zeros = [jnp.zeros((rows, LANES), F32) for _ in range(own_heads)]
        sums = lax.fori_loop(0, step_count[tile], step, zeros)
        for head in range(own_heads):
            grad_query[head, own_rows, :] = sums[head]

        @pl.when((tile + 1) * rows > pad_from[0])
        def self_terms():
            place = tile * rows + lax.broadcasted_iota(jnp.int32, (rows, 1), 0)
            padded = place >= pad_from[0]
            for head in range(own_heads):
                keys = key[head, own_rows, :].astype(F32)
                queries = query[head].astype(F32)
                outs = grads_out[head].astype(F32)
                counted = low_lanes | (lane >= HEAD_DIM + 8)
                score = jnp.sum(jnp.where(counted, queries * keys, 0.0), axis=1, keepdims=True)
                prob = jnp.where(padded, jnp.exp(jnp.where(padded, score, 0.0)), 0.0)
                grad_prob = jnp.sum(
                    outs * value[head, own_rows, :].astype(F32), axis=1, keepdims=True
                )
                grad_score = (prob * grad_prob).astype(BF16).astype(F32)
                low_prob = prob.astype(BF16).astype(F32)
                grad_query[head, own_rows, :] += grad_score * jnp.where(low_lanes, keys, 0.0)
                grad_key[head, own_rows, :] += grad_score * queries
                grad_value[head, own_rows, :] += low_prob * outs

    @pl.when(tile >= tile_count)
    def finish():
        size = grads.shape[0]
        at = pl.ds(pl.multiple_of((tile - tile_count) * size, ROW_ALIGN), size)
        lane = lane_index(size)
        low_lanes = lane < HEAD_DIM
        first_half = lane % HEAD_DIM < HEAD_DIM // 2
        values, turns = [], []
        for head in range(own_heads):
            both = jnp.where(
                low_lanes,
                grad_query[head, at, :] * SCORE_SCALE,
                pltpu.roll(grad_key[head, at, :], HEAD_DIM, 1),
            )
            shifted = both * sine[...]
            turned = jnp.where(
                first_half,
                pltpu.roll(shifted, LANES - HEAD_DIM // 2, 1),
                -pltpu.roll(shifted, HEAD_DIM // 2, 1),
            )
            turns.append(both * cosine[...] + turned)
            values.append(jnp.where(low_lanes, grad_value[head, at, :], 0.0))
        swapped = pltpu.roll(turns[1], HEAD_DIM, 1)
        grads[:, :LANES] = jnp.where(low_lanes, turns[0], swapped).astype(BF16)
        grads[:, LANES : 2 * LANES] = jnp.where(low_lanes, turns[2], turns[0]).astype(BF16)
        grads[:, 2 * LANES : 3 * LANES] = jnp.where(low_lanes, swapped, turns[2]).astype(BF16)
        base = own_heads * LANES
        grads[:, base : base + LANES] = (values[0] + pltpu.roll(values[1], HEAD_DIM, 1)).astype(
            BF16
        )
        grads[:, base + LANES : base + 2 * LANES] = values[2].astype(BF16)


def refresh_kernel(
    full, own, select, stat_left, stat_right, root_left, right_root, weight, *refs, kept
):
    new_left, new_right, new_weight, columns, total = refs[kept:]
    step = pl.program_id(0)
    chosen = select.shape[0]
    count = new_right.shape[-2]
    outer = dot_rows(jnp.concatenate([select[...], own[...]]), full[...])
    columns[...] = outer[:chosen]
    new_left[0] = 0.5 * stat_left[0] + 0.5 * outer[chosen:]
    left = jnp.concatenate([outer[:chosen].astype(BF16), root_left[0].astype(BF16)])
    product = dot_plain(left, full[...])

    @pl.when(step == 0)
    def begin():
        total[...] = product

    @pl.when(step > 0)
    def add():
        total[...] += product

    @pl.when(step == pl.num_programs(0) - 1)
    def finish():
        new_right[0] = 0.5 * stat_right[0] + 0.5 * total[:count, :]
        update = dot_plain(total[chosen:, :].astype(BF16), right_root[...])
        new_weight[0] = weight[0] - SHAMPOO_RATE * update


def refresh(at, full, own, select, stat_left, stat_right, root_left, right_root, weight, previous):
    in_dim, out_dim = full.shape
    chunk = REFRESH_ROWS
    rows, count, chosen = own.shape[0], stat_right.shape[1], select.shape[0]

    def by_chunk(rows):
        return pl.BlockSpec((1, rows, chunk), lambda i: (at, 0, i))

    def whole(*shape):
        return pl.BlockSpec(shape, lambda i: (0,) * len(shape))

    def stacked(array):
        return pl.BlockSpec((1,) + array.shape[1:], lambda i: (at, 0, 0))

    kept = [pl.BlockSpec(memory_space=pl.ANY)] * len(previous)
    return pl.pallas_call(
        functools.partial(refresh_kernel, kept=len(previous)),
        grid=(in_dim // chunk,),
        in_specs=[
            pl.BlockSpec((chunk, out_dim), lambda i: (i, 0)),
            whole(*own.shape),
            whole(*select.shape),
            by_chunk(rows),
            stacked(stat_right),
            by_chunk(rows),
            whole(*right_root.shape),
            stacked(weight),
        ]
        + kept,
        out_specs=[
            by_chunk(rows),
            stacked(stat_right),
            stacked(weight),
            pl.BlockSpec((chosen, chunk), lambda i: (0, i)),
        ],
        out_shape=[
            jax.ShapeDtypeStruct(stat_left.shape, F32),
            jax.ShapeDtypeStruct(stat_right.shape, F32),
            jax.ShapeDtypeStruct(weight.shape, F32),
            jax.ShapeDtypeStruct((chosen, in_dim), F32),
        ],
        scratch_shapes=[pltpu.VMEM((chosen + rows, out_dim), F32)],
        input_output_aliases={8 + i: i for i in range(len(previous))},
        compiler_params=pltpu.CompilerParams(vmem_limit_bytes=VMEM_BYTES),
        cost_estimate=pl.CostEstimate(
            flops=4 * (chosen + rows) * in_dim * out_dim,
            bytes_accessed=2 * in_dim * out_dim + 12 * rows * in_dim + 2 * out_dim * out_dim,
            transcendentals=0,
        ),
        name="refresh",
    )(
        full,
        own,
        select,
        stat_left,
        stat_right,
        root_left,
        right_root,
        weight,
        *previous,
    )


def exchange(values, axis, offset):
    size = lax.axis_size(axis)
    return lax.ppermute(values, axis, [(i, i ^ offset) for i in range(size)])


def arrange_kernel(own_at, *refs, count, moves):
    blocks, outs, sems = refs[:count], refs[count:-1], refs[-1]
    copies = []
    for index, (number, offset, source, which, target) in enumerate(moves):
        place = own_at[0] ^ offset
        start = blocks[number].at[source] if source else blocks[number]
        end = outs[which].at[tuple(place if at == "place" else at for at in target)]
        copies.append(pltpu.make_async_copy(start, end, sems.at[index]))
    for copy in copies:
        copy.start()
    for copy in copies:
        copy.wait()


def arrange(blocks, own_at, shapes, moves):
    count = len(blocks)
    return pl.pallas_call(
        functools.partial(arrange_kernel, count=count, moves=moves),
        in_specs=[pl.BlockSpec(memory_space=pltpu.SMEM)]
        + [pl.BlockSpec(memory_space=pl.ANY)] * count,
        out_specs=[pl.BlockSpec(memory_space=pltpu.VMEM)] * len(shapes),
        scratch_shapes=[pltpu.SemaphoreType.DMA((len(moves),))],
        out_shape=[jax.ShapeDtypeStruct(shape, blocks[0].dtype) for shape in shapes],
        compiler_params=pltpu.CompilerParams(vmem_limit_bytes=VMEM_BYTES),
        cost_estimate=pl.CostEstimate(
            flops=0, bytes_accessed=2 * count * blocks[0].size * 2, transcendentals=0
        ),
        name="arrange",
    )(own_at[None], *blocks)


def terms_kernel(
    core, grad_proj, ffn_in, grad_out, attended, cotangent, middle, send, keep
):
    step = pl.program_id(0)
    groups, rows, _ = send.shape
    width = ffn_in.shape[1]
    chunk = 2 * groups * rows
    pieces = [(grad_proj, part * width, ffn_in) for part in range(grad_proj.shape[1] // width)]
    pieces += [(grad_out, 0, attended), (cotangent, 0, middle)]
    first = 0
    for left, offset, right in pieces:
        columns = pl.ds(pl.multiple_of(offset + step * chunk, KEY_ALIGN), chunk)
        term = dot_first(left[:, columns], right[...]).astype(BF16)
        last = first + right.shape[1]
        for own in range(2):

            @pl.when(core[0] == own)
            def store():
                for group in range(groups):
                    for side, out in ((own, keep), (1 - own, send)):
                        at = (2 * group + side) * rows
                        out[group, :, first:last] = term[at : at + rows]

        first = last


def gather_plane(values, by_steps=False):
    far = exchange(values, "seq", 2)
    last = exchange(far, "seq", 1) if by_steps else exchange(values, "seq", 3)
    blocks = [values, exchange(values, "seq", 1), far, last]
    shape = (len(blocks),) + values.shape
    moves = [(k, k, (), 0, ("place",)) for k in range(len(blocks))]
    return arrange(blocks, lax.axis_index("seq"), [shape], moves)[0]


def gather_partners(plane):
    half = plane.shape[0] // 2
    left, right = plane[:half], plane[half:]
    left_two, right_four = exchange(left, "dp", 2), exchange(right, "dp", 4)
    left_four, right_two = exchange(left, "dp", 4), exchange(right, "dp", 2)
    left_six, right_six = exchange(left_two, "dp", 4), exchange(right_four, "dp", 2)
    return [left, right, left_two, right_two, left_four, right_four, left_six, right_six]


def gather_cores(even):
    blocks = []
    for k in range(0, len(even), 2):
        blocks += [*even[k : k + 2], *(exchange(block, "dp", 1) for block in even[k : k + 2])]
    return blocks


def half_moves(blocks, cuts):
    half = blocks[0].shape[0]
    moves = []
    for number in range(len(blocks)):
        rows = slice(number % 2 * half, (number % 2 + 1) * half)
        for source, which, target in cuts:
            end = tuple(rows if at == "half" else at for at in target)
            moves.append((number, number // 2, source, which, end))
    return moves


def column_moves(blocks, widths):
    shapes, cuts, first = [], [], 0
    half, rows, _ = blocks[0].shape
    for which, width in enumerate(widths):
        shapes.append((len(blocks) // 2, 2 * half, rows, width))
        source = (slice(None), slice(None), slice(first, first + width))
        cuts.append((source, which, ("place", "half")))
        first += width
    return shapes, half_moves(blocks, cuts)


def fence(*values):
    return lax.optimization_barrier(values)


def add_blocks(blocks):
    total = blocks[0].astype(F32)
    for block in blocks[1:]:
        total = total + block.astype(F32)
    return total


def pair_sums(send, keep, axis=0):
    came = exchange(send, "dp", 1)
    own_at = lax.axis_index("dp") >> 1
    return [
        add_blocks(
            [
                lax.dynamic_index_in_dim(side, own_at ^ k, axis, keepdims=False)
                for side in (keep, came)
            ]
        )
        for k in range(keep.shape[axis])
    ]


def add_partners(blocks, axis, unit):
    return add_blocks(
        blocks[:1] + [exchange(block, axis, k * unit) for k, block in enumerate(blocks) if k]
    )


def lows(blocks):
    return [block.astype(BF16) for block in blocks]


def by_distance(values, axis):
    own_at = lax.axis_index(axis)
    return [
        lax.dynamic_index_in_dim(values, own_at ^ k, 0, keepdims=False)
        for k in range(values.shape[0])
    ]


def head_body(
    tokens,
    cotangent,
    doc_lengths,
    pad_counts,
    w_in,
    w_ao,
    w_fo,
    norm_gains,
    gain_moment,
    gain_second,
    stat_l_in,
    stat_r_in,
    stat_l_ao,
    stat_r_ao,
    stat_l_fo,
    stat_r_fo,
    root_l_in,
    root_r_in,
    root_l_ao,
    root_r_ao,
    root_l_fo,
    root_r_fo,
):
    token_count, width = tokens.shape
    hidden = w_fo.shape[1]
    seq_count, dp_count = lax.axis_size("seq"), lax.axis_size("dp")
    all_count = seq_count * dp_count
    row_length = token_count * seq_count
    seq_at = lax.axis_index("seq")
    dev_at = lax.axis_index(("dp", "seq"))
    head_count = width // HEAD_DIM
    own_heads = head_count // seq_count
    own_width = own_heads * HEAD_DIM
    in_rows = w_in.shape[1]
    ao_rows = w_ao.shape[0]
    gain_cols = norm_gains.shape[1]

    gain_lanes = jnp.zeros((in_rows, LANES), BF16).at[:2, :gain_cols].set(norm_gains.astype(BF16))
    up_parts = in_rows // ao_rows
    row_tokens = lax.all_gather(tokens, "seq", axis=0, tiled=True)
    qkv_blocks = gather_cores(
        gather_partners(gather_plane(jnp.concatenate([w_in[0].astype(BF16), gain_lanes], axis=1)))
    )
    full_qkv, gain_blocks = arrange(
        qkv_blocks, lax.axis_index("dp"), *column_moves(qkv_blocks, [width, LANES])
    )
    full_qkv = full_qkv.reshape(all_count * in_rows, width)
    gain_rows = (
        jnp.transpose(gain_blocks[:, :, :2, :gain_cols], (2, 0, 1, 3)).reshape(2, width).astype(F32)
    )
    full_up = lax.all_gather(w_in[1].astype(BF16), ("dp", "seq"), axis=0, tiled=True)
    out_weights = jnp.concatenate([w_ao.astype(BF16), w_fo.astype(BF16)], axis=1)
    row_tokens, out_weights = fence(row_tokens, out_weights)
    out_plane = gather_plane(out_weights)
    root_rows = stat_r_in.shape[1]
    fo_columns = root_r_fo.shape[0] * hidden // root_rows
    roots = jnp.concatenate(
        [
            root_r_in[0].astype(BF16),
            root_r_in[1].astype(BF16),
            root_r_ao.astype(BF16),
            root_r_fo.astype(BF16).reshape(root_rows, fo_columns),
        ],
        axis=1,
    )
    roots = lax.all_gather(roots, ("dp", "seq"), axis=0, tiled=True)

    lengths = doc_lengths[0]
    segment, within, is_valid = doc_tables(lengths, pad_counts[0], row_length)
    pad_from = row_length - pad_counts[0]
    doc_ids = jnp.arange(lengths.shape[0], dtype=jnp.int32)
    places = jnp.arange(row_length, dtype=jnp.int32)
    doc_begin = places - within
    doc_end = doc_begin + jnp.sum(
        jnp.where(segment[:, None] == doc_ids[None, :], lengths[None, :], 0), axis=1
    )
    freq_index = jnp.arange(0, HEAD_DIM, 2, dtype=F32)
    inverse = 1.0 / jnp.power(ROPE_THETA, freq_index / HEAD_DIM)
    angles = within.astype(F32)[:, None] * inverse[None, :]
    copies = LANES // (HEAD_DIM // 2)
    cos_table = jnp.concatenate([jnp.cos(angles)] * copies, axis=1)
    sin_table = jnp.concatenate([jnp.sin(angles)] * copies, axis=1)
    lane = jnp.arange(LANES, dtype=jnp.int32)
    in_doc = lane[None, :] - HEAD_DIM == segment[:, None]
    mask_lanes = (lane >= HEAD_DIM) & (lane < HEAD_DIM + 8)
    one_lanes = (lane >= HEAD_DIM + 8) & (lane < HEAD_DIM + 11)
    query_mask = in_doc.astype(BF16)
    key_mask = jnp.where(
        mask_lanes[None, :] & ~(in_doc & is_valid[:, None]),
        MASK_BIT,
        jnp.where(one_lanes[None, :], 1.0, 0.0),
    ).astype(BF16)
    tile_starts = doc_begin[::QUERY_TILE] // KEY_ALIGN
    tile_ends = jnp.minimum(doc_end[QUERY_TILE - 1 :: QUERY_TILE], pad_from)
    tile_steps = jnp.maximum(-((tile_starts * KEY_ALIGN - tile_ends) // KEY_STEP), 0)
    tile_count = row_length // QUERY_TILE
    pad_at = pad_from[None]

    qkv_heads = lax.dynamic_slice_in_dim(
        full_qkv.reshape(3, head_count, HEAD_DIM, width), seq_at * own_heads, own_heads, 1
    )
    own_weight = jnp.concatenate(
        [
            jnp.transpose(qkv_heads[:2], (1, 0, 2, 3)).reshape(2 * own_width, width),
            qkv_heads[2].reshape(own_width, width),
            jnp.zeros((HEAD_DIM, width), BF16),
        ]
    )
    back_weight = jnp.concatenate(
        [qkv_heads.reshape(3 * own_width, width), jnp.zeros((HEAD_DIM, width), BF16)]
    )
    own_columns = own_weight.shape[0]
    prep_count = row_length // PREP_TILE
    key_length = row_length + PREP_TILE

    def row_block(columns):
        return pl.BlockSpec(
            (PREP_TILE, columns), lambda i, *_: (jnp.minimum(i, prep_count - 1), 0)
        )

    def fixed_block(*shape):
        return pl.BlockSpec(shape, lambda i, *_: (0,) * len(shape))

    head_block = pl.BlockSpec((own_heads, PREP_TILE, LANES), lambda i, *_: (0, i, 0))
    attn_in, query_ext, key_ext, value_ext = pl.pallas_call(
        project_kernel,
        grid=(prep_count + 1,),
        in_specs=[
            row_block(width),
            fixed_block(own_columns, width),
            fixed_block(1, width),
            row_block(LANES),
            row_block(LANES),
            row_block(LANES),
            row_block(LANES),
        ],
        out_specs=[
            row_block(width),
            pl.BlockSpec(
                (own_heads, PREP_TILE, LANES), lambda i: (0, jnp.minimum(i, prep_count - 1), 0)
            ),
            head_block,
            head_block,
        ],
        out_shape=[
            jax.ShapeDtypeStruct((row_length, width), BF16),
            jax.ShapeDtypeStruct((own_heads, row_length, LANES), BF16),
            jax.ShapeDtypeStruct((own_heads, key_length, LANES), BF16),
            jax.ShapeDtypeStruct((own_heads, key_length, LANES), BF16),
        ],
        compiler_params=pltpu.CompilerParams(vmem_limit_bytes=VMEM_BYTES),
        cost_estimate=pl.CostEstimate(
            flops=2 * row_length * own_columns * width,
            bytes_accessed=14_000_000,
            transcendentals=0,
        ),
        name="project",
    )(
        row_tokens,
        own_weight,
        gain_rows[:1],
        cos_table,
        sin_table,
        query_mask,
        key_mask,
    )

    query_ext, key_ext, value_ext, out_plane = fence(query_ext, key_ext, value_ext, out_plane)
    out_partners = gather_partners(out_plane)

    def tile_block(columns):
        return pl.BlockSpec(
            (QUERY_TILE, columns), lambda i, *_: (jnp.minimum(i, tile_count - 1), 0)
        )

    head_tile = pl.BlockSpec(
        (own_heads, QUERY_TILE, LANES), lambda i, *_: (0, jnp.minimum(i, tile_count - 1), 0)
    )
    whole_keys = fixed_block(own_heads, key_length, LANES)
    pair_out, extra_out, query_low = pl.pallas_call(
        attend_kernel,
        grid_spec=pltpu.PrefetchScalarGridSpec(
            num_scalar_prefetch=3,
            grid=(tile_count,),
            in_specs=[head_tile, whole_keys, whole_keys],
            out_specs=[tile_block(LANES), tile_block(LANES), head_tile],
        ),
        out_shape=[
            jax.ShapeDtypeStruct((row_length, LANES), BF16),
            jax.ShapeDtypeStruct((row_length, LANES), BF16),
            jax.ShapeDtypeStruct((own_heads, row_length, LANES), BF16),
        ],
        compiler_params=pltpu.CompilerParams(vmem_limit_bytes=VMEM_BYTES),
        cost_estimate=pl.CostEstimate(
            flops=2 * own_heads * row_length * row_length * LANES,
            bytes_accessed=12_000_000,
            transcendentals=0,
        ),
        name="attend",
    )(tile_starts, tile_steps, pad_at, query_ext, key_ext, value_ext)

    fenced = fence(pair_out, extra_out, query_low, *out_partners)
    pair_out, extra_out, query_low = fenced[:3]
    out_blocks = gather_cores(fenced[3:])
    full_ao, full_fo = arrange(
        out_blocks, lax.axis_index("dp"), *column_moves(out_blocks, [width, hidden])
    )
    full_ao = full_ao.reshape(width, width)
    full_fo = full_fo.reshape(width, hidden)

    half_tokens = token_count // 2

    def fold(extra):
        blocks = extra[:, :HEAD_DIM].reshape(seq_count, 2, half_tokens, HEAD_DIM)
        return jnp.concatenate([blocks[:, 0], blocks[:, 1]], axis=-1)

    def unfold(folded):
        return jnp.concatenate([folded[:, :, :HEAD_DIM], folded[:, :, HEAD_DIM:]], axis=1)

    packed = jnp.concatenate(
        [pair_out.reshape(seq_count, token_count, LANES), fold(extra_out)], axis=1
    )
    packed = lax.all_to_all(packed, "seq", 0, 0, tiled=True)
    attn_low = jnp.concatenate([packed[:, :token_count], unfold(packed[:, token_count:])], axis=-1)
    attn_low = jnp.transpose(attn_low, (1, 0, 2)).reshape(token_count, width)

    inputs = tokens.astype(F32)
    residual = inputs + apply_rows(attn_low, full_ao)
    normed_two, spread_two = norm_forward(residual)
    ffn_in = (normed_two * gain_rows[1]).astype(BF16)
    projected = apply_rows(ffn_in, full_up)
    inner_part = projected[:, :hidden]
    gate_part = projected[:, hidden:]
    activated = gelu_value(inner_part)
    mid_low = (activated * gate_part).astype(BF16)
    layer_out = (residual + apply_rows(mid_low, full_fo)).astype(BF16)
    grad_mid = jnp.dot(cotangent, full_fo, preferred_element_type=F32)
    grad_proj = jnp.concatenate(
        [grad_mid * gate_part * gelu_slope(inner_part), grad_mid * activated], axis=1
    ).astype(BF16)
    grad_ffn_in = jnp.dot(grad_proj, full_up, preferred_element_type=F32)
    grad_norm_two, _ = norm_backward(grad_ffn_in, normed_two, spread_two, gain_rows[1])
    grad_resid = cotangent.astype(F32) + grad_norm_two
    grad_out_attn = grad_resid.astype(BF16)
    grad_attn = jnp.dot(grad_out_attn, full_ao, preferred_element_type=F32).astype(BF16)

    grad_blocks = jnp.transpose(
        grad_attn.reshape(token_count, seq_count, own_width), (1, 0, 2)
    )
    folded = grad_blocks[:, :, LANES:].reshape(seq_count, 2, half_tokens, HEAD_DIM)
    packed_back = jnp.concatenate(
        [grad_blocks[:, :, :LANES], jnp.concatenate([folded[:, 0], folded[:, 1]], axis=-1)], axis=1
    )
    back_blocks = by_distance(packed_back, "seq")
    back_blocks = [back_blocks[0]] + [
        exchange(block, "seq", k) for k, block in enumerate(back_blocks) if k
    ]

    pack_width = up_parts * width + width + hidden
    pair_count = dp_count // 2
    block_rows = seq_count * ao_rows
    core = lax.axis_index("dp") & 1
    operands = (grad_proj, ffn_in, grad_out_attn, attn_low, cotangent, mid_low)
    half_block = pl.BlockSpec((pair_count // 2, block_rows, pack_width), lambda i: (i, 0, 0))
    send_terms, keep_terms = pl.pallas_call(
        terms_kernel,
        grid=(2,),
        in_specs=[pl.BlockSpec(memory_space=pltpu.SMEM)]
        + [pl.BlockSpec(operand.shape, lambda i: (0, 0)) for operand in operands],
        out_specs=[half_block, half_block],
        out_shape=[jax.ShapeDtypeStruct((pair_count, block_rows, pack_width), BF16)] * 2,
        compiler_params=pltpu.CompilerParams(vmem_limit_bytes=VMEM_BYTES),
        cost_estimate=pl.CostEstimate(
            flops=2 * token_count * width * pack_width,
            bytes_accessed=13_000_000,
            transcendentals=0,
        ),
        name="terms",
    )(core[None], *operands)
    fenced = fence(send_terms, *back_blocks)
    send_terms, back_blocks = fenced[0], fenced[1:]
    pair_blocks = lows(pair_sums(send_terms, keep_terms))
    folded_tokens = token_count + half_tokens
    grad_pair, grad_extra = arrange(
        back_blocks,
        seq_at,
        [(seq_count, token_count, LANES), (seq_count, half_tokens, LANES)],
        [
            (k, k, (rows,), which, ("place",))
            for k in range(seq_count)
            for which, rows in enumerate(
                (slice(0, token_count), slice(token_count, folded_tokens))
            )
        ],
    )
    grad_pair = grad_pair.reshape(row_length, LANES)
    grad_extra = unfold(grad_extra).reshape(row_length, HEAD_DIM)
    grad_extra = jnp.pad(grad_extra, ((0, 0), (0, LANES - HEAD_DIM)))
    fenced = fence(grad_pair, grad_extra, *pair_blocks)
    grad_pair, grad_extra, pair_blocks = fenced[0], fenced[1], fenced[2:]
    plane_blocks = [pair_blocks[0]] + [
        exchange(block, "dp", 2 * k) for k, block in enumerate(pair_blocks) if k
    ]

    finish_count = prep_count

    def finish_block(columns):
        return pl.BlockSpec(
            (PREP_TILE, columns), lambda i, *_: (jnp.maximum(i - tile_count, 0), 0)
        )

    grad_qkv = pl.pallas_call(
        attend_back_kernel,
        grid_spec=pltpu.PrefetchScalarGridSpec(
            num_scalar_prefetch=3,
            grid=(tile_count + finish_count,),
            in_specs=[
                head_tile,
                tile_block(LANES),
                tile_block(LANES),
                tile_block(LANES),
                tile_block(LANES),
                whole_keys,
                whole_keys,
                finish_block(LANES),
                finish_block(LANES),
            ],
            out_specs=finish_block(own_columns),
            scratch_shapes=[
                pltpu.VMEM((own_heads, row_length, LANES), F32),
                pltpu.VMEM((own_heads, key_length, LANES), F32),
                pltpu.VMEM((own_heads, key_length, LANES), F32),
            ],
        ),
        out_shape=jax.ShapeDtypeStruct((row_length, own_columns), BF16),
        compiler_params=pltpu.CompilerParams(vmem_limit_bytes=VMEM_BYTES),
        cost_estimate=pl.CostEstimate(
            flops=5 * own_heads * row_length * row_length * LANES,
            bytes_accessed=15_000_000,
            transcendentals=0,
        ),
        name="attend_back",
    )(
        tile_starts,
        tile_steps,
        pad_at,
        query_low,
        pair_out,
        extra_out,
        grad_pair,
        grad_extra,
        key_ext,
        value_ext,
        cos_table,
        sin_table,
    )
    right_qkv = roots[:, :width]
    right_up = roots[:, width : 2 * width]
    right_ao = roots[:, 2 * width : 3 * width]
    right_fo = roots[:, 3 * width :].reshape(hidden, hidden)
    fenced = fence(grad_qkv, *plane_blocks)
    grad_qkv = fenced[0]
    plane_sum = add_blocks(fenced[1:]).astype(BF16).reshape(seq_count, ao_rows, pack_width)
    summed = add_partners(by_distance(plane_sum, "seq"), "seq", 1)
    low_sum = summed.astype(BF16)
    term_plane = gather_plane(low_sum, by_steps=True)
    low_ao = low_sum[:, up_parts * width : (up_parts + 1) * width]
    low_fo = low_sum[:, (up_parts + 1) * width :]
    summed_ao = summed[:, up_parts * width : (up_parts + 1) * width]
    summed_fo = summed[:, (up_parts + 1) * width :]

    qkv_term = outer_sum(grad_qkv, attn_in)[: 3 * own_width].astype(BF16)
    qkv_rows = own_width // dp_count
    qkv_term = qkv_term.reshape(3, pair_count, 2, qkv_rows, width)
    qkv_halves = [
        lax.dynamic_index_in_dim(qkv_term, side, 2, keepdims=False) for side in (1 - core, core)
    ]
    qkv_sum = add_partners(lows(pair_sums(*qkv_halves, axis=1)), "dp", 2).astype(BF16)
    qkv_plane = gather_plane(qkv_sum, by_steps=True)
    grad_qkv = fence(grad_qkv, qkv_plane, term_plane)[0]
    fenced = fence(right_fo, *gather_partners(qkv_plane))
    right_fo, qkv_blocks = fenced[0], gather_cores(fenced[1:])
    [whole_qkv] = arrange(
        qkv_blocks,
        lax.axis_index("dp"),
        [(3, seq_count, dp_count, qkv_rows, width)],
        half_moves(qkv_blocks, [((slice(None), part), 0, (part, "half", "place")) for part in range(3)]),
    )
    whole_qkv = whole_qkv.reshape(3 * width, width)
    low_qkv = lax.dynamic_slice_in_dim(whole_qkv, dev_at * in_rows, in_rows, 0)

    input_term = jnp.dot(grad_qkv, back_weight, preferred_element_type=F32).astype(BF16)
    grad_attn_in = lax.psum_scatter(input_term, "seq", scatter_dimension=0, tiled=True).astype(F32)
    normed_one, spread_one = norm_forward(inputs)
    grad_norm_one, _ = norm_backward(grad_attn_in, normed_one, spread_one, gain_rows[0])
    grad_input = grad_resid + grad_norm_one

    def select(count, size):
        places = jnp.arange(-(-count // 16) * 16, dtype=jnp.int32)[:, None]
        wanted = jnp.where(places < count, dev_at * count + places, -1)
        return (wanted == jnp.arange(size, dtype=jnp.int32)[None, :]).astype(BF16)

    select_in = select(stat_r_in.shape[1], width)
    select_fo = select(stat_r_fo.shape[0], hidden)
    *stacked, qkv_columns = refresh(
        0, whole_qkv, low_qkv, select_in, stat_l_in, stat_r_in, root_l_in, right_qkv, w_in, []
    )
    term_partners = gather_partners(term_plane)
    fenced = fence(stacked, *term_partners)
    stacked, term_blocks = fenced[0], gather_cores(fenced[1:])
    whole_shape = (dp_count, seq_count, ao_rows)
    cut = (slice(None), slice(None))
    whole_up, whole_ao, whole_fo = arrange(
        term_blocks,
        lax.axis_index("dp"),
        [(up_parts,) + whole_shape + (width,), whole_shape + (width,), whole_shape + (hidden,)],
        half_moves(
            term_blocks,
            [
                (cut + (slice(part * width, (part + 1) * width),), 0, (part, "place", "half"))
                for part in range(up_parts)
            ]
            + [
                (cut + (slice(up_parts * width, (up_parts + 1) * width),), 1, ("place", "half")),
                (cut + (slice((up_parts + 1) * width, pack_width),), 2, ("place", "half")),
            ],
        ),
    )
    whole_up = whole_up.reshape(up_parts * width, width)
    whole_ao = whole_ao.reshape(width, width)
    whole_fo = whole_fo.reshape(width, hidden)
    low_up = lax.dynamic_slice_in_dim(whole_up, dev_at * in_rows, in_rows, 0)
    left_ao, right_stat_ao, new_ao, _ = refresh(
        0,
        whole_ao,
        low_ao,
        select_in,
        stat_l_ao[None],
        stat_r_ao[None],
        root_l_ao[None],
        right_ao,
        w_ao[None],
        [],
    )
    left_fo, right_stat_fo, new_fo, _ = refresh(
        0,
        whole_fo,
        low_fo,
        select_fo,
        stat_l_fo[None],
        stat_r_fo[None],
        root_l_fo[None],
        right_fo,
        w_fo[None],
        [],
    )
    *stacked, up_columns = refresh(
        1, whole_up, low_up, select_in, stat_l_in, stat_r_in, root_l_in, right_up, w_in, stacked
    )
    new_left_in, new_right_in, new_in = stacked

    def gain_gradient(weight, columns, gain):
        own_weight_columns = lax.dynamic_slice_in_dim(weight, dev_at * gain_cols, gain_cols, 1)
        products = jnp.transpose(own_weight_columns).astype(F32) * columns[:gain_cols]
        own_gain = lax.dynamic_slice_in_dim(gain, dev_at * gain_cols, gain_cols)
        return jnp.sum(products, axis=1) / own_gain

    summed_gains = jnp.stack(
        [
            gain_gradient(full_qkv, qkv_columns, gain_rows[0]),
            gain_gradient(full_up, up_columns, gain_rows[1]),
        ]
    )
    new_moment = 0.9 * gain_moment + 0.1 * summed_gains
    new_second = 0.999 * gain_second + 0.001 * summed_gains * summed_gains
    new_gains = norm_gains - ADAM_RATE * new_moment / (jnp.sqrt(new_second) + 1e-08)
    return (
        layer_out,
        grad_input,
        jnp.stack([low_qkv, low_up]).astype(F32),
        summed_ao,
        summed_fo,
        summed_gains,
        new_moment,
        new_second,
        new_gains,
        new_left_in,
        new_right_in,
        left_ao[0],
        right_stat_ao[0],
        left_fo[0],
        right_stat_fo[0],
        new_in,
        new_ao[0],
        new_fo[0],
    )


def body(tokens, *others):
    seq_count, dp_count = lax.axis_size("seq"), lax.axis_size("dp")
    token_count, width = tokens.shape
    row_length = token_count * seq_count
    by_heads = (
        width // HEAD_DIM == 3 * seq_count
        and dp_count & (dp_count - 1) == 0
        and seq_count & (seq_count - 1) == 0
        and row_length % QUERY_TILE == 0
        and token_count == PREP_TILE
        and dp_count == 8
        and seq_count == 4
        and others[3].shape[1] == 3 * others[4].shape[0]
        and others[1].shape[1] == 8
    )
    return head_body(tokens, *others) if by_heads else sequence_body(tokens, *others)


def solution(mesh):
    in_specs = (
        P(("dp", "seq"), None),
        P(("dp", "seq"), None),
        P("dp", None),
        P("dp"),
        P(None, ("dp", "seq"), None),
        P(("dp", "seq"), None),
        P(("dp", "seq"), None),
        P(None, ("dp", "seq")),
        P(None, ("dp", "seq")),
        P(None, ("dp", "seq")),
        P(None, ("dp", "seq"), None),
        P(None, ("dp", "seq"), None),
        P(("dp", "seq"), None),
        P(("dp", "seq"), None),
        P(("dp", "seq"), None),
        P(("dp", "seq"), None),
        P(None, ("dp", "seq"), None),
        P(None, ("dp", "seq"), None),
        P(("dp", "seq"), None),
        P(("dp", "seq"), None),
        P(("dp", "seq"), None),
        P(("dp", "seq"), None),
    )
    out_specs = (
        P(("dp", "seq"), None),
        P(("dp", "seq"), None),
        P(None, ("dp", "seq"), None),
        P(("dp", "seq"), None),
        P(("dp", "seq"), None),
        P(None, ("dp", "seq")),
        P(None, ("dp", "seq")),
        P(None, ("dp", "seq")),
        P(None, ("dp", "seq")),
        P(None, ("dp", "seq"), None),
        P(None, ("dp", "seq"), None),
        P(("dp", "seq"), None),
        P(("dp", "seq"), None),
        P(("dp", "seq"), None),
        P(("dp", "seq"), None),
        P(None, ("dp", "seq"), None),
        P(("dp", "seq"), None),
        P(("dp", "seq"), None),
    )
    return jax.shard_map(body, mesh=mesh, in_specs=in_specs, out_specs=out_specs, check_vma=False)
```

```python
import functools
import math

import jax
import jax.numpy as jnp
from jax import lax
from jax.experimental import pallas as pl
from jax.experimental.pallas import tpu as pltpu
from jax.sharding import PartitionSpec as P

HEAD_DIM = 64


NORM_EPS = 1e-05
ROPE_THETA = 160000.0
SCORE_SCALE = 0.125
MASK_FILL = -1e30
ADAM_RATE = 0.2
SHAMPOO_RATE = 1.0
HIGHEST = lax.Precision.HIGHEST


def norm_forward(values):
    center = values - jnp.mean(values, axis=-1, keepdims=True)
    inv_spread = lax.rsqrt(jnp.mean(center * center, axis=-1, keepdims=True) + NORM_EPS)
    return (center * inv_spread, inv_spread)


def norm_backward(grad_out, normed, inv_spread, gain_row):
    scaled = grad_out * gain_row
    inner_term = (
        scaled
        - jnp.mean(scaled, axis=-1, keepdims=True)
        - normed * jnp.mean(scaled * normed, axis=-1, keepdims=True)
    )
    return (inner_term * inv_spread, jnp.sum(grad_out * normed, axis=0))


def gelu_value(inputs):
    return 0.5 * inputs * (1.0 + lax.erf(inputs * (1.0 / math.sqrt(2.0))))


def gelu_slope(inputs):
    cumulative = 0.5 * (1.0 + lax.erf(inputs * (1.0 / math.sqrt(2.0))))
    return cumulative + inputs * jnp.exp(-0.5 * inputs * inputs) * (1.0 / math.sqrt(2.0 * math.pi))


def rotate(values, cos_table, sin_table):
    half_dim = values.shape[-1] // 2
    turned = jnp.concatenate([-values[..., half_dim:], values[..., :half_dim]], axis=-1)
    return values * cos_table + turned * sin_table


def unrotate(gradient, cos_table, sin_table):
    half_dim = gradient.shape[-1] // 2
    shifted = gradient * sin_table
    back_turn = jnp.concatenate([shifted[..., half_dim:], -shifted[..., :half_dim]], axis=-1)
    return gradient * cos_table + back_turn


def rope_tables(within):
    freq_index = jnp.arange(0, HEAD_DIM, 2, dtype=jnp.float32)
    inverse = 1.0 / jnp.power(ROPE_THETA, freq_index / HEAD_DIM)
    angles = within.astype(jnp.float32)[:, None] * inverse[None, :]
    angles = jnp.concatenate([angles, angles], axis=-1)
    return (jnp.cos(angles), jnp.sin(angles))


def doc_tables(lengths_row, pad_count, row_length):
    doc_order = jnp.arange(lengths_row.shape[0], dtype=jnp.int32)
    doc_ends = jnp.sum(
        jnp.where(doc_order[:, None] >= doc_order[None, :], lengths_row[None, :], 0), axis=1
    )
    starts = doc_ends - lengths_row
    places = jnp.arange(row_length, dtype=jnp.int32)
    segment = jnp.sum((places[:, None] >= doc_ends[None, :]).astype(jnp.int32), axis=1)
    doc_ids = jnp.arange(lengths_row.shape[0], dtype=jnp.int32)
    doc_begin = jnp.sum(jnp.where(segment[:, None] == doc_ids[None, :], starts[None, :], 0), axis=1)
    is_valid = places < row_length - pad_count
    return (segment, places - doc_begin, is_valid)


def apply_rows(activations, weight):
    return lax.dot_general(
        activations, weight, (((1,), (1,)), ((), ())), preferred_element_type=jnp.float32
    )


def outer_sum(grad_rows, act_rows):
    return lax.dot_general(
        grad_rows, act_rows, (((0,), (0,)), ((), ())), preferred_element_type=jnp.float32
    )


def sequence_body(
    tokens,
    cotangent,
    doc_lengths,
    pad_counts,
    w_in,
    w_ao,
    w_fo,
    norm_gains,
    gain_moment,
    gain_second,
    stat_l_in,
    stat_r_in,
    stat_l_ao,
    stat_r_ao,
    stat_l_fo,
    stat_r_fo,
    root_l_in,
    root_r_in,
    root_l_ao,
    root_r_ao,
    root_l_fo,
    root_r_fo,
):
    token_count, model_width = tokens.shape
    head_count = model_width // HEAD_DIM
    pair_count = head_count // 2
    pair_width = 2 * HEAD_DIM
    hidden_width = w_fo.shape[1]
    seq_count = lax.axis_size("seq")
    row_length = token_count * seq_count
    first_place = lax.axis_index("seq") * token_count
    segment, within, is_valid = doc_tables(doc_lengths[0], pad_counts[0], row_length)
    own_places = first_place + jnp.arange(token_count, dtype=jnp.int32)
    all_places = jnp.arange(row_length, dtype=jnp.int32)
    own_segment = lax.dynamic_slice_in_dim(segment, first_place, token_count)
    own_within = lax.dynamic_slice_in_dim(within, first_place, token_count)
    allowed = (own_segment[:, None] == segment[None, :]) & (
        is_valid[None, :] | (own_places[:, None] == all_places[None, :])
    )
    cos_table, sin_table = rope_tables(own_within)
    cos_table = cos_table[:, None, :]
    sin_table = sin_table[:, None, :]
    low_weights = (
        w_in.astype(jnp.bfloat16),
        w_ao.astype(jnp.bfloat16),
        w_fo.astype(jnp.bfloat16),
        norm_gains.astype(jnp.bfloat16),
    )
    full_in, full_ao, full_fo, full_gains = (
        lax.all_gather(low_weights[0], ("dp", "seq"), axis=1, tiled=True),
        lax.all_gather(low_weights[1], ("dp", "seq"), axis=0, tiled=True),
        lax.all_gather(low_weights[2], ("dp", "seq"), axis=0, tiled=True),
        lax.all_gather(low_weights[3], ("dp", "seq"), axis=1, tiled=True),
    )
    gain_rows = full_gains.astype(jnp.float32)
    inputs = tokens.astype(jnp.float32)
    normed_one, spread_one = norm_forward(inputs)
    attn_in = (normed_one * gain_rows[0]).astype(jnp.bfloat16)
    qkv_raw = apply_rows(attn_in, full_in[0])
    query_low = (
        rotate(
            qkv_raw[:, :model_width].reshape(token_count, head_count, HEAD_DIM),
            cos_table,
            sin_table,
        )
        .reshape(token_count, model_width)
        .astype(jnp.bfloat16)
    )
    key_low = (
        rotate(
            qkv_raw[:, model_width : 2 * model_width].reshape(token_count, head_count, HEAD_DIM),
            cos_table,
            sin_table,
        )
        .reshape(token_count, model_width)
        .astype(jnp.bfloat16)
    )
    value_low = qkv_raw[:, 2 * model_width :].astype(jnp.bfloat16)
    keys_all, values_all = (
        lax.all_gather(key_low, "seq", axis=0, tiled=True),
        lax.all_gather(value_low, "seq", axis=0, tiled=True),
    )

    def pair_slice(matrix, pair_index):
        return lax.dynamic_slice_in_dim(matrix, pair_index * pair_width, pair_width, 1).reshape(
            matrix.shape[0], 2, HEAD_DIM
        )

    def pair_scores(query_pair, key_pair, allow_mask):
        raw_scores = (
            jnp.einsum("thd,khd->htk", query_pair, key_pair, preferred_element_type=jnp.float32)
            * SCORE_SCALE
        )
        return jnp.where(allow_mask[None], raw_scores, MASK_FILL)

    def forward_pair(loop_carry, pair_index):
        scores = pair_scores(
            pair_slice(query_low, pair_index), pair_slice(keys_all, pair_index), allowed
        )
        row_max = jnp.max(scores, axis=-1, keepdims=True)
        exponent = jnp.exp(scores - row_max)
        row_sum = jnp.sum(exponent, axis=-1, keepdims=True)
        weights_low = (exponent / row_sum).astype(jnp.bfloat16)
        attended = jnp.einsum(
            "htk,khd->thd",
            weights_low,
            pair_slice(values_all, pair_index),
            preferred_element_type=jnp.float32,
        )
        return (
            loop_carry,
            (attended.reshape(token_count, pair_width), (row_max + jnp.log(row_sum))[..., 0]),
        )

    unused, (attended_pairs, log_norms) = lax.scan(forward_pair, 0, jnp.arange(pair_count))
    attn_low = (
        jnp.transpose(attended_pairs, (1, 0, 2))
        .reshape(token_count, model_width)
        .astype(jnp.bfloat16)
    )
    residual = inputs + apply_rows(attn_low, full_ao)
    normed_two, spread_two = norm_forward(residual)
    ffn_in = (normed_two * gain_rows[1]).astype(jnp.bfloat16)
    projected = apply_rows(ffn_in, full_in[1])
    inner_part = projected[:, :hidden_width]
    gate_part = projected[:, hidden_width:]
    activated = gelu_value(inner_part)
    mid_low = (activated * gate_part).astype(jnp.bfloat16)
    layer_out = (residual + apply_rows(mid_low, full_fo)).astype(jnp.bfloat16)
    back_in, back_ao, back_fo, back_gains = (
        lax.all_gather(low_weights[0], ("dp", "seq"), axis=1, tiled=True),
        lax.all_gather(low_weights[1], ("dp", "seq"), axis=0, tiled=True),
        lax.all_gather(low_weights[2], ("dp", "seq"), axis=0, tiled=True),
        lax.all_gather(low_weights[3], ("dp", "seq"), axis=1, tiled=True),
    )
    back_rows = back_gains.astype(jnp.float32)
    grad_fo_w = outer_sum(cotangent, mid_low)
    grad_mid = jnp.dot(cotangent, back_fo, preferred_element_type=jnp.float32)
    grad_proj = jnp.concatenate(
        [grad_mid * gate_part * gelu_slope(inner_part), grad_mid * activated], axis=1
    ).astype(jnp.bfloat16)
    grad_ffn_w = outer_sum(grad_proj, ffn_in)
    grad_ffn_in = jnp.dot(grad_proj, back_in[1], preferred_element_type=jnp.float32)
    grad_norm_two, grad_gain_two = norm_backward(grad_ffn_in, normed_two, spread_two, back_rows[1])
    grad_resid = cotangent.astype(jnp.float32) + grad_norm_two
    grad_out_attn = grad_resid.astype(jnp.bfloat16)
    grad_ao_w = outer_sum(grad_out_attn, attn_low)
    grad_attn = jnp.dot(grad_out_attn, back_ao, preferred_element_type=jnp.float32).astype(
        jnp.bfloat16
    )

    def query_side_grads(pair_index):
        query_pair = pair_slice(query_low, pair_index)
        key_pair = pair_slice(keys_all, pair_index)
        value_pair = pair_slice(values_all, pair_index)
        grad_pair = pair_slice(grad_attn, pair_index)
        scores = pair_scores(query_pair, key_pair, allowed)
        softmax_out = jnp.exp(scores - log_norms[pair_index][..., None])
        grad_weights = jnp.einsum(
            "thd,khd->htk", grad_pair, value_pair, preferred_element_type=jnp.float32
        )
        delta_row = jnp.sum(softmax_out * grad_weights, axis=-1, keepdims=True)
        grad_scores = (softmax_out * (grad_weights - delta_row)).astype(jnp.bfloat16)
        grad_query = (
            jnp.einsum("htk,khd->thd", grad_scores, key_pair, preferred_element_type=jnp.float32)
            * SCORE_SCALE
        )
        return (query_pair, grad_pair, softmax_out, grad_scores, grad_query, delta_row)

    def backward_pair(loop_carry, pair_index):
        query_pair, grad_pair, softmax_out, grad_scores, grad_query, delta_row = query_side_grads(
            pair_index
        )
        grad_key = (
            jnp.einsum("htk,thd->khd", grad_scores, query_pair, preferred_element_type=jnp.float32)
            * SCORE_SCALE
        )
        grad_value = jnp.einsum(
            "htk,thd->khd",
            softmax_out.astype(jnp.bfloat16),
            grad_pair,
            preferred_element_type=jnp.float32,
        )
        return (
            loop_carry,
            (
                grad_query.reshape(token_count, pair_width),
                grad_key.reshape(row_length, pair_width),
                grad_value.reshape(row_length, pair_width),
            ),
        )

    unused, (grad_query_pairs, grad_key_parts, grad_value_parts) = lax.scan(
        backward_pair, 0, jnp.arange(pair_count)
    )
    grad_key_pairs, grad_value_pairs = (
        lax.psum_scatter(
            grad_key_parts.astype(jnp.bfloat16), "seq", scatter_dimension=1, tiled=True
        ).astype(jnp.float32),
        lax.psum_scatter(
            grad_value_parts.astype(jnp.bfloat16), "seq", scatter_dimension=1, tiled=True
        ).astype(jnp.float32),
    )

    def heads_of(pairs_array):
        return jnp.transpose(pairs_array, (1, 0, 2)).reshape(token_count, head_count, HEAD_DIM)

    grad_qkv = jnp.concatenate(
        [
            unrotate(heads_of(grad_query_pairs), cos_table, sin_table).reshape(
                token_count, model_width
            ),
            unrotate(heads_of(grad_key_pairs), cos_table, sin_table).reshape(
                token_count, model_width
            ),
            heads_of(grad_value_pairs).reshape(token_count, model_width),
        ],
        axis=1,
    ).astype(jnp.bfloat16)
    grad_qkv_w = outer_sum(grad_qkv, attn_in)
    grad_attn_in = jnp.dot(grad_qkv, back_in[0], preferred_element_type=jnp.float32)
    grad_norm_one, grad_gain_one = norm_backward(grad_attn_in, normed_one, spread_one, back_rows[0])
    grad_input = grad_resid + grad_norm_one
    w_terms = jnp.stack([grad_qkv_w, grad_ffn_w])
    gain_terms = jnp.stack([grad_gain_one, grad_gain_two])
    summed_in, summed_ao, summed_fo, summed_gains = (
        lax.psum_scatter(w_terms, ("dp", "seq"), scatter_dimension=1, tiled=True),
        lax.psum_scatter(grad_ao_w, ("dp", "seq"), scatter_dimension=0, tiled=True),
        lax.psum_scatter(grad_fo_w, ("dp", "seq"), scatter_dimension=0, tiled=True),
        lax.psum_scatter(gain_terms, ("dp", "seq"), scatter_dimension=1, tiled=True),
    )
    new_moment = 0.9 * gain_moment + 0.1 * summed_gains
    new_second = 0.999 * gain_second + 0.001 * summed_gains * summed_gains
    new_gains = norm_gains - ADAM_RATE * new_moment / (jnp.sqrt(new_second) + 1e-08)
    whole_in, whole_ao, whole_fo = (
        lax.all_gather(summed_in.astype(jnp.bfloat16), ("dp", "seq"), axis=1, tiled=True).astype(
            summed_in.dtype
        ),
        lax.all_gather(summed_ao.astype(jnp.bfloat16), ("dp", "seq"), axis=0, tiled=True).astype(
            summed_ao.dtype
        ),
        lax.all_gather(summed_fo.astype(jnp.bfloat16), ("dp", "seq"), axis=0, tiled=True).astype(
            summed_fo.dtype
        ),
    )
    dev_index = lax.axis_index(("dp", "seq"))

    def refresh(grad_shard, grad_full, stat_left, stat_right, root_right):
        col_count = stat_right.shape[1]
        new_left = 0.5 * stat_left + 0.5 * jnp.einsum(
            "arn,amn->arm", grad_shard, grad_full, precision=HIGHEST
        )
        full_cols = lax.dynamic_slice_in_dim(grad_full, dev_index * col_count, col_count, 2)
        new_right = 0.5 * stat_right + 0.5 * jnp.einsum(
            "amc,amn->acn", full_cols, grad_full, precision=HIGHEST
        )
        applied = jnp.einsum("amn,acn->amc", grad_full, root_right, precision=HIGHEST)
        return (new_left, new_right, applied)

    left_in, right_in, applied_in = refresh(summed_in, whole_in, stat_l_in, stat_r_in, root_r_in)
    left_ao, right_ao, applied_ao = refresh(
        summed_ao[None], whole_ao[None], stat_l_ao[None], stat_r_ao[None], root_r_ao[None]
    )
    left_fo, right_fo, applied_fo = refresh(
        summed_fo[None], whole_fo[None], stat_l_fo[None], stat_r_fo[None], root_r_fo[None]
    )
    product_in, product_ao, product_fo = (
        lax.all_gather(applied_in.astype(jnp.bfloat16), ("dp", "seq"), axis=2, tiled=True).astype(
            applied_in.dtype
        ),
        lax.all_gather(applied_ao.astype(jnp.bfloat16), ("dp", "seq"), axis=2, tiled=True).astype(
            applied_ao.dtype
        ),
        lax.all_gather(applied_fo.astype(jnp.bfloat16), ("dp", "seq"), axis=2, tiled=True).astype(
            applied_fo.dtype
        ),
    )
    new_w_in = w_in - SHAMPOO_RATE * jnp.einsum(
        "arm,amn->arn", root_l_in, product_in, precision=HIGHEST
    )
    new_w_ao = (
        w_ao
        - SHAMPOO_RATE
        * jnp.einsum("arm,amn->arn", root_l_ao[None], product_ao, precision=HIGHEST)[0]
    )
    new_w_fo = (
        w_fo
        - SHAMPOO_RATE
        * jnp.einsum("arm,amn->arn", root_l_fo[None], product_fo, precision=HIGHEST)[0]
    )
    return (
        layer_out,
        grad_input,
        summed_in,
        summed_ao,
        summed_fo,
        summed_gains,
        new_moment,
        new_second,
        new_gains,
        left_in,
        right_in,
        left_ao[0],
        right_ao[0],
        left_fo[0],
        right_fo[0],
        new_w_in,
        new_w_ao,
        new_w_fo,
    )


QUERY_TILE = 480
ROW_ALIGN = 16
KEY_STEP = 512
KEY_ALIGN = 128
PREP_TILE = 480
LANES = 128
REFRESH_ROWS = 768
ROOT_SPLIT = 640
MASK_BIT = -(2.0**100)
NO_MAX = -3e38
BF16 = jnp.bfloat16
F32 = jnp.float32
VMEM_BYTES = 56 * 2**20


def dot_rows(left, right):
    return lax.dot_general(left, right, (((1,), (1,)), ((), ())), preferred_element_type=F32)


def dot_plain(left, right):
    return lax.dot_general(left, right, (((1,), (0,)), ((), ())), preferred_element_type=F32)


def dot_first(left, right):
    return lax.dot_general(left, right, (((0,), (0,)), ((), ())), preferred_element_type=F32)


def lane_index(rows):
    return lax.broadcasted_iota(jnp.int32, (rows, LANES), 1)


def three_pieces(column):
    first = column.astype(BF16).astype(F32)
    second = (column - first).astype(BF16).astype(F32)
    return first, second, column - first - second


def with_pieces(values, column, lane, at):
    one, two, three = three_pieces(column)
    return jnp.where(
        lane == at, one, jnp.where(lane == at + 1, two, jnp.where(lane == at + 2, three, values))
    ).astype(BF16)


def project_kernel(
    tokens, weight, gain, cosine, sine, query_mask, key_mask, attn_in, query, key, value
):
    step = pl.program_id(0)
    last = pl.num_programs(0) - 1
    own_heads = query.shape[0]
    rows = tokens.shape[0]
    lane = lane_index(rows)
    low_lanes = lane < HEAD_DIM

    @pl.when(step < last)
    def compute():
        normed = norm_forward(tokens[...].astype(F32))[0]
        low = (normed * gain[...]).astype(BF16)
        attn_in[...] = low
        raw = dot_rows(low, weight[...])
        first_half = lane % HEAD_DIM < HEAD_DIM // 2
        ones = jnp.where(lane < HEAD_DIM + 3, 1.0, 0.0)
        for head in range(own_heads):
            both = raw[:, head * LANES : (head + 1) * LANES]
            turned = jnp.where(
                first_half,
                -pltpu.roll(both, LANES - HEAD_DIM // 2, 1),
                pltpu.roll(both, HEAD_DIM // 2, 1),
            )
            both = both * cosine[...] + turned * sine[...]
            query[head] = jnp.where(
                low_lanes, both * SCORE_SCALE, query_mask[...].astype(F32)
            ).astype(BF16)
            key[head] = jnp.where(
                low_lanes, pltpu.roll(both, HEAD_DIM, 1), key_mask[...].astype(F32)
            ).astype(BF16)
            at = own_heads + head // 2
            pair = raw[:, at * LANES : (at + 1) * LANES]
            if head % 2:
                pair = pltpu.roll(pair, HEAD_DIM, 1)
            value[head] = jnp.where(low_lanes, pair, ones).astype(BF16)

    @pl.when(step == last)
    def pad():
        blocked = jnp.where(
            low_lanes,
            0.0,
            jnp.where(lane < HEAD_DIM + 8, MASK_BIT, jnp.where(lane < HEAD_DIM + 11, 1.0, 0.0)),
        ).astype(BF16)
        for head in range(own_heads):
            key[head] = blocked
            value[head] = jnp.zeros((rows, LANES), BF16)


def attend_kernel(
    start_at, step_count, pad_from, query, key, value, pair_out, extra_out, query_out
):
    tile = pl.program_id(0)
    own_heads, rows, _ = query.shape
    lane = lane_index(rows)
    low_lanes = lane < HEAD_DIM
    place = tile * rows + lax.broadcasted_iota(jnp.int32, (rows, 1), 0)
    padded = place >= pad_from[0]
    own_rows = pl.ds(pl.multiple_of(tile * rows, ROW_ALIGN), rows)
    maxima, totals = [], []
    for head in range(own_heads):
        products = query[head].astype(F32) * key[head, own_rows, :].astype(F32)
        self_score = jnp.sum(jnp.where(low_lanes, products, 0.0), axis=1, keepdims=True)
        maxima.append(jnp.where(padded, self_score, NO_MAX))
        totals.append(jnp.where(padded, value[head, own_rows, :].astype(F32), 0.0))
    first = start_at[tile] * KEY_ALIGN

    def step(index, carry):
        maxima, totals = carry
        at = pl.ds(pl.multiple_of(first + index * KEY_STEP, KEY_ALIGN), KEY_STEP)
        new_maxima, new_totals = [], []
        for head in range(own_heads):
            scores = dot_rows(query[head], key[head, at, :])
            row_max = jnp.maximum(maxima[head], jnp.max(scores, axis=1, keepdims=True))
            weights = jnp.exp(scores - row_max).astype(BF16)
            new_totals.append(
                totals[head] * jnp.exp(maxima[head] - row_max)
                + dot_plain(weights, value[head, at, :])
            )
            new_maxima.append(row_max)
        return new_maxima, new_totals

    maxima, totals = lax.fori_loop(0, step_count[tile], step, (maxima, totals))
    outs = []
    for head in range(own_heads):
        row_sum = totals[head][:, HEAD_DIM : HEAD_DIM + 1]
        outs.append(jnp.where(low_lanes, totals[head] * (1.0 / row_sum), 0.0))
        query_out[head] = with_pieces(
            query[head].astype(F32), -(maxima[head] + jnp.log(row_sum)), lane, HEAD_DIM + 8
        )
    pair_out[...] = (outs[0] + pltpu.roll(outs[1], HEAD_DIM, 1)).astype(BF16)
    extra_out[...] = outs[2].astype(BF16)


def attend_back_kernel(
    start_at,
    step_count,
    pad_from,
    query,
    pair_out,
    extra_out,
    grad_pair,
    grad_extra,
    key,
    value,
    cosine,
    sine,
    grads,
    grad_query,
    grad_key,
    grad_value,
):
    tile = pl.program_id(0)
    own_heads, rows, _ = query.shape
    tile_count = grad_query.shape[1] // rows

    @pl.when(tile == 0)
    def clear():
        grad_key[...] = jnp.zeros_like(grad_key)
        grad_value[...] = jnp.zeros_like(grad_value)

    @pl.when(tile < tile_count)
    def accumulate():
        lane = lane_index(rows)
        low_lanes = lane < HEAD_DIM
        own_rows = pl.ds(pl.multiple_of(tile * rows, ROW_ALIGN), rows)
        first = start_at[tile] * KEY_ALIGN
        pair = grad_pair[...].astype(F32)
        extra = grad_extra[...].astype(F32)
        pair_product = pair * pair_out[...].astype(F32)
        products = [
            jnp.where(low_lanes, pair_product, 0.0),
            jnp.where(low_lanes, 0.0, pair_product),
            extra * extra_out[...].astype(F32),
        ]
        incoming = [pair, pltpu.roll(pair, HEAD_DIM, 1), extra]
        grads_out = []
        for head in range(own_heads):
            own = jnp.where(low_lanes, incoming[head], 0.0)
            delta = jnp.sum(products[head], axis=1, keepdims=True)
            grads_out.append(with_pieces(own, -delta, lane, HEAD_DIM))

        def step(index, carry):
            at = pl.ds(pl.multiple_of(first + index * KEY_STEP, KEY_ALIGN), KEY_STEP)
            sums = []
            for head in range(own_heads):
                keys = key[head, at, :]
                probs = jnp.exp(dot_rows(keys, query[head]))
                grad_scores = (probs * dot_rows(value[head, at, :], grads_out[head])).astype(BF16)
                grad_value[head, at, :] += dot_plain(probs.astype(BF16), grads_out[head])
                grad_key[head, at, :] += dot_plain(grad_scores, query[head])
                sums.append(carry[head] + dot_first(grad_scores, keys))
            return sums

        zeros = [jnp.zeros((rows, LANES), F32) for _ in range(own_heads)]
        sums = lax.fori_loop(0, step_count[tile], step, zeros)
        for head in range(own_heads):
            grad_query[head, own_rows, :] = sums[head]

        @pl.when((tile + 1) * rows > pad_from[0])
        def self_terms():
            place = tile * rows + lax.broadcasted_iota(jnp.int32, (rows, 1), 0)
            padded = place >= pad_from[0]
            for head in range(own_heads):
                keys = key[head, own_rows, :].astype(F32)
                queries = query[head].astype(F32)
                outs = grads_out[head].astype(F32)
                counted = low_lanes | (lane >= HEAD_DIM + 8)
                score = jnp.sum(jnp.where(counted, queries * keys, 0.0), axis=1, keepdims=True)
                prob = jnp.where(padded, jnp.exp(jnp.where(padded, score, 0.0)), 0.0)
                grad_prob = jnp.sum(
                    outs * value[head, own_rows, :].astype(F32), axis=1, keepdims=True
                )
                grad_score = (prob * grad_prob).astype(BF16).astype(F32)
                low_prob = prob.astype(BF16).astype(F32)
                grad_query[head, own_rows, :] += grad_score * jnp.where(low_lanes, keys, 0.0)
                grad_key[head, own_rows, :] += grad_score * queries
                grad_value[head, own_rows, :] += low_prob * outs

    @pl.when(tile >= tile_count)
    def finish():
        size = grads.shape[0]
        at = pl.ds(pl.multiple_of((tile - tile_count) * size, ROW_ALIGN), size)
        lane = lane_index(size)
        low_lanes = lane < HEAD_DIM
        first_half = lane % HEAD_DIM < HEAD_DIM // 2
        values, turns = [], []
        for head in range(own_heads):
            both = jnp.where(
                low_lanes,
                grad_query[head, at, :] * SCORE_SCALE,
                pltpu.roll(grad_key[head, at, :], HEAD_DIM, 1),
            )
            shifted = both * sine[...]
            turned = jnp.where(
                first_half,
                pltpu.roll(shifted, LANES - HEAD_DIM // 2, 1),
                -pltpu.roll(shifted, HEAD_DIM // 2, 1),
            )
            turns.append(both * cosine[...] + turned)
            values.append(jnp.where(low_lanes, grad_value[head, at, :], 0.0))
        swapped = pltpu.roll(turns[1], HEAD_DIM, 1)
        grads[:, :LANES] = jnp.where(low_lanes, turns[0], swapped).astype(BF16)
        grads[:, LANES : 2 * LANES] = jnp.where(low_lanes, turns[2], turns[0]).astype(BF16)
        grads[:, 2 * LANES : 3 * LANES] = jnp.where(low_lanes, swapped, turns[2]).astype(BF16)
        base = own_heads * LANES
        grads[:, base : base + LANES] = (values[0] + pltpu.roll(values[1], HEAD_DIM, 1)).astype(
            BF16
        )
        grads[:, base + LANES : base + 2 * LANES] = values[2].astype(BF16)


def refresh_kernel(
    full, own, select, stat_left, stat_right, root_left, right_root, weight, *refs, kept, own_at, root_at
):
    new_left, new_right, new_weight, columns, total = refs[kept:]
    step = pl.program_id(0)
    chosen = select.shape[0]
    count = new_right.shape[-2]
    own_rows = own[:, own_at : own_at + full.shape[1]]
    outer = dot_rows(jnp.concatenate([select[...], own_rows]), full[...])
    columns[...] = outer[:chosen]
    new_left[0] = 0.5 * stat_left[0] + 0.5 * outer[chosen:]
    left = jnp.concatenate([outer[:chosen].astype(BF16), root_left[0].astype(BF16)])
    product = dot_plain(left, full[...])

    @pl.when(step == 0)
    def begin():
        total[...] = product

    @pl.when(step > 0)
    def add():
        total[...] += product

    @pl.when(step == pl.num_programs(0) - 1)
    def finish():
        new_right[0] = 0.5 * stat_right[0] + 0.5 * total[:count, :]
        product = total[chosen:, :].astype(BF16)
        if root_at is None:
            new_weight[0] = weight[0] - SHAMPOO_RATE * dot_plain(product, right_root[...])
        else:
            size = product.shape[1]
            rest = root_at + size
            new_weight[0] = dot_rows(product, right_root[:, root_at:rest])
            new_weight[1] = dot_rows(
                product[:, :ROOT_SPLIT], right_root[:, rest : rest + ROOT_SPLIT]
            )
            new_weight[2] = dot_rows(
                product[:, ROOT_SPLIT:], right_root[:, rest : rest + size - ROOT_SPLIT]
            )


def refresh(
    at, full, own, own_at, select, stat_left, stat_right, root_left, roots, root_at, weight, previous
):
    in_dim, out_dim = full.shape
    chunk = REFRESH_ROWS
    rows, count, chosen = own.shape[0], stat_right.shape[1], select.shape[0]

    def by_chunk(rows):
        return pl.BlockSpec((1, rows, chunk), lambda i: (at, 0, i))

    def whole(*shape):
        return pl.BlockSpec(shape, lambda i: (0,) * len(shape))

    def stacked(array):
        return pl.BlockSpec((1,) + array.shape[1:], lambda i: (at, 0, 0))

    kept = [pl.BlockSpec(memory_space=pl.ANY)] * len(previous)
    square = root_at >= 0
    if square:
        new_weight = stacked(weight), weight.shape
        root_block = pl.BlockSpec((out_dim, out_dim), lambda i: (0, root_at))
    else:
        parts = (3, rows, roots.shape[0])
        new_weight = whole(*parts), parts
        root_block = whole(*roots.shape)
    return pl.pallas_call(
        functools.partial(
            refresh_kernel,
            kept=len(previous),
            own_at=own_at,
            root_at=None if square else -root_at,
        ),
        grid=(in_dim // chunk,),
        in_specs=[
            pl.BlockSpec((chunk, out_dim), lambda i: (i, 0)),
            whole(*own.shape),
            whole(*select.shape),
            by_chunk(rows),
            stacked(stat_right),
            by_chunk(rows),
            root_block,
            stacked(weight),
        ]
        + kept,
        out_specs=[
            by_chunk(rows),
            stacked(stat_right),
            new_weight[0],
            pl.BlockSpec((chosen, chunk), lambda i: (0, i)),
        ],
        out_shape=[
            jax.ShapeDtypeStruct(stat_left.shape, F32),
            jax.ShapeDtypeStruct(stat_right.shape, F32),
            jax.ShapeDtypeStruct(new_weight[1], F32),
            jax.ShapeDtypeStruct((chosen, in_dim), F32),
        ],
        scratch_shapes=[pltpu.VMEM((chosen + rows, out_dim), F32)],
        input_output_aliases={8 + i: i for i in range(len(previous))},
        compiler_params=pltpu.CompilerParams(vmem_limit_bytes=VMEM_BYTES),
        cost_estimate=pl.CostEstimate(
            flops=4 * (chosen + rows) * in_dim * out_dim,
            bytes_accessed=2 * in_dim * out_dim + 12 * rows * in_dim + 2 * out_dim * out_dim,
            transcendentals=0,
        ),
        name="refresh",
    )(
        full,
        own,
        select,
        stat_left,
        stat_right,
        root_left,
        roots,
        weight,
        *previous,
    )


def exchange(values, axis, offset):
    size = lax.axis_size(axis)
    return lax.ppermute(values, axis, [(i, i ^ offset) for i in range(size)])


def arrange_kernel(own_at, *refs, count, moves):
    blocks, outs, sems = refs[:count], refs[count:-1], refs[-1]
    copies = []
    for index, (number, offset, source, which, target) in enumerate(moves):
        place = own_at[0] ^ offset
        start = blocks[number].at[source] if source else blocks[number]
        end = outs[which].at[tuple(place if at == "place" else at for at in target)]
        copies.append(pltpu.make_async_copy(start, end, sems.at[index]))
    for copy in copies:
        copy.start()
    for copy in copies:
        copy.wait()


def arrange(blocks, own_at, shapes, moves):
    count = len(blocks)
    return pl.pallas_call(
        functools.partial(arrange_kernel, count=count, moves=moves),
        in_specs=[pl.BlockSpec(memory_space=pltpu.SMEM)]
        + [pl.BlockSpec(memory_space=pl.ANY)] * count,
        out_specs=[pl.BlockSpec(memory_space=pltpu.VMEM)] * len(shapes),
        scratch_shapes=[pltpu.SemaphoreType.DMA((len(moves),))],
        out_shape=[jax.ShapeDtypeStruct(shape, blocks[0].dtype) for shape in shapes],
        compiler_params=pltpu.CompilerParams(vmem_limit_bytes=VMEM_BYTES),
        cost_estimate=pl.CostEstimate(
            flops=0, bytes_accessed=2 * count * blocks[0].size * 2, transcendentals=0
        ),
        name="arrange",
    )(own_at[None], *blocks)


def terms_kernel(
    core, grad_proj, ffn_in, grad_out, attended, cotangent, middle, send, keep
):
    step = pl.program_id(0)
    groups, rows, _ = send.shape
    width = ffn_in.shape[1]
    chunk = 2 * groups * rows
    pieces = [(grad_proj, part * width, ffn_in) for part in range(grad_proj.shape[1] // width)]
    pieces += [(grad_out, 0, attended), (cotangent, 0, middle)]
    first = 0
    for left, offset, right in pieces:
        columns = pl.ds(pl.multiple_of(offset + step * chunk, KEY_ALIGN), chunk)
        term = dot_first(left[:, columns], right[...]).astype(BF16)
        last = first + right.shape[1]
        for own in range(2):

            @pl.when(core[0] == own)
            def store():
                for group in range(groups):
                    for side, out in ((own, keep), (1 - own, send)):
                        at = (2 * group + side) * rows
                        out[group, :, first:last] = term[at : at + rows]

        first = last


def gather_plane(values, by_steps=False):
    last = None if by_steps else exchange(values, "seq", 3)
    far = exchange(values, "seq", 2)
    last = exchange(far, "seq", 1) if by_steps else last
    blocks = [values, exchange(values, "seq", 1), far, last]
    shape = (len(blocks),) + values.shape
    moves = [(k, k, (), 0, ("place",)) for k in range(len(blocks))]
    return arrange(blocks, lax.axis_index("seq"), [shape], moves)[0]


def gather_near(plane):
    half = plane.shape[0] // 2
    left, right = plane[:half], plane[half:]
    left_two, right_four = exchange(left, "dp", 2), exchange(right, "dp", 4)
    return [left, right, left_two, exchange(right, "dp", 2), exchange(left, "dp", 4), right_four]


def gather_far(near):
    return [*near, exchange(near[2], "dp", 4), exchange(near[5], "dp", 2)]


def gather_partners(plane):
    return gather_far(gather_near(plane))


def gather_cores(even):
    blocks = []
    for k in range(0, len(even), 2):
        blocks += [*even[k : k + 2], *(exchange(block, "dp", 1) for block in even[k : k + 2])]
    return blocks


def half_moves(blocks, cuts):
    half = blocks[0].shape[0]
    moves = []
    for number in range(len(blocks)):
        rows = slice(number % 2 * half, (number % 2 + 1) * half)
        for source, which, target in cuts:
            end = tuple(rows if at == "half" else at for at in target)
            moves.append((number, number // 2, source, which, end))
    return moves


def column_moves(blocks, widths):
    shapes, cuts, first = [], [], 0
    half, rows, _ = blocks[0].shape
    for which, width in enumerate(widths):
        shapes.append((len(blocks) // 2, 2 * half, rows, width))
        source = (slice(None), slice(None), slice(first, first + width))
        cuts.append((source, which, ("place", "half")))
        first += width
    return shapes, half_moves(blocks, cuts)


def fence(*values):
    return lax.optimization_barrier(values)


def add_blocks(blocks):
    total = blocks[0].astype(F32)
    for block in blocks[1:]:
        total = total + block.astype(F32)
    return total


def pair_sums(send, keep, axis=0):
    came = exchange(send, "dp", 1)
    own_at = lax.axis_index("dp") >> 1
    return [
        add_blocks(
            [
                lax.dynamic_index_in_dim(side, own_at ^ k, axis, keepdims=False)
                for side in (keep, came)
            ]
        )
        for k in range(keep.shape[axis])
    ]


def swap_blocks(blocks, axis, unit):
    came = [exchange(blocks[k], axis, k * unit) for k in range(len(blocks) - 1, 0, -1)]
    return [blocks[0]] + came[::-1]


def add_partners(blocks, axis, unit):
    return add_blocks(swap_blocks(blocks, axis, unit))


def lows(blocks):
    return [block.astype(BF16) for block in blocks]


def by_distance(values, axis):
    own_at = lax.axis_index(axis)
    return [
        lax.dynamic_index_in_dim(values, own_at ^ k, 0, keepdims=False)
        for k in range(values.shape[0])
    ]


def head_body(
    tokens,
    cotangent,
    doc_lengths,
    pad_counts,
    w_in,
    w_ao,
    w_fo,
    norm_gains,
    gain_moment,
    gain_second,
    stat_l_in,
    stat_r_in,
    stat_l_ao,
    stat_r_ao,
    stat_l_fo,
    stat_r_fo,
    root_l_in,
    root_r_in,
    root_l_ao,
    root_r_ao,
    root_l_fo,
    root_r_fo,
):
    token_count, width = tokens.shape
    hidden = w_fo.shape[1]
    seq_count, dp_count = lax.axis_size("seq"), lax.axis_size("dp")
    all_count = seq_count * dp_count
    row_length = token_count * seq_count
    seq_at = lax.axis_index("seq")
    dev_at = lax.axis_index(("dp", "seq"))
    head_count = width // HEAD_DIM
    own_heads = head_count // seq_count
    own_width = own_heads * HEAD_DIM
    in_rows = w_in.shape[1]
    ao_rows = w_ao.shape[0]
    gain_cols = norm_gains.shape[1]

    gain_lanes = jnp.zeros((in_rows, LANES), BF16).at[:2, :gain_cols].set(norm_gains.astype(BF16))
    up_parts = in_rows // ao_rows
    row_tokens = lax.all_gather(tokens, "seq", axis=0, tiled=True)
    qkv_blocks = gather_cores(
        gather_partners(gather_plane(jnp.concatenate([w_in[0].astype(BF16), gain_lanes], axis=1)))
    )
    full_qkv, gain_blocks = arrange(
        qkv_blocks, lax.axis_index("dp"), *column_moves(qkv_blocks, [width, LANES])
    )
    full_qkv = full_qkv.reshape(all_count * in_rows, width)
    gain_rows = (
        jnp.transpose(gain_blocks[:, :, :2, :gain_cols], (2, 0, 1, 3)).reshape(2, width).astype(F32)
    )
    full_up = lax.all_gather(w_in[1].astype(BF16), ("dp", "seq"), axis=0, tiled=True)
    out_weights = jnp.concatenate([w_ao.astype(BF16), w_fo.astype(BF16)], axis=1)
    row_tokens, out_weights = fence(row_tokens, out_weights)
    out_plane = gather_plane(out_weights)
    root_rows = stat_r_in.shape[1]
    fo_rest = root_r_fo.shape[0] - root_rows
    rest_rows = root_r_fo[root_rows:].astype(BF16)
    wrapped = jnp.concatenate(
        [
            rest_rows[:, :ROOT_SPLIT],
            jnp.pad(rest_rows[:, ROOT_SPLIT:], ((0, 0), (0, 2 * ROOT_SPLIT - hidden))),
        ]
    )
    roots = jnp.concatenate(
        [
            root_r_in[0].astype(BF16),
            root_r_in[1].astype(BF16),
            root_r_ao.astype(BF16),
            root_r_fo[:root_rows].astype(BF16),
            wrapped,
        ],
        axis=1,
    )

    lengths = doc_lengths[0]
    segment, within, is_valid = doc_tables(lengths, pad_counts[0], row_length)
    pad_from = row_length - pad_counts[0]
    doc_ids = jnp.arange(lengths.shape[0], dtype=jnp.int32)
    places = jnp.arange(row_length, dtype=jnp.int32)
    doc_begin = places - within
    doc_end = doc_begin + jnp.sum(
        jnp.where(segment[:, None] == doc_ids[None, :], lengths[None, :], 0), axis=1
    )
    freq_index = jnp.arange(0, HEAD_DIM, 2, dtype=F32)
    inverse = 1.0 / jnp.power(ROPE_THETA, freq_index / HEAD_DIM)
    angles = within.astype(F32)[:, None] * inverse[None, :]
    copies = LANES // (HEAD_DIM // 2)
    cos_table = jnp.concatenate([jnp.cos(angles)] * copies, axis=1)
    sin_table = jnp.concatenate([jnp.sin(angles)] * copies, axis=1)
    lane = jnp.arange(LANES, dtype=jnp.int32)
    in_doc = lane[None, :] - HEAD_DIM == segment[:, None]
    mask_lanes = (lane >= HEAD_DIM) & (lane < HEAD_DIM + 8)
    one_lanes = (lane >= HEAD_DIM + 8) & (lane < HEAD_DIM + 11)
    query_mask = in_doc.astype(BF16)
    key_mask = jnp.where(
        mask_lanes[None, :] & ~(in_doc & is_valid[:, None]),
        MASK_BIT,
        jnp.where(one_lanes[None, :], 1.0, 0.0),
    ).astype(BF16)
    tile_starts = doc_begin[::QUERY_TILE] // KEY_ALIGN
    tile_ends = jnp.minimum(doc_end[QUERY_TILE - 1 :: QUERY_TILE], pad_from)
    tile_steps = jnp.maximum(-((tile_starts * KEY_ALIGN - tile_ends) // KEY_STEP), 0)
    tile_count = row_length // QUERY_TILE
    pad_at = pad_from[None]

    qkv_heads = lax.dynamic_slice_in_dim(
        full_qkv.reshape(3, head_count, HEAD_DIM, width), seq_at * own_heads, own_heads, 1
    )
    own_weight = jnp.concatenate(
        [
            jnp.transpose(qkv_heads[:2], (1, 0, 2, 3)).reshape(2 * own_width, width),
            qkv_heads[2].reshape(own_width, width),
            jnp.zeros((HEAD_DIM, width), BF16),
        ]
    )
    back_weight = jnp.concatenate(
        [qkv_heads.reshape(3 * own_width, width), jnp.zeros((HEAD_DIM, width), BF16)]
    )
    own_columns = own_weight.shape[0]
    prep_count = row_length // PREP_TILE
    key_length = row_length + PREP_TILE

    def row_block(columns):
        return pl.BlockSpec(
            (PREP_TILE, columns), lambda i, *_: (jnp.minimum(i, prep_count - 1), 0)
        )

    def fixed_block(*shape):
        return pl.BlockSpec(shape, lambda i, *_: (0,) * len(shape))

    head_block = pl.BlockSpec((own_heads, PREP_TILE, LANES), lambda i, *_: (0, i, 0))
    attn_in, query_ext, key_ext, value_ext = pl.pallas_call(
        project_kernel,
        grid=(prep_count + 1,),
        in_specs=[
            row_block(width),
            fixed_block(own_columns, width),
            fixed_block(1, width),
            row_block(LANES),
            row_block(LANES),
            row_block(LANES),
            row_block(LANES),
        ],
        out_specs=[
            row_block(width),
            pl.BlockSpec(
                (own_heads, PREP_TILE, LANES), lambda i: (0, jnp.minimum(i, prep_count - 1), 0)
            ),
            head_block,
            head_block,
        ],
        out_shape=[
            jax.ShapeDtypeStruct((row_length, width), BF16),
            jax.ShapeDtypeStruct((own_heads, row_length, LANES), BF16),
            jax.ShapeDtypeStruct((own_heads, key_length, LANES), BF16),
            jax.ShapeDtypeStruct((own_heads, key_length, LANES), BF16),
        ],
        compiler_params=pltpu.CompilerParams(vmem_limit_bytes=VMEM_BYTES),
        cost_estimate=pl.CostEstimate(
            flops=2 * row_length * own_columns * width,
            bytes_accessed=14_000_000,
            transcendentals=0,
        ),
        name="project",
    )(
        row_tokens,
        own_weight,
        gain_rows[:1],
        cos_table,
        sin_table,
        query_mask,
        key_mask,
    )

    query_ext, key_ext, value_ext, out_plane = fence(query_ext, key_ext, value_ext, out_plane)
    out_partners = gather_partners(out_plane)

    def tile_block(columns):
        return pl.BlockSpec(
            (QUERY_TILE, columns), lambda i, *_: (jnp.minimum(i, tile_count - 1), 0)
        )

    head_tile = pl.BlockSpec(
        (own_heads, QUERY_TILE, LANES), lambda i, *_: (0, jnp.minimum(i, tile_count - 1), 0)
    )
    whole_keys = fixed_block(own_heads, key_length, LANES)
    pair_out, extra_out, query_low = pl.pallas_call(
        attend_kernel,
        grid_spec=pltpu.PrefetchScalarGridSpec(
            num_scalar_prefetch=3,
            grid=(tile_count,),
            in_specs=[head_tile, whole_keys, whole_keys],
            out_specs=[tile_block(LANES), tile_block(LANES), head_tile],
        ),
        out_shape=[
            jax.ShapeDtypeStruct((row_length, LANES), BF16),
            jax.ShapeDtypeStruct((row_length, LANES), BF16),
            jax.ShapeDtypeStruct((own_heads, row_length, LANES), BF16),
        ],
        compiler_params=pltpu.CompilerParams(vmem_limit_bytes=VMEM_BYTES),
        cost_estimate=pl.CostEstimate(
            flops=2 * own_heads * row_length * row_length * LANES,
            bytes_accessed=12_000_000,
            transcendentals=0,
        ),
        name="attend",
    )(tile_starts, tile_steps, pad_at, query_ext, key_ext, value_ext)

    fenced = fence(pair_out, extra_out, query_low, *out_partners)
    pair_out, extra_out, query_low = fenced[:3]
    out_blocks = gather_cores(fenced[3:])
    full_ao, full_fo = arrange(
        out_blocks, lax.axis_index("dp"), *column_moves(out_blocks, [width, hidden])
    )
    full_ao = full_ao.reshape(width, width)
    full_fo = full_fo.reshape(width, hidden)

    half_tokens = token_count // 2

    def fold(extra):
        blocks = extra[:, :HEAD_DIM].reshape(seq_count, 2, half_tokens, HEAD_DIM)
        return jnp.concatenate([blocks[:, 0], blocks[:, 1]], axis=-1)

    def unfold(folded):
        return jnp.concatenate([folded[:, :, :HEAD_DIM], folded[:, :, HEAD_DIM:]], axis=1)

    packed = jnp.concatenate(
        [pair_out.reshape(seq_count, token_count, LANES), fold(extra_out)], axis=1
    )
    packed = lax.all_to_all(packed, "seq", 0, 0, tiled=True)
    attn_low = jnp.concatenate([packed[:, :token_count], unfold(packed[:, token_count:])], axis=-1)
    attn_low = jnp.transpose(attn_low, (1, 0, 2)).reshape(token_count, width)

    inputs = tokens.astype(F32)
    residual = inputs + apply_rows(attn_low, full_ao)
    normed_two, spread_two = norm_forward(residual)
    ffn_in = (normed_two * gain_rows[1]).astype(BF16)
    projected = apply_rows(ffn_in, full_up)
    inner_part = projected[:, :hidden]
    gate_part = projected[:, hidden:]
    activated = gelu_value(inner_part)
    mid_low = (activated * gate_part).astype(BF16)
    layer_out = (residual + apply_rows(mid_low, full_fo)).astype(BF16)
    grad_mid = jnp.dot(cotangent, full_fo, preferred_element_type=F32)
    grad_proj = jnp.concatenate(
        [grad_mid * gate_part * gelu_slope(inner_part), grad_mid * activated], axis=1
    ).astype(BF16)
    grad_ffn_in = jnp.dot(grad_proj, full_up, preferred_element_type=F32)
    grad_norm_two, _ = norm_backward(grad_ffn_in, normed_two, spread_two, gain_rows[1])
    grad_resid = cotangent.astype(F32) + grad_norm_two
    grad_out_attn = grad_resid.astype(BF16)
    grad_attn = jnp.dot(grad_out_attn, full_ao, preferred_element_type=F32).astype(BF16)

    grad_blocks = jnp.transpose(
        grad_attn.reshape(token_count, seq_count, own_width), (1, 0, 2)
    )
    folded = grad_blocks[:, :, LANES:].reshape(seq_count, 2, half_tokens, HEAD_DIM)
    packed_back = jnp.concatenate(
        [grad_blocks[:, :, :LANES], jnp.concatenate([folded[:, 0], folded[:, 1]], axis=-1)], axis=1
    )
    packed_back = lax.all_to_all(packed_back, "seq", 0, 0, tiled=True)

    pack_width = up_parts * width + width + hidden
    pair_count = dp_count // 2
    block_rows = seq_count * ao_rows
    core = lax.axis_index("dp") & 1
    operands = (grad_proj, ffn_in, grad_out_attn, attn_low, cotangent, mid_low)
    half_block = pl.BlockSpec((pair_count // 2, block_rows, pack_width), lambda i: (i, 0, 0))
    send_terms, keep_terms = pl.pallas_call(
        terms_kernel,
        grid=(2,),
        in_specs=[pl.BlockSpec(memory_space=pltpu.SMEM)]
        + [pl.BlockSpec(operand.shape, lambda i: (0, 0)) for operand in operands],
        out_specs=[half_block, half_block],
        out_shape=[jax.ShapeDtypeStruct((pair_count, block_rows, pack_width), BF16)] * 2,
        compiler_params=pltpu.CompilerParams(vmem_limit_bytes=VMEM_BYTES),
        cost_estimate=pl.CostEstimate(
            flops=2 * token_count * width * pack_width,
            bytes_accessed=13_000_000,
            transcendentals=0,
        ),
        name="terms",
    )(core[None], *operands)
    send_terms, packed_back, roots = fence(send_terms, packed_back, roots)
    roots = lax.all_gather(roots, ("dp", "seq"), axis=0, tiled=True)
    pair_blocks = lows(pair_sums(send_terms, keep_terms))
    grad_pair = packed_back[:, :token_count]
    grad_extra = packed_back[:, token_count:]
    grad_pair = grad_pair.reshape(row_length, LANES)
    grad_extra = unfold(grad_extra).reshape(row_length, HEAD_DIM)
    grad_extra = jnp.pad(grad_extra, ((0, 0), (0, LANES - HEAD_DIM)))
    fenced = fence(grad_pair, grad_extra, *pair_blocks)
    grad_pair, grad_extra, pair_blocks = fenced[0], fenced[1], fenced[2:]
    plane_blocks = [pair_blocks[0]] + [
        exchange(block, "dp", 2 * k) for k, block in enumerate(pair_blocks) if k
    ]

    finish_count = prep_count

    def finish_block(columns):
        return pl.BlockSpec(
            (PREP_TILE, columns), lambda i, *_: (jnp.maximum(i - tile_count, 0), 0)
        )

    grad_qkv = pl.pallas_call(
        attend_back_kernel,
        grid_spec=pltpu.PrefetchScalarGridSpec(
            num_scalar_prefetch=3,
            grid=(tile_count + finish_count,),
            in_specs=[
                head_tile,
                tile_block(LANES),
                tile_block(LANES),
                tile_block(LANES),
                tile_block(LANES),
                whole_keys,
                whole_keys,
                finish_block(LANES),
                finish_block(LANES),
            ],
            out_specs=finish_block(own_columns),
            scratch_shapes=[
                pltpu.VMEM((own_heads, row_length, LANES), F32),
                pltpu.VMEM((own_heads, key_length, LANES), F32),
                pltpu.VMEM((own_heads, key_length, LANES), F32),
            ],
        ),
        out_shape=jax.ShapeDtypeStruct((row_length, own_columns), BF16),
        compiler_params=pltpu.CompilerParams(vmem_limit_bytes=VMEM_BYTES),
        cost_estimate=pl.CostEstimate(
            flops=5 * own_heads * row_length * row_length * LANES,
            bytes_accessed=15_000_000,
            transcendentals=0,
        ),
        name="attend_back",
    )(
        tile_starts,
        tile_steps,
        pad_at,
        query_low,
        pair_out,
        extra_out,
        grad_pair,
        grad_extra,
        key_ext,
        value_ext,
        cos_table,
        sin_table,
    )
    fenced = fence(grad_qkv, *plane_blocks)
    grad_qkv = fenced[0]
    plane_sum = add_blocks(fenced[1:]).astype(BF16).reshape(seq_count, ao_rows, pack_width)
    seq_blocks = by_distance(plane_sum, "seq")
    far_sum = add_blocks([seq_blocks[2], exchange(seq_blocks[3], "seq", 1)]).astype(BF16)
    near_sum = add_blocks([seq_blocks[0], exchange(seq_blocks[1], "seq", 1)])
    summed = add_blocks([near_sum, exchange(far_sum, "seq", 2)])
    low_sum = summed.astype(BF16)
    term_plane = gather_plane(low_sum, by_steps=True)
    summed_ao = summed[:, up_parts * width : (up_parts + 1) * width]
    summed_fo = summed[:, (up_parts + 1) * width :]

    qkv_term = outer_sum(grad_qkv, attn_in)[: 3 * own_width].astype(BF16)
    qkv_rows = own_width // dp_count
    qkv_term = qkv_term.reshape(3, pair_count, 2, qkv_rows, width)
    qkv_halves = [
        lax.dynamic_index_in_dim(qkv_term, side, 2, keepdims=False) for side in (1 - core, core)
    ]
    qkv_sum = add_partners(lows(pair_sums(*qkv_halves, axis=1)), "dp", 2).astype(BF16)
    qkv_plane = gather_plane(qkv_sum, by_steps=True)
    input_term = jnp.dot(grad_qkv, back_weight, preferred_element_type=F32).astype(BF16)
    input_term, roots = fence(input_term, roots, qkv_plane, term_plane)[:2]
    qkv_blocks = gather_cores(gather_partners(qkv_plane))
    term_partners = gather_partners(term_plane)
    grad_attn_in = lax.psum_scatter(input_term, "seq", scatter_dimension=0, tiled=True).astype(F32)
    normed_one, spread_one = norm_forward(inputs)
    grad_norm_one, _ = norm_backward(grad_attn_in, normed_one, spread_one, gain_rows[0])
    grad_input = grad_resid + grad_norm_one

    def select(count, size):
        places = jnp.arange(-(-count // 16) * 16, dtype=jnp.int32)[:, None]
        wanted = jnp.where(places < count, dev_at * count + places, -1)
        return (wanted == jnp.arange(size, dtype=jnp.int32)[None, :]).astype(BF16)

    select_in = select(stat_r_in.shape[1], width)
    select_fo = select(stat_r_fo.shape[0], hidden)
    [whole_qkv] = arrange(
        qkv_blocks,
        lax.axis_index("dp"),
        [(3, seq_count, dp_count, qkv_rows, width)],
        half_moves(qkv_blocks, [((slice(None), part), 0, (part, "half", "place")) for part in range(3)]),
    )
    whole_qkv = whole_qkv.reshape(3 * width, width)
    low_qkv = lax.dynamic_slice_in_dim(whole_qkv, dev_at * in_rows, in_rows, 0)
    *stacked, qkv_columns = refresh(
        0, whole_qkv, low_qkv, 0, select_in, stat_l_in, stat_r_in, root_l_in, roots, 0, w_in, []
    )
    fenced = fence(stacked, *term_partners)
    stacked, term_blocks = fenced[0], gather_cores(fenced[1:])
    whole_shape = (dp_count, seq_count, ao_rows)
    cut = (slice(None), slice(None))
    whole_up, whole_ao, whole_fo = arrange(
        term_blocks,
        lax.axis_index("dp"),
        [(up_parts,) + whole_shape + (width,), whole_shape + (width,), whole_shape + (hidden,)],
        half_moves(
            term_blocks,
            [
                (cut + (slice(part * width, (part + 1) * width),), 0, (part, "place", "half"))
                for part in range(up_parts)
            ]
            + [
                (cut + (slice(up_parts * width, (up_parts + 1) * width),), 1, ("place", "half")),
                (cut + (slice((up_parts + 1) * width, pack_width),), 2, ("place", "half")),
            ],
        ),
    )
    whole_up = whole_up.reshape(up_parts * width, width)
    whole_ao = whole_ao.reshape(width, width)
    whole_fo = whole_fo.reshape(width, hidden)
    low_up = lax.dynamic_slice_in_dim(whole_up, dev_at * in_rows, in_rows, 0)
    left_ao, right_stat_ao, new_ao, _ = refresh(
        0,
        whole_ao,
        low_sum,
        up_parts * width,
        select_in,
        stat_l_ao[None],
        stat_r_ao[None],
        root_l_ao[None],
        roots,
        2,
        w_ao[None],
        [],
    )
    left_fo, right_stat_fo, fo_parts, _ = refresh(
        0,
        whole_fo,
        low_sum,
        (up_parts + 1) * width,
        select_fo,
        stat_l_fo[None],
        stat_r_fo[None],
        root_l_fo[None],
        roots,
        -3 * width,
        w_fo[None],
        [],
    )
    update_first = fo_parts[0].reshape(ao_rows, all_count, root_rows)
    update_rest = fo_parts[1].reshape(ao_rows, all_count, root_rows)[:, :, :fo_rest]
    update_rest += fo_parts[2].reshape(ao_rows, all_count, root_rows)[:, :, fo_rest:]
    update = jnp.concatenate([update_first, update_rest], axis=2).reshape(ao_rows, hidden)
    new_fo = w_fo - SHAMPOO_RATE * update
    *stacked, up_columns = refresh(
        1, whole_up, low_up, 0, select_in, stat_l_in, stat_r_in, root_l_in, roots, 1, w_in, stacked
    )
    new_left_in, new_right_in, new_in = stacked

    def gain_gradient(weight, columns, gain):
        own_weight_columns = lax.dynamic_slice_in_dim(weight, dev_at * gain_cols, gain_cols, 1)
        products = jnp.transpose(own_weight_columns).astype(F32) * columns[:gain_cols]
        own_gain = lax.dynamic_slice_in_dim(gain, dev_at * gain_cols, gain_cols)
        return jnp.sum(products, axis=1) / own_gain

    summed_gains = jnp.stack(
        [
            gain_gradient(full_qkv, qkv_columns, gain_rows[0]),
            gain_gradient(full_up, up_columns, gain_rows[1]),
        ]
    )
    new_moment = 0.9 * gain_moment + 0.1 * summed_gains
    new_second = 0.999 * gain_second + 0.001 * summed_gains * summed_gains
    new_gains = norm_gains - ADAM_RATE * new_moment / (jnp.sqrt(new_second) + 1e-08)
    return (
        layer_out,
        grad_input,
        jnp.stack([low_qkv, low_up]).astype(F32),
        summed_ao,
        summed_fo,
        summed_gains,
        new_moment,
        new_second,
        new_gains,
        new_left_in,
        new_right_in,
        left_ao[0],
        right_stat_ao[0],
        left_fo[0],
        right_stat_fo[0],
        new_in,
        new_ao[0],
        new_fo,
    )


def body(tokens, *others):
    seq_count, dp_count = lax.axis_size("seq"), lax.axis_size("dp")
    token_count, width = tokens.shape
    row_length = token_count * seq_count
    by_heads = (
        width // HEAD_DIM == 3 * seq_count
        and dp_count & (dp_count - 1) == 0
        and seq_count & (seq_count - 1) == 0
        and row_length % QUERY_TILE == 0
        and token_count == PREP_TILE
        and dp_count == 8
        and seq_count == 4
        and others[3].shape[1] == 3 * others[4].shape[0]
        and others[5].shape[1] == 1152
        and others[1].shape[1] == 8
    )
    return head_body(tokens, *others) if by_heads else sequence_body(tokens, *others)


def solution(mesh):
    in_specs = (
        P(("dp", "seq"), None),
        P(("dp", "seq"), None),
        P("dp", None),
        P("dp"),
        P(None, ("dp", "seq"), None),
        P(("dp", "seq"), None),
        P(("dp", "seq"), None),
        P(None, ("dp", "seq")),
        P(None, ("dp", "seq")),
        P(None, ("dp", "seq")),
        P(None, ("dp", "seq"), None),
        P(None, ("dp", "seq"), None),
        P(("dp", "seq"), None),
        P(("dp", "seq"), None),
        P(("dp", "seq"), None),
        P(("dp", "seq"), None),
        P(None, ("dp", "seq"), None),
        P(None, ("dp", "seq"), None),
        P(("dp", "seq"), None),
        P(("dp", "seq"), None),
        P(("dp", "seq"), None),
        P(("dp", "seq"), None),
    )
    out_specs = (
        P(("dp", "seq"), None),
        P(("dp", "seq"), None),
        P(None, ("dp", "seq"), None),
        P(("dp", "seq"), None),
        P(("dp", "seq"), None),
        P(None, ("dp", "seq")),
        P(None, ("dp", "seq")),
        P(None, ("dp", "seq")),
        P(None, ("dp", "seq")),
        P(None, ("dp", "seq"), None),
        P(None, ("dp", "seq"), None),
        P(("dp", "seq"), None),
        P(("dp", "seq"), None),
        P(("dp", "seq"), None),
        P(("dp", "seq"), None),
        P(None, ("dp", "seq"), None),
        P(("dp", "seq"), None),
        P(("dp", "seq"), None),
    )
    return jax.shard_map(body, mesh=mesh, in_specs=in_specs, out_specs=out_specs, check_vma=False)
```

```python
import functools
import math

import jax
import jax.numpy as jnp
from jax import lax
from jax.experimental import pallas as pl
from jax.experimental.pallas import tpu as pltpu
from jax.sharding import PartitionSpec as P

HEAD_DIM = 64


NORM_EPS = 1e-05
ROPE_THETA = 160000.0
SCORE_SCALE = 0.125
MASK_FILL = -1e30
ADAM_RATE = 0.2
SHAMPOO_RATE = 1.0
HIGHEST = lax.Precision.HIGHEST


def norm_forward(values):
    center = values - jnp.mean(values, axis=-1, keepdims=True)
    inv_spread = lax.rsqrt(jnp.mean(center * center, axis=-1, keepdims=True) + NORM_EPS)
    return (center * inv_spread, inv_spread)


def norm_backward(grad_out, normed, inv_spread, gain_row):
    scaled = grad_out * gain_row
    inner_term = (
        scaled
        - jnp.mean(scaled, axis=-1, keepdims=True)
        - normed * jnp.mean(scaled * normed, axis=-1, keepdims=True)
    )
    return (inner_term * inv_spread, jnp.sum(grad_out * normed, axis=0))


def gelu_value(inputs):
    return 0.5 * inputs * (1.0 + lax.erf(inputs * (1.0 / math.sqrt(2.0))))


def gelu_slope(inputs):
    cumulative = 0.5 * (1.0 + lax.erf(inputs * (1.0 / math.sqrt(2.0))))
    return cumulative + inputs * jnp.exp(-0.5 * inputs * inputs) * (1.0 / math.sqrt(2.0 * math.pi))


def rotate(values, cos_table, sin_table):
    half_dim = values.shape[-1] // 2
    turned = jnp.concatenate([-values[..., half_dim:], values[..., :half_dim]], axis=-1)
    return values * cos_table + turned * sin_table


def unrotate(gradient, cos_table, sin_table):
    half_dim = gradient.shape[-1] // 2
    shifted = gradient * sin_table
    back_turn = jnp.concatenate([shifted[..., half_dim:], -shifted[..., :half_dim]], axis=-1)
    return gradient * cos_table + back_turn


def rope_tables(within):
    freq_index = jnp.arange(0, HEAD_DIM, 2, dtype=jnp.float32)
    inverse = 1.0 / jnp.power(ROPE_THETA, freq_index / HEAD_DIM)
    angles = within.astype(jnp.float32)[:, None] * inverse[None, :]
    angles = jnp.concatenate([angles, angles], axis=-1)
    return (jnp.cos(angles), jnp.sin(angles))


def doc_tables(lengths_row, pad_count, row_length):
    doc_order = jnp.arange(lengths_row.shape[0], dtype=jnp.int32)
    doc_ends = jnp.sum(
        jnp.where(doc_order[:, None] >= doc_order[None, :], lengths_row[None, :], 0), axis=1
    )
    starts = doc_ends - lengths_row
    places = jnp.arange(row_length, dtype=jnp.int32)
    segment = jnp.sum((places[:, None] >= doc_ends[None, :]).astype(jnp.int32), axis=1)
    doc_ids = jnp.arange(lengths_row.shape[0], dtype=jnp.int32)
    doc_begin = jnp.sum(jnp.where(segment[:, None] == doc_ids[None, :], starts[None, :], 0), axis=1)
    is_valid = places < row_length - pad_count
    return (segment, places - doc_begin, is_valid)


def apply_rows(activations, weight):
    return lax.dot_general(
        activations, weight, (((1,), (1,)), ((), ())), preferred_element_type=jnp.float32
    )


def outer_sum(grad_rows, act_rows):
    return lax.dot_general(
        grad_rows, act_rows, (((0,), (0,)), ((), ())), preferred_element_type=jnp.float32
    )


def sequence_body(
    tokens,
    cotangent,
    doc_lengths,
    pad_counts,
    w_in,
    w_ao,
    w_fo,
    norm_gains,
    gain_moment,
    gain_second,
    stat_l_in,
    stat_r_in,
    stat_l_ao,
    stat_r_ao,
    stat_l_fo,
    stat_r_fo,
    root_l_in,
    root_r_in,
    root_l_ao,
    root_r_ao,
    root_l_fo,
    root_r_fo,
):
    token_count, model_width = tokens.shape
    head_count = model_width // HEAD_DIM
    pair_count = head_count // 2
    pair_width = 2 * HEAD_DIM
    hidden_width = w_fo.shape[1]
    seq_count = lax.axis_size("seq")
    row_length = token_count * seq_count
    first_place = lax.axis_index("seq") * token_count
    segment, within, is_valid = doc_tables(doc_lengths[0], pad_counts[0], row_length)
    own_places = first_place + jnp.arange(token_count, dtype=jnp.int32)
    all_places = jnp.arange(row_length, dtype=jnp.int32)
    own_segment = lax.dynamic_slice_in_dim(segment, first_place, token_count)
    own_within = lax.dynamic_slice_in_dim(within, first_place, token_count)
    allowed = (own_segment[:, None] == segment[None, :]) & (
        is_valid[None, :] | (own_places[:, None] == all_places[None, :])
    )
    cos_table, sin_table = rope_tables(own_within)
    cos_table = cos_table[:, None, :]
    sin_table = sin_table[:, None, :]
    low_weights = (
        w_in.astype(jnp.bfloat16),
        w_ao.astype(jnp.bfloat16),
        w_fo.astype(jnp.bfloat16),
        norm_gains.astype(jnp.bfloat16),
    )
    full_in, full_ao, full_fo, full_gains = (
        lax.all_gather(low_weights[0], ("dp", "seq"), axis=1, tiled=True),
        lax.all_gather(low_weights[1], ("dp", "seq"), axis=0, tiled=True),
        lax.all_gather(low_weights[2], ("dp", "seq"), axis=0, tiled=True),
        lax.all_gather(low_weights[3], ("dp", "seq"), axis=1, tiled=True),
    )
    gain_rows = full_gains.astype(jnp.float32)
    inputs = tokens.astype(jnp.float32)
    normed_one, spread_one = norm_forward(inputs)
    attn_in = (normed_one * gain_rows[0]).astype(jnp.bfloat16)
    qkv_raw = apply_rows(attn_in, full_in[0])
    query_low = (
        rotate(
            qkv_raw[:, :model_width].reshape(token_count, head_count, HEAD_DIM),
            cos_table,
            sin_table,
        )
        .reshape(token_count, model_width)
        .astype(jnp.bfloat16)
    )
    key_low = (
        rotate(
            qkv_raw[:, model_width : 2 * model_width].reshape(token_count, head_count, HEAD_DIM),
            cos_table,
            sin_table,
        )
        .reshape(token_count, model_width)
        .astype(jnp.bfloat16)
    )
    value_low = qkv_raw[:, 2 * model_width :].astype(jnp.bfloat16)
    keys_all, values_all = (
        lax.all_gather(key_low, "seq", axis=0, tiled=True),
        lax.all_gather(value_low, "seq", axis=0, tiled=True),
    )

    def pair_slice(matrix, pair_index):
        return lax.dynamic_slice_in_dim(matrix, pair_index * pair_width, pair_width, 1).reshape(
            matrix.shape[0], 2, HEAD_DIM
        )

    def pair_scores(query_pair, key_pair, allow_mask):
        raw_scores = (
            jnp.einsum("thd,khd->htk", query_pair, key_pair, preferred_element_type=jnp.float32)
            * SCORE_SCALE
        )
        return jnp.where(allow_mask[None], raw_scores, MASK_FILL)

    def forward_pair(loop_carry, pair_index):
        scores = pair_scores(
            pair_slice(query_low, pair_index), pair_slice(keys_all, pair_index), allowed
        )
        row_max = jnp.max(scores, axis=-1, keepdims=True)
        exponent = jnp.exp(scores - row_max)
        row_sum = jnp.sum(exponent, axis=-1, keepdims=True)
        weights_low = (exponent / row_sum).astype(jnp.bfloat16)
        attended = jnp.einsum(
            "htk,khd->thd",
            weights_low,
            pair_slice(values_all, pair_index),
            preferred_element_type=jnp.float32,
        )
        return (
            loop_carry,
            (attended.reshape(token_count, pair_width), (row_max + jnp.log(row_sum))[..., 0]),
        )

    unused, (attended_pairs, log_norms) = lax.scan(forward_pair, 0, jnp.arange(pair_count))
    attn_low = (
        jnp.transpose(attended_pairs, (1, 0, 2))
        .reshape(token_count, model_width)
        .astype(jnp.bfloat16)
    )
    residual = inputs + apply_rows(attn_low, full_ao)
    normed_two, spread_two = norm_forward(residual)
    ffn_in = (normed_two * gain_rows[1]).astype(jnp.bfloat16)
    projected = apply_rows(ffn_in, full_in[1])
    inner_part = projected[:, :hidden_width]
    gate_part = projected[:, hidden_width:]
    activated = gelu_value(inner_part)
    mid_low = (activated * gate_part).astype(jnp.bfloat16)
    layer_out = (residual + apply_rows(mid_low, full_fo)).astype(jnp.bfloat16)
    back_in, back_ao, back_fo, back_gains = (
        lax.all_gather(low_weights[0], ("dp", "seq"), axis=1, tiled=True),
        lax.all_gather(low_weights[1], ("dp", "seq"), axis=0, tiled=True),
        lax.all_gather(low_weights[2], ("dp", "seq"), axis=0, tiled=True),
        lax.all_gather(low_weights[3], ("dp", "seq"), axis=1, tiled=True),
    )
    back_rows = back_gains.astype(jnp.float32)
    grad_fo_w = outer_sum(cotangent, mid_low)
    grad_mid = jnp.dot(cotangent, back_fo, preferred_element_type=jnp.float32)
    grad_proj = jnp.concatenate(
        [grad_mid * gate_part * gelu_slope(inner_part), grad_mid * activated], axis=1
    ).astype(jnp.bfloat16)
    grad_ffn_w = outer_sum(grad_proj, ffn_in)
    grad_ffn_in = jnp.dot(grad_proj, back_in[1], preferred_element_type=jnp.float32)
    grad_norm_two, grad_gain_two = norm_backward(grad_ffn_in, normed_two, spread_two, back_rows[1])
    grad_resid = cotangent.astype(jnp.float32) + grad_norm_two
    grad_out_attn = grad_resid.astype(jnp.bfloat16)
    grad_ao_w = outer_sum(grad_out_attn, attn_low)
    grad_attn = jnp.dot(grad_out_attn, back_ao, preferred_element_type=jnp.float32).astype(
        jnp.bfloat16
    )

    def query_side_grads(pair_index):
        query_pair = pair_slice(query_low, pair_index)
        key_pair = pair_slice(keys_all, pair_index)
        value_pair = pair_slice(values_all, pair_index)
        grad_pair = pair_slice(grad_attn, pair_index)
        scores = pair_scores(query_pair, key_pair, allowed)
        softmax_out = jnp.exp(scores - log_norms[pair_index][..., None])
        grad_weights = jnp.einsum(
            "thd,khd->htk", grad_pair, value_pair, preferred_element_type=jnp.float32
        )
        delta_row = jnp.sum(softmax_out * grad_weights, axis=-1, keepdims=True)
        grad_scores = (softmax_out * (grad_weights - delta_row)).astype(jnp.bfloat16)
        grad_query = (
            jnp.einsum("htk,khd->thd", grad_scores, key_pair, preferred_element_type=jnp.float32)
            * SCORE_SCALE
        )
        return (query_pair, grad_pair, softmax_out, grad_scores, grad_query, delta_row)

    def backward_pair(loop_carry, pair_index):
        query_pair, grad_pair, softmax_out, grad_scores, grad_query, delta_row = query_side_grads(
            pair_index
        )
        grad_key = (
            jnp.einsum("htk,thd->khd", grad_scores, query_pair, preferred_element_type=jnp.float32)
            * SCORE_SCALE
        )
        grad_value = jnp.einsum(
            "htk,thd->khd",
            softmax_out.astype(jnp.bfloat16),
            grad_pair,
            preferred_element_type=jnp.float32,
        )
        return (
            loop_carry,
            (
                grad_query.reshape(token_count, pair_width),
                grad_key.reshape(row_length, pair_width),
                grad_value.reshape(row_length, pair_width),
            ),
        )

    unused, (grad_query_pairs, grad_key_parts, grad_value_parts) = lax.scan(
        backward_pair, 0, jnp.arange(pair_count)
    )
    grad_key_pairs, grad_value_pairs = (
        lax.psum_scatter(
            grad_key_parts.astype(jnp.bfloat16), "seq", scatter_dimension=1, tiled=True
        ).astype(jnp.float32),
        lax.psum_scatter(
            grad_value_parts.astype(jnp.bfloat16), "seq", scatter_dimension=1, tiled=True
        ).astype(jnp.float32),
    )

    def heads_of(pairs_array):
        return jnp.transpose(pairs_array, (1, 0, 2)).reshape(token_count, head_count, HEAD_DIM)

    grad_qkv = jnp.concatenate(
        [
            unrotate(heads_of(grad_query_pairs), cos_table, sin_table).reshape(
                token_count, model_width
            ),
            unrotate(heads_of(grad_key_pairs), cos_table, sin_table).reshape(
                token_count, model_width
            ),
            heads_of(grad_value_pairs).reshape(token_count, model_width),
        ],
        axis=1,
    ).astype(jnp.bfloat16)
    grad_qkv_w = outer_sum(grad_qkv, attn_in)
    grad_attn_in = jnp.dot(grad_qkv, back_in[0], preferred_element_type=jnp.float32)
    grad_norm_one, grad_gain_one = norm_backward(grad_attn_in, normed_one, spread_one, back_rows[0])
    grad_input = grad_resid + grad_norm_one
    w_terms = jnp.stack([grad_qkv_w, grad_ffn_w])
    gain_terms = jnp.stack([grad_gain_one, grad_gain_two])
    summed_in, summed_ao, summed_fo, summed_gains = (
        lax.psum_scatter(w_terms, ("dp", "seq"), scatter_dimension=1, tiled=True),
        lax.psum_scatter(grad_ao_w, ("dp", "seq"), scatter_dimension=0, tiled=True),
        lax.psum_scatter(grad_fo_w, ("dp", "seq"), scatter_dimension=0, tiled=True),
        lax.psum_scatter(gain_terms, ("dp", "seq"), scatter_dimension=1, tiled=True),
    )
    new_moment = 0.9 * gain_moment + 0.1 * summed_gains
    new_second = 0.999 * gain_second + 0.001 * summed_gains * summed_gains
    new_gains = norm_gains - ADAM_RATE * new_moment / (jnp.sqrt(new_second) + 1e-08)
    whole_in, whole_ao, whole_fo = (
        lax.all_gather(summed_in.astype(jnp.bfloat16), ("dp", "seq"), axis=1, tiled=True).astype(
            summed_in.dtype
        ),
        lax.all_gather(summed_ao.astype(jnp.bfloat16), ("dp", "seq"), axis=0, tiled=True).astype(
            summed_ao.dtype
        ),
        lax.all_gather(summed_fo.astype(jnp.bfloat16), ("dp", "seq"), axis=0, tiled=True).astype(
            summed_fo.dtype
        ),
    )
    dev_index = lax.axis_index(("dp", "seq"))

    def refresh(grad_shard, grad_full, stat_left, stat_right, root_right):
        col_count = stat_right.shape[1]
        new_left = 0.5 * stat_left + 0.5 * jnp.einsum(
            "arn,amn->arm", grad_shard, grad_full, precision=HIGHEST
        )
        full_cols = lax.dynamic_slice_in_dim(grad_full, dev_index * col_count, col_count, 2)
        new_right = 0.5 * stat_right + 0.5 * jnp.einsum(
            "amc,amn->acn", full_cols, grad_full, precision=HIGHEST
        )
        applied = jnp.einsum("amn,acn->amc", grad_full, root_right, precision=HIGHEST)
        return (new_left, new_right, applied)

    left_in, right_in, applied_in = refresh(summed_in, whole_in, stat_l_in, stat_r_in, root_r_in)
    left_ao, right_ao, applied_ao = refresh(
        summed_ao[None], whole_ao[None], stat_l_ao[None], stat_r_ao[None], root_r_ao[None]
    )
    left_fo, right_fo, applied_fo = refresh(
        summed_fo[None], whole_fo[None], stat_l_fo[None], stat_r_fo[None], root_r_fo[None]
    )
    product_in, product_ao, product_fo = (
        lax.all_gather(applied_in.astype(jnp.bfloat16), ("dp", "seq"), axis=2, tiled=True).astype(
            applied_in.dtype
        ),
        lax.all_gather(applied_ao.astype(jnp.bfloat16), ("dp", "seq"), axis=2, tiled=True).astype(
            applied_ao.dtype
        ),
        lax.all_gather(applied_fo.astype(jnp.bfloat16), ("dp", "seq"), axis=2, tiled=True).astype(
            applied_fo.dtype
        ),
    )
    new_w_in = w_in - SHAMPOO_RATE * jnp.einsum(
        "arm,amn->arn", root_l_in, product_in, precision=HIGHEST
    )
    new_w_ao = (
        w_ao
        - SHAMPOO_RATE
        * jnp.einsum("arm,amn->arn", root_l_ao[None], product_ao, precision=HIGHEST)[0]
    )
    new_w_fo = (
        w_fo
        - SHAMPOO_RATE
        * jnp.einsum("arm,amn->arn", root_l_fo[None], product_fo, precision=HIGHEST)[0]
    )
    return (
        layer_out,
        grad_input,
        summed_in,
        summed_ao,
        summed_fo,
        summed_gains,
        new_moment,
        new_second,
        new_gains,
        left_in,
        right_in,
        left_ao[0],
        right_ao[0],
        left_fo[0],
        right_fo[0],
        new_w_in,
        new_w_ao,
        new_w_fo,
    )


QUERY_TILE = 480
ROW_ALIGN = 16
KEY_STEP = 512
KEY_ALIGN = 128
PREP_TILE = 480
LANES = 128
REFRESH_ROWS = 768
ROOT_SPLIT = 640
MASK_BIT = -(2.0**100)
NO_MAX = -3e38
BF16 = jnp.bfloat16
F32 = jnp.float32
VMEM_BYTES = 56 * 2**20


def dot_rows(left, right):
    return lax.dot_general(left, right, (((1,), (1,)), ((), ())), preferred_element_type=F32)


def dot_plain(left, right):
    return lax.dot_general(left, right, (((1,), (0,)), ((), ())), preferred_element_type=F32)


def dot_first(left, right):
    return lax.dot_general(left, right, (((0,), (0,)), ((), ())), preferred_element_type=F32)


def lane_index(rows):
    return lax.broadcasted_iota(jnp.int32, (rows, LANES), 1)


def three_pieces(column):
    first = column.astype(BF16).astype(F32)
    second = (column - first).astype(BF16).astype(F32)
    return first, second, column - first - second


def with_pieces(values, column, lane, at):
    one, two, three = three_pieces(column)
    return jnp.where(
        lane == at, one, jnp.where(lane == at + 1, two, jnp.where(lane == at + 2, three, values))
    ).astype(BF16)


def project_kernel(
    tokens, weight, gain, cosine, sine, query_mask, key_mask, attn_in, query, key, value
):
    step = pl.program_id(0)
    last = pl.num_programs(0) - 1
    own_heads = query.shape[0]
    rows = tokens.shape[0]
    lane = lane_index(rows)
    low_lanes = lane < HEAD_DIM

    @pl.when(step < last)
    def compute():
        normed = norm_forward(tokens[...].astype(F32))[0]
        low = (normed * gain[...]).astype(BF16)
        attn_in[...] = low
        raw = dot_rows(low, weight[...])
        first_half = lane % HEAD_DIM < HEAD_DIM // 2
        ones = jnp.where(lane < HEAD_DIM + 3, 1.0, 0.0)
        for head in range(own_heads):
            both = raw[:, head * LANES : (head + 1) * LANES]
            turned = jnp.where(
                first_half,
                -pltpu.roll(both, LANES - HEAD_DIM // 2, 1),
                pltpu.roll(both, HEAD_DIM // 2, 1),
            )
            both = both * cosine[...] + turned * sine[...]
            query[head] = jnp.where(
                low_lanes, both * SCORE_SCALE, query_mask[...].astype(F32)
            ).astype(BF16)
            key[head] = jnp.where(
                low_lanes, pltpu.roll(both, HEAD_DIM, 1), key_mask[...].astype(F32)
            ).astype(BF16)
            at = own_heads + head // 2
            pair = raw[:, at * LANES : (at + 1) * LANES]
            if head % 2:
                pair = pltpu.roll(pair, HEAD_DIM, 1)
            value[head] = jnp.where(low_lanes, pair, ones).astype(BF16)

    @pl.when(step == last)
    def pad():
        blocked = jnp.where(
            low_lanes,
            0.0,
            jnp.where(lane < HEAD_DIM + 8, MASK_BIT, jnp.where(lane < HEAD_DIM + 11, 1.0, 0.0)),
        ).astype(BF16)
        for head in range(own_heads):
            key[head] = blocked
            value[head] = jnp.zeros((rows, LANES), BF16)


def attend_kernel(
    start_at, step_count, pad_from, query, key, value, pair_out, extra_out, query_out
):
    tile = pl.program_id(0)
    own_heads, rows, _ = query.shape
    lane = lane_index(rows)
    low_lanes = lane < HEAD_DIM
    place = tile * rows + lax.broadcasted_iota(jnp.int32, (rows, 1), 0)
    padded = place >= pad_from[0]
    own_rows = pl.ds(pl.multiple_of(tile * rows, ROW_ALIGN), rows)
    maxima, totals = [], []
    for head in range(own_heads):
        products = query[head].astype(F32) * key[head, own_rows, :].astype(F32)
        self_score = jnp.sum(jnp.where(low_lanes, products, 0.0), axis=1, keepdims=True)
        maxima.append(jnp.where(padded, self_score, NO_MAX))
        totals.append(jnp.where(padded, value[head, own_rows, :].astype(F32), 0.0))
    first = start_at[tile] * KEY_ALIGN

    def step(index, carry):
        maxima, totals = carry
        at = pl.ds(pl.multiple_of(first + index * KEY_STEP, KEY_ALIGN), KEY_STEP)
        new_maxima, new_totals = [], []
        for head in range(own_heads):
            scores = dot_rows(query[head], key[head, at, :])
            row_max = jnp.maximum(maxima[head], jnp.max(scores, axis=1, keepdims=True))
            weights = jnp.exp(scores - row_max).astype(BF16)
            new_totals.append(
                totals[head] * jnp.exp(maxima[head] - row_max)
                + dot_plain(weights, value[head, at, :])
            )
            new_maxima.append(row_max)
        return new_maxima, new_totals

    maxima, totals = lax.fori_loop(0, step_count[tile], step, (maxima, totals))
    outs = []
    for head in range(own_heads):
        row_sum = totals[head][:, HEAD_DIM : HEAD_DIM + 1]
        outs.append(jnp.where(low_lanes, totals[head] * (1.0 / row_sum), 0.0))
        query_out[head] = with_pieces(
            query[head].astype(F32), -(maxima[head] + jnp.log(row_sum)), lane, HEAD_DIM + 8
        )
    pair_out[...] = (outs[0] + pltpu.roll(outs[1], HEAD_DIM, 1)).astype(BF16)
    extra_out[...] = outs[2].astype(BF16)


def attend_back_kernel(
    start_at,
    step_count,
    pad_from,
    query,
    pair_out,
    extra_out,
    grad_pair,
    grad_extra,
    key,
    value,
    cosine,
    sine,
    grads,
    grad_query,
    grad_key,
    grad_value,
):
    tile = pl.program_id(0)
    own_heads, rows, _ = query.shape
    tile_count = grad_query.shape[1] // rows

    @pl.when(tile == 0)
    def clear():
        grad_key[...] = jnp.zeros_like(grad_key)
        grad_value[...] = jnp.zeros_like(grad_value)

    @pl.when(tile < tile_count)
    def accumulate():
        lane = lane_index(rows)
        low_lanes = lane < HEAD_DIM
        own_rows = pl.ds(pl.multiple_of(tile * rows, ROW_ALIGN), rows)
        first = start_at[tile] * KEY_ALIGN
        pair = grad_pair[...].astype(F32)
        extra = grad_extra[...].astype(F32)
        pair_product = pair * pair_out[...].astype(F32)
        products = [
            jnp.where(low_lanes, pair_product, 0.0),
            jnp.where(low_lanes, 0.0, pair_product),
            extra * extra_out[...].astype(F32),
        ]
        incoming = [pair, pltpu.roll(pair, HEAD_DIM, 1), extra]
        grads_out = []
        for head in range(own_heads):
            own = jnp.where(low_lanes, incoming[head], 0.0)
            delta = jnp.sum(products[head], axis=1, keepdims=True)
            grads_out.append(with_pieces(own, -delta, lane, HEAD_DIM))

        def step(index, carry):
            at = pl.ds(pl.multiple_of(first + index * KEY_STEP, KEY_ALIGN), KEY_STEP)
            sums = []
            for head in range(own_heads):
                keys = key[head, at, :]
                probs = jnp.exp(dot_rows(keys, query[head]))
                grad_scores = (probs * dot_rows(value[head, at, :], grads_out[head])).astype(BF16)
                grad_value[head, at, :] += dot_plain(probs.astype(BF16), grads_out[head])
                grad_key[head, at, :] += dot_plain(grad_scores, query[head])
                sums.append(carry[head] + dot_first(grad_scores, keys))
            return sums

        zeros = [jnp.zeros((rows, LANES), F32) for _ in range(own_heads)]
        sums = lax.fori_loop(0, step_count[tile], step, zeros)
        for head in range(own_heads):
            grad_query[head, own_rows, :] = sums[head]

        @pl.when((tile + 1) * rows > pad_from[0])
        def self_terms():
            place = tile * rows + lax.broadcasted_iota(jnp.int32, (rows, 1), 0)
            padded = place >= pad_from[0]
            for head in range(own_heads):
                keys = key[head, own_rows, :].astype(F32)
                queries = query[head].astype(F32)
                outs = grads_out[head].astype(F32)
                counted = low_lanes | (lane >= HEAD_DIM + 8)
                score = jnp.sum(jnp.where(counted, queries * keys, 0.0), axis=1, keepdims=True)
                prob = jnp.where(padded, jnp.exp(jnp.where(padded, score, 0.0)), 0.0)
                grad_prob = jnp.sum(
                    outs * value[head, own_rows, :].astype(F32), axis=1, keepdims=True
                )
                grad_score = (prob * grad_prob).astype(BF16).astype(F32)
                low_prob = prob.astype(BF16).astype(F32)
                grad_query[head, own_rows, :] += grad_score * jnp.where(low_lanes, keys, 0.0)
                grad_key[head, own_rows, :] += grad_score * queries
                grad_value[head, own_rows, :] += low_prob * outs

    @pl.when(tile >= tile_count)
    def finish():
        size = grads.shape[0]
        at = pl.ds(pl.multiple_of((tile - tile_count) * size, ROW_ALIGN), size)
        lane = lane_index(size)
        low_lanes = lane < HEAD_DIM
        first_half = lane % HEAD_DIM < HEAD_DIM // 2
        values, turns = [], []
        for head in range(own_heads):
            both = jnp.where(
                low_lanes,
                grad_query[head, at, :] * SCORE_SCALE,
                pltpu.roll(grad_key[head, at, :], HEAD_DIM, 1),
            )
            shifted = both * sine[...]
            turned = jnp.where(
                first_half,
                pltpu.roll(shifted, LANES - HEAD_DIM // 2, 1),
                -pltpu.roll(shifted, HEAD_DIM // 2, 1),
            )
            turns.append(both * cosine[...] + turned)
            values.append(jnp.where(low_lanes, grad_value[head, at, :], 0.0))
        swapped = pltpu.roll(turns[1], HEAD_DIM, 1)
        grads[:, :LANES] = jnp.where(low_lanes, turns[0], swapped).astype(BF16)
        grads[:, LANES : 2 * LANES] = jnp.where(low_lanes, turns[2], turns[0]).astype(BF16)
        grads[:, 2 * LANES : 3 * LANES] = jnp.where(low_lanes, swapped, turns[2]).astype(BF16)
        base = own_heads * LANES
        grads[:, base : base + LANES] = (values[0] + pltpu.roll(values[1], HEAD_DIM, 1)).astype(
            BF16
        )
        grads[:, base + LANES : base + 2 * LANES] = values[2].astype(BF16)


def refresh_kernel(
    full, own, select, stat_left, stat_right, root_left, right_root, weight, *refs, kept, own_at, root_at
):
    new_left, new_right, new_weight, columns, total = refs[kept:]
    step = pl.program_id(0)
    chosen = select.shape[0]
    count = new_right.shape[-2]
    own_rows = own[:, own_at : own_at + full.shape[1]]
    outer = dot_rows(jnp.concatenate([select[...], own_rows]), full[...])
    columns[...] = outer[:chosen]
    new_left[0] = 0.5 * stat_left[0] + 0.5 * outer[chosen:]
    left = jnp.concatenate([outer[:chosen].astype(BF16), root_left[0].astype(BF16)])
    product = dot_plain(left, full[...])

    @pl.when(step == 0)
    def begin():
        total[...] = product

    @pl.when(step > 0)
    def add():
        total[...] += product

    @pl.when(step == pl.num_programs(0) - 1)
    def finish():
        new_right[0] = 0.5 * stat_right[0] + 0.5 * total[:count, :]
        product = total[chosen:, :].astype(BF16)
        if root_at is None:
            new_weight[0] = weight[0] - SHAMPOO_RATE * dot_plain(product, right_root[...])
        else:
            size = product.shape[1]
            rest = root_at + size
            new_weight[0] = dot_rows(product, right_root[:, root_at:rest])
            new_weight[1] = dot_rows(
                product[:, :ROOT_SPLIT], right_root[:, rest : rest + ROOT_SPLIT]
            )
            new_weight[2] = dot_rows(
                product[:, ROOT_SPLIT:], right_root[:, rest : rest + size - ROOT_SPLIT]
            )


def refresh(
    at, full, own, own_at, select, stat_left, stat_right, root_left, roots, root_at, weight, previous
):
    in_dim, out_dim = full.shape
    chunk = REFRESH_ROWS
    rows, count, chosen = own.shape[0], stat_right.shape[1], select.shape[0]

    def by_chunk(rows):
        return pl.BlockSpec((1, rows, chunk), lambda i: (at, 0, i))

    def whole(*shape):
        return pl.BlockSpec(shape, lambda i: (0,) * len(shape))

    def stacked(array):
        return pl.BlockSpec((1,) + array.shape[1:], lambda i: (at, 0, 0))

    kept = [pl.BlockSpec(memory_space=pl.ANY)] * len(previous)
    square = root_at >= 0
    if square:
        new_weight = stacked(weight), weight.shape
        root_block = pl.BlockSpec((out_dim, out_dim), lambda i: (0, root_at))
    else:
        parts = (3, rows, roots.shape[0])
        new_weight = whole(*parts), parts
        root_block = whole(*roots.shape)
    return pl.pallas_call(
        functools.partial(
            refresh_kernel,
            kept=len(previous),
            own_at=own_at,
            root_at=None if square else -root_at,
        ),
        grid=(in_dim // chunk,),
        in_specs=[
            pl.BlockSpec((chunk, out_dim), lambda i: (i, 0)),
            whole(*own.shape),
            whole(*select.shape),
            by_chunk(rows),
            stacked(stat_right),
            by_chunk(rows),
            root_block,
            stacked(weight),
        ]
        + kept,
        out_specs=[
            by_chunk(rows),
            stacked(stat_right),
            new_weight[0],
            pl.BlockSpec((chosen, chunk), lambda i: (0, i)),
        ],
        out_shape=[
            jax.ShapeDtypeStruct(stat_left.shape, F32),
            jax.ShapeDtypeStruct(stat_right.shape, F32),
            jax.ShapeDtypeStruct(new_weight[1], F32),
            jax.ShapeDtypeStruct((chosen, in_dim), F32),
        ],
        scratch_shapes=[pltpu.VMEM((chosen + rows, out_dim), F32)],
        input_output_aliases={8 + i: i for i in range(len(previous))},
        compiler_params=pltpu.CompilerParams(vmem_limit_bytes=VMEM_BYTES),
        cost_estimate=pl.CostEstimate(
            flops=4 * (chosen + rows) * in_dim * out_dim,
            bytes_accessed=2 * in_dim * out_dim + 12 * rows * in_dim + 2 * out_dim * out_dim,
            transcendentals=0,
        ),
        name="refresh",
    )(
        full,
        own,
        select,
        stat_left,
        stat_right,
        root_left,
        roots,
        weight,
        *previous,
    )


def exchange(values, axis, offset):
    size = lax.axis_size(axis)
    return lax.ppermute(values, axis, [(i, i ^ offset) for i in range(size)])


def arrange_kernel(own_at, *refs, count, moves):
    blocks, outs, sems = refs[:count], refs[count:-1], refs[-1]
    copies = []
    for index, (number, offset, source, which, target) in enumerate(moves):
        place = own_at[0] ^ offset
        start = blocks[number].at[source] if source else blocks[number]
        end = outs[which].at[tuple(place if at == "place" else at for at in target)]
        copies.append(pltpu.make_async_copy(start, end, sems.at[index]))
    for copy in copies:
        copy.start()
    for copy in copies:
        copy.wait()


def arrange(blocks, own_at, shapes, moves):
    count = len(blocks)
    return pl.pallas_call(
        functools.partial(arrange_kernel, count=count, moves=moves),
        in_specs=[pl.BlockSpec(memory_space=pltpu.SMEM)]
        + [pl.BlockSpec(memory_space=pl.ANY)] * count,
        out_specs=[pl.BlockSpec(memory_space=pltpu.VMEM)] * len(shapes),
        scratch_shapes=[pltpu.SemaphoreType.DMA((len(moves),))],
        out_shape=[jax.ShapeDtypeStruct(shape, blocks[0].dtype) for shape in shapes],
        compiler_params=pltpu.CompilerParams(vmem_limit_bytes=VMEM_BYTES),
        cost_estimate=pl.CostEstimate(
            flops=0, bytes_accessed=2 * count * blocks[0].size * 2, transcendentals=0
        ),
        name="arrange",
    )(own_at[None], *blocks)


def terms_kernel(
    core, grad_proj, ffn_in, grad_out, attended, cotangent, middle, send, keep
):
    step = pl.program_id(0)
    groups, rows, _ = send.shape
    width = ffn_in.shape[1]
    chunk = 2 * groups * rows
    pieces = [(grad_proj, part * width, ffn_in) for part in range(grad_proj.shape[1] // width)]
    pieces += [(grad_out, 0, attended), (cotangent, 0, middle)]
    first = 0
    for left, offset, right in pieces:
        columns = pl.ds(pl.multiple_of(offset + step * chunk, KEY_ALIGN), chunk)
        term = dot_first(left[:, columns], right[...]).astype(BF16)
        last = first + right.shape[1]
        for own in range(2):

            @pl.when(core[0] == own)
            def store():
                for group in range(groups):
                    for side, out in ((own, keep), (1 - own, send)):
                        at = (2 * group + side) * rows
                        out[group, :, first:last] = term[at : at + rows]

        first = last


def gather_plane(values, by_steps=False):
    last = None if by_steps else exchange(values, "seq", 3)
    far = exchange(values, "seq", 2)
    last = exchange(far, "seq", 1) if by_steps else last
    blocks = [values, exchange(values, "seq", 1), far, last]
    shape = (len(blocks),) + values.shape
    moves = [(k, k, (), 0, ("place",)) for k in range(len(blocks))]
    return arrange(blocks, lax.axis_index("seq"), [shape], moves)[0]


def gather_near(plane):
    half = plane.shape[0] // 2
    left, right = plane[:half], plane[half:]
    left_two, right_four = exchange(left, "dp", 2), exchange(right, "dp", 4)
    return [left, right, left_two, exchange(right, "dp", 2), exchange(left, "dp", 4), right_four]


def gather_far(near):
    return [*near, exchange(near[2], "dp", 4), exchange(near[5], "dp", 2)]


def gather_partners(plane):
    return gather_far(gather_near(plane))


def gather_cores(even):
    blocks = []
    for k in range(0, len(even), 2):
        blocks += [*even[k : k + 2], *(exchange(block, "dp", 1) for block in even[k : k + 2])]
    return blocks


def half_moves(blocks, cuts):
    half = blocks[0].shape[0]
    moves = []
    for number in range(len(blocks)):
        rows = slice(number % 2 * half, (number % 2 + 1) * half)
        for source, which, target in cuts:
            end = tuple(rows if at == "half" else at for at in target)
            moves.append((number, number // 2, source, which, end))
    return moves


def column_moves(blocks, widths):
    shapes, cuts, first = [], [], 0
    half, rows, _ = blocks[0].shape
    for which, width in enumerate(widths):
        shapes.append((len(blocks) // 2, 2 * half, rows, width))
        source = (slice(None), slice(None), slice(first, first + width))
        cuts.append((source, which, ("place", "half")))
        first += width
    return shapes, half_moves(blocks, cuts)


def fence(*values):
    return lax.optimization_barrier(values)


def add_blocks(blocks):
    total = blocks[0].astype(F32)
    for block in blocks[1:]:
        total = total + block.astype(F32)
    return total


def pair_sums(send, keep, axis=0):
    came = exchange(send, "dp", 1)
    own_at = lax.axis_index("dp") >> 1
    return [
        add_blocks(
            [
                lax.dynamic_index_in_dim(side, own_at ^ k, axis, keepdims=False)
                for side in (keep, came)
            ]
        )
        for k in range(keep.shape[axis])
    ]


def swap_blocks(blocks, axis, unit):
    came = [exchange(blocks[k], axis, k * unit) for k in range(len(blocks) - 1, 0, -1)]
    return [blocks[0]] + came[::-1]


def add_partners(blocks, axis, unit):
    return add_blocks(swap_blocks(blocks, axis, unit))


def lows(blocks):
    return [block.astype(BF16) for block in blocks]


def by_distance(values, axis):
    own_at = lax.axis_index(axis)
    return [
        lax.dynamic_index_in_dim(values, own_at ^ k, 0, keepdims=False)
        for k in range(values.shape[0])
    ]


def head_body(
    tokens,
    cotangent,
    doc_lengths,
    pad_counts,
    w_in,
    w_ao,
    w_fo,
    norm_gains,
    gain_moment,
    gain_second,
    stat_l_in,
    stat_r_in,
    stat_l_ao,
    stat_r_ao,
    stat_l_fo,
    stat_r_fo,
    root_l_in,
    root_r_in,
    root_l_ao,
    root_r_ao,
    root_l_fo,
    root_r_fo,
):
    token_count, width = tokens.shape
    hidden = w_fo.shape[1]
    seq_count, dp_count = lax.axis_size("seq"), lax.axis_size("dp")
    all_count = seq_count * dp_count
    row_length = token_count * seq_count
    seq_at = lax.axis_index("seq")
    dev_at = lax.axis_index(("dp", "seq"))
    head_count = width // HEAD_DIM
    own_heads = head_count // seq_count
    own_width = own_heads * HEAD_DIM
    in_rows = w_in.shape[1]
    ao_rows = w_ao.shape[0]
    gain_cols = norm_gains.shape[1]

    gain_lanes = jnp.zeros((in_rows, LANES), BF16).at[:2, :gain_cols].set(norm_gains.astype(BF16))
    up_parts = in_rows // ao_rows
    row_tokens = lax.all_gather(tokens, "seq", axis=0, tiled=True)
    qkv_blocks = gather_cores(
        gather_partners(gather_plane(jnp.concatenate([w_in[0].astype(BF16), gain_lanes], axis=1)))
    )
    full_qkv, gain_blocks = arrange(
        qkv_blocks, lax.axis_index("dp"), *column_moves(qkv_blocks, [width, LANES])
    )
    full_qkv = full_qkv.reshape(all_count * in_rows, width)
    gain_rows = (
        jnp.transpose(gain_blocks[:, :, :2, :gain_cols], (2, 0, 1, 3)).reshape(2, width).astype(F32)
    )
    full_up = lax.all_gather(w_in[1].astype(BF16), ("dp", "seq"), axis=0, tiled=True)
    out_weights = jnp.concatenate([w_ao.astype(BF16), w_fo.astype(BF16)], axis=1)
    row_tokens, out_weights = fence(row_tokens, out_weights)
    out_plane = gather_plane(out_weights)
    root_rows = stat_r_in.shape[1]
    fo_rest = root_r_fo.shape[0] - root_rows
    rest_rows = root_r_fo[root_rows:].astype(BF16)
    wrapped = jnp.concatenate(
        [
            rest_rows[:, :ROOT_SPLIT],
            jnp.pad(rest_rows[:, ROOT_SPLIT:], ((0, 0), (0, 2 * ROOT_SPLIT - hidden))),
        ]
    )
    roots = jnp.concatenate(
        [
            root_r_in[0].astype(BF16),
            root_r_in[1].astype(BF16),
            root_r_ao.astype(BF16),
            root_r_fo[:root_rows].astype(BF16),
            wrapped,
        ],
        axis=1,
    )

    lengths = doc_lengths[0]
    segment, within, is_valid = doc_tables(lengths, pad_counts[0], row_length)
    pad_from = row_length - pad_counts[0]
    doc_ids = jnp.arange(lengths.shape[0], dtype=jnp.int32)
    places = jnp.arange(row_length, dtype=jnp.int32)
    doc_begin = places - within
    doc_end = doc_begin + jnp.sum(
        jnp.where(segment[:, None] == doc_ids[None, :], lengths[None, :], 0), axis=1
    )
    freq_index = jnp.arange(0, HEAD_DIM, 2, dtype=F32)
    inverse = 1.0 / jnp.power(ROPE_THETA, freq_index / HEAD_DIM)
    angles = within.astype(F32)[:, None] * inverse[None, :]
    copies = LANES // (HEAD_DIM // 2)
    cos_table = jnp.concatenate([jnp.cos(angles)] * copies, axis=1)
    sin_table = jnp.concatenate([jnp.sin(angles)] * copies, axis=1)
    lane = jnp.arange(LANES, dtype=jnp.int32)
    in_doc = lane[None, :] - HEAD_DIM == segment[:, None]
    mask_lanes = (lane >= HEAD_DIM) & (lane < HEAD_DIM + 8)
    one_lanes = (lane >= HEAD_DIM + 8) & (lane < HEAD_DIM + 11)
    query_mask = in_doc.astype(BF16)
    key_mask = jnp.where(
        mask_lanes[None, :] & ~(in_doc & is_valid[:, None]),
        MASK_BIT,
        jnp.where(one_lanes[None, :], 1.0, 0.0),
    ).astype(BF16)
    tile_starts = doc_begin[::QUERY_TILE] // KEY_ALIGN
    tile_ends = jnp.minimum(doc_end[QUERY_TILE - 1 :: QUERY_TILE], pad_from)
    tile_steps = jnp.maximum(-((tile_starts * KEY_ALIGN - tile_ends) // KEY_STEP), 0)
    tile_count = row_length // QUERY_TILE
    pad_at = pad_from[None]

    qkv_heads = lax.dynamic_slice_in_dim(
        full_qkv.reshape(3, head_count, HEAD_DIM, width), seq_at * own_heads, own_heads, 1
    )
    own_weight = jnp.concatenate(
        [
            jnp.transpose(qkv_heads[:2], (1, 0, 2, 3)).reshape(2 * own_width, width),
            qkv_heads[2].reshape(own_width, width),
            jnp.zeros((HEAD_DIM, width), BF16),
        ]
    )
    back_weight = jnp.concatenate(
        [qkv_heads.reshape(3 * own_width, width), jnp.zeros((HEAD_DIM, width), BF16)]
    )
    own_columns = own_weight.shape[0]
    prep_count = row_length // PREP_TILE
    key_length = row_length + PREP_TILE

    def row_block(columns):
        return pl.BlockSpec(
            (PREP_TILE, columns), lambda i, *_: (jnp.minimum(i, prep_count - 1), 0)
        )

    def fixed_block(*shape):
        return pl.BlockSpec(shape, lambda i, *_: (0,) * len(shape))

    head_block = pl.BlockSpec((own_heads, PREP_TILE, LANES), lambda i, *_: (0, i, 0))
    attn_in, query_ext, key_ext, value_ext = pl.pallas_call(
        project_kernel,
        grid=(prep_count + 1,),
        in_specs=[
            row_block(width),
            fixed_block(own_columns, width),
            fixed_block(1, width),
            row_block(LANES),
            row_block(LANES),
            row_block(LANES),
            row_block(LANES),
        ],
        out_specs=[
            row_block(width),
            pl.BlockSpec(
                (own_heads, PREP_TILE, LANES), lambda i: (0, jnp.minimum(i, prep_count - 1), 0)
            ),
            head_block,
            head_block,
        ],
        out_shape=[
            jax.ShapeDtypeStruct((row_length, width), BF16),
            jax.ShapeDtypeStruct((own_heads, row_length, LANES), BF16),
            jax.ShapeDtypeStruct((own_heads, key_length, LANES), BF16),
            jax.ShapeDtypeStruct((own_heads, key_length, LANES), BF16),
        ],
        compiler_params=pltpu.CompilerParams(vmem_limit_bytes=VMEM_BYTES),
        cost_estimate=pl.CostEstimate(
            flops=2 * row_length * own_columns * width,
            bytes_accessed=14_000_000,
            transcendentals=0,
        ),
        name="project",
    )(
        row_tokens,
        own_weight,
        gain_rows[:1],
        cos_table,
        sin_table,
        query_mask,
        key_mask,
    )

    query_ext, key_ext, value_ext, out_plane = fence(query_ext, key_ext, value_ext, out_plane)
    out_partners = gather_partners(out_plane)

    def tile_block(columns):
        return pl.BlockSpec(
            (QUERY_TILE, columns), lambda i, *_: (jnp.minimum(i, tile_count - 1), 0)
        )

    head_tile = pl.BlockSpec(
        (own_heads, QUERY_TILE, LANES), lambda i, *_: (0, jnp.minimum(i, tile_count - 1), 0)
    )
    whole_keys = fixed_block(own_heads, key_length, LANES)
    pair_out, extra_out, query_low = pl.pallas_call(
        attend_kernel,
        grid_spec=pltpu.PrefetchScalarGridSpec(
            num_scalar_prefetch=3,
            grid=(tile_count,),
            in_specs=[head_tile, whole_keys, whole_keys],
            out_specs=[tile_block(LANES), tile_block(LANES), head_tile],
        ),
        out_shape=[
            jax.ShapeDtypeStruct((row_length, LANES), BF16),
            jax.ShapeDtypeStruct((row_length, LANES), BF16),
            jax.ShapeDtypeStruct((own_heads, row_length, LANES), BF16),
        ],
        compiler_params=pltpu.CompilerParams(vmem_limit_bytes=VMEM_BYTES),
        cost_estimate=pl.CostEstimate(
            flops=2 * own_heads * row_length * row_length * LANES,
            bytes_accessed=12_000_000,
            transcendentals=0,
        ),
        name="attend",
    )(tile_starts, tile_steps, pad_at, query_ext, key_ext, value_ext)

    fenced = fence(pair_out, extra_out, query_low, *out_partners)
    pair_out, extra_out, query_low = fenced[:3]
    out_blocks = gather_cores(fenced[3:])
    full_ao, full_fo = arrange(
        out_blocks, lax.axis_index("dp"), *column_moves(out_blocks, [width, hidden])
    )
    full_ao = full_ao.reshape(width, width)
    full_fo = full_fo.reshape(width, hidden)

    half_tokens = token_count // 2

    def fold(extra):
        blocks = extra[:, :HEAD_DIM].reshape(seq_count, 2, half_tokens, HEAD_DIM)
        return jnp.concatenate([blocks[:, 0], blocks[:, 1]], axis=-1)

    def unfold(folded):
        return jnp.concatenate([folded[:, :, :HEAD_DIM], folded[:, :, HEAD_DIM:]], axis=1)

    packed = jnp.concatenate(
        [pair_out.reshape(seq_count, token_count, LANES), fold(extra_out)], axis=1
    )
    packed = lax.all_to_all(packed, "seq", 0, 0, tiled=True)
    attn_low = jnp.concatenate([packed[:, :token_count], unfold(packed[:, token_count:])], axis=-1)
    attn_low = jnp.transpose(attn_low, (1, 0, 2)).reshape(token_count, width)

    inputs = tokens.astype(F32)
    residual = inputs + apply_rows(attn_low, full_ao)
    normed_two, spread_two = norm_forward(residual)
    ffn_in = (normed_two * gain_rows[1]).astype(BF16)
    projected = apply_rows(ffn_in, full_up)
    inner_part = projected[:, :hidden]
    gate_part = projected[:, hidden:]
    activated = gelu_value(inner_part)
    mid_low = (activated * gate_part).astype(BF16)
    layer_out = (residual + apply_rows(mid_low, full_fo)).astype(BF16)
    grad_mid = jnp.dot(cotangent, full_fo, preferred_element_type=F32)
    grad_proj = jnp.concatenate(
        [grad_mid * gate_part * gelu_slope(inner_part), grad_mid * activated], axis=1
    ).astype(BF16)
    grad_ffn_in = jnp.dot(grad_proj, full_up, preferred_element_type=F32)
    grad_norm_two, _ = norm_backward(grad_ffn_in, normed_two, spread_two, gain_rows[1])
    grad_resid = cotangent.astype(F32) + grad_norm_two
    grad_out_attn = grad_resid.astype(BF16)
    grad_attn = jnp.dot(grad_out_attn, full_ao, preferred_element_type=F32).astype(BF16)

    grad_blocks = jnp.transpose(
        grad_attn.reshape(token_count, seq_count, own_width), (1, 0, 2)
    )
    folded = grad_blocks[:, :, LANES:].reshape(seq_count, 2, half_tokens, HEAD_DIM)
    packed_back = jnp.concatenate(
        [grad_blocks[:, :, :LANES], jnp.concatenate([folded[:, 0], folded[:, 1]], axis=-1)], axis=1
    )
    packed_back = lax.all_to_all(packed_back, "seq", 0, 0, tiled=True)

    pack_width = up_parts * width + width + hidden
    pair_count = dp_count // 2
    block_rows = seq_count * ao_rows
    core = lax.axis_index("dp") & 1
    operands = (grad_proj, ffn_in, grad_out_attn, attn_low, cotangent, mid_low)
    half_block = pl.BlockSpec((pair_count // 2, block_rows, pack_width), lambda i: (i, 0, 0))
    send_terms, keep_terms = pl.pallas_call(
        terms_kernel,
        grid=(2,),
        in_specs=[pl.BlockSpec(memory_space=pltpu.SMEM)]
        + [pl.BlockSpec(operand.shape, lambda i: (0, 0)) for operand in operands],
        out_specs=[half_block, half_block],
        out_shape=[jax.ShapeDtypeStruct((pair_count, block_rows, pack_width), BF16)] * 2,
        compiler_params=pltpu.CompilerParams(vmem_limit_bytes=VMEM_BYTES),
        cost_estimate=pl.CostEstimate(
            flops=2 * token_count * width * pack_width,
            bytes_accessed=13_000_000,
            transcendentals=0,
        ),
        name="terms",
    )(core[None], *operands)
    send_terms, packed_back, roots = fence(send_terms, packed_back, roots)
    roots = lax.all_gather(roots, ("dp", "seq"), axis=0, tiled=True)
    pair_blocks = lows(pair_sums(send_terms, keep_terms))
    grad_pair = packed_back[:, :token_count]
    grad_extra = packed_back[:, token_count:]
    grad_pair = grad_pair.reshape(row_length, LANES)
    grad_extra = unfold(grad_extra).reshape(row_length, HEAD_DIM)
    grad_extra = jnp.pad(grad_extra, ((0, 0), (0, LANES - HEAD_DIM)))
    fenced = fence(grad_pair, grad_extra, *pair_blocks)
    grad_pair, grad_extra, pair_blocks = fenced[0], fenced[1], fenced[2:]
    plane_blocks = [pair_blocks[0]] + [
        exchange(block, "dp", 2 * k) for k, block in enumerate(pair_blocks) if k
    ]

    finish_count = prep_count

    def finish_block(columns):
        return pl.BlockSpec(
            (PREP_TILE, columns), lambda i, *_: (jnp.maximum(i - tile_count, 0), 0)
        )

    grad_qkv = pl.pallas_call(
        attend_back_kernel,
        grid_spec=pltpu.PrefetchScalarGridSpec(
            num_scalar_prefetch=3,
            grid=(tile_count + finish_count,),
            in_specs=[
                head_tile,
                tile_block(LANES),
                tile_block(LANES),
                tile_block(LANES),
                tile_block(LANES),
                whole_keys,
                whole_keys,
                finish_block(LANES),
                finish_block(LANES),
            ],
            out_specs=finish_block(own_columns),
            scratch_shapes=[
                pltpu.VMEM((own_heads, row_length, LANES), F32),
                pltpu.VMEM((own_heads, key_length, LANES), F32),
                pltpu.VMEM((own_heads, key_length, LANES), F32),
            ],
        ),
        out_shape=jax.ShapeDtypeStruct((row_length, own_columns), BF16),
        compiler_params=pltpu.CompilerParams(vmem_limit_bytes=VMEM_BYTES),
        cost_estimate=pl.CostEstimate(
            flops=5 * own_heads * row_length * row_length * LANES,
            bytes_accessed=15_000_000,
            transcendentals=0,
        ),
        name="attend_back",
    )(
        tile_starts,
        tile_steps,
        pad_at,
        query_low,
        pair_out,
        extra_out,
        grad_pair,
        grad_extra,
        key_ext,
        value_ext,
        cos_table,
        sin_table,
    )
    fenced = fence(grad_qkv, *plane_blocks)
    grad_qkv = fenced[0]
    plane_sum = add_blocks(fenced[1:]).astype(BF16).reshape(seq_count, ao_rows, pack_width)
    seq_blocks = by_distance(plane_sum, "seq")
    far_sum = add_blocks([seq_blocks[2], exchange(seq_blocks[3], "seq", 1)]).astype(BF16)
    near_sum = add_blocks([seq_blocks[0], exchange(seq_blocks[1], "seq", 1)])
    summed = add_blocks([near_sum, exchange(far_sum, "seq", 2)])
    low_sum = summed.astype(BF16)
    term_plane = gather_plane(low_sum, by_steps=True)
    summed_ao = summed[:, up_parts * width : (up_parts + 1) * width]
    summed_fo = summed[:, (up_parts + 1) * width :]

    qkv_term = outer_sum(grad_qkv, attn_in)[: 3 * own_width].astype(BF16)
    qkv_rows = own_width // dp_count
    qkv_term = qkv_term.reshape(3, pair_count, 2, qkv_rows, width)
    qkv_halves = [
        lax.dynamic_index_in_dim(qkv_term, side, 2, keepdims=False) for side in (1 - core, core)
    ]
    qkv_sum = add_partners(lows(pair_sums(*qkv_halves, axis=1)), "dp", 2).astype(BF16)
    qkv_plane = gather_plane(qkv_sum)
    input_term = jnp.dot(grad_qkv, back_weight, preferred_element_type=F32).astype(BF16)
    input_term, roots = fence(input_term, roots, qkv_plane, term_plane)[:2]
    qkv_blocks = gather_cores(gather_partners(qkv_plane))
    term_partners = gather_partners(term_plane)
    grad_attn_in = lax.psum_scatter(input_term, "seq", scatter_dimension=0, tiled=True).astype(F32)
    normed_one, spread_one = norm_forward(inputs)
    grad_norm_one, _ = norm_backward(grad_attn_in, normed_one, spread_one, gain_rows[0])
    grad_input = grad_resid + grad_norm_one

    def select(count, size):
        places = jnp.arange(-(-count // 16) * 16, dtype=jnp.int32)[:, None]
        wanted = jnp.where(places < count, dev_at * count + places, -1)
        return (wanted == jnp.arange(size, dtype=jnp.int32)[None, :]).astype(BF16)

    select_in = select(stat_r_in.shape[1], width)
    select_fo = select(stat_r_fo.shape[0], hidden)
    [whole_qkv] = arrange(
        qkv_blocks,
        lax.axis_index("dp"),
        [(3, seq_count, dp_count, qkv_rows, width)],
        half_moves(qkv_blocks, [((slice(None), part), 0, (part, "half", "place")) for part in range(3)]),
    )
    whole_qkv = whole_qkv.reshape(3 * width, width)
    low_qkv = lax.dynamic_slice_in_dim(whole_qkv, dev_at * in_rows, in_rows, 0)
    *stacked, qkv_columns = refresh(
        0, whole_qkv, low_qkv, 0, select_in, stat_l_in, stat_r_in, root_l_in, roots, 0, w_in, []
    )
    fenced = fence(stacked, *term_partners)
    stacked, term_blocks = fenced[0], gather_cores(fenced[1:])
    whole_shape = (dp_count, seq_count, ao_rows)
    cut = (slice(None), slice(None))
    whole_up, whole_ao, whole_fo = arrange(
        term_blocks,
        lax.axis_index("dp"),
        [(up_parts,) + whole_shape + (width,), whole_shape + (width,), whole_shape + (hidden,)],
        half_moves(
            term_blocks,
            [
                (cut + (slice(part * width, (part + 1) * width),), 0, (part, "place", "half"))
                for part in range(up_parts)
            ]
            + [
                (cut + (slice(up_parts * width, (up_parts + 1) * width),), 1, ("place", "half")),
                (cut + (slice((up_parts + 1) * width, pack_width),), 2, ("place", "half")),
            ],
        ),
    )
    whole_up = whole_up.reshape(up_parts * width, width)
    whole_ao = whole_ao.reshape(width, width)
    whole_fo = whole_fo.reshape(width, hidden)
    low_up = lax.dynamic_slice_in_dim(whole_up, dev_at * in_rows, in_rows, 0)
    left_ao, right_stat_ao, new_ao, _ = refresh(
        0,
        whole_ao,
        low_sum,
        up_parts * width,
        select_in,
        stat_l_ao[None],
        stat_r_ao[None],
        root_l_ao[None],
        roots,
        2,
        w_ao[None],
        [],
    )
    left_fo, right_stat_fo, fo_parts, _ = refresh(
        0,
        whole_fo,
        low_sum,
        (up_parts + 1) * width,
        select_fo,
        stat_l_fo[None],
        stat_r_fo[None],
        root_l_fo[None],
        roots,
        -3 * width,
        w_fo[None],
        [],
    )
    update_first = fo_parts[0].reshape(ao_rows, all_count, root_rows)
    update_rest = fo_parts[1].reshape(ao_rows, all_count, root_rows)[:, :, :fo_rest]
    update_rest += fo_parts[2].reshape(ao_rows, all_count, root_rows)[:, :, fo_rest:]
    update = jnp.concatenate([update_first, update_rest], axis=2).reshape(ao_rows, hidden)
    new_fo = w_fo - SHAMPOO_RATE * update
    *stacked, up_columns = refresh(
        1, whole_up, low_up, 0, select_in, stat_l_in, stat_r_in, root_l_in, roots, 1, w_in, stacked
    )
    new_left_in, new_right_in, new_in = stacked

    def gain_gradient(weight, columns, gain):
        own_weight_columns = lax.dynamic_slice_in_dim(weight, dev_at * gain_cols, gain_cols, 1)
        products = jnp.transpose(own_weight_columns).astype(F32) * columns[:gain_cols]
        own_gain = lax.dynamic_slice_in_dim(gain, dev_at * gain_cols, gain_cols)
        return jnp.sum(products, axis=1) / own_gain

    summed_gains = jnp.stack(
        [
            gain_gradient(full_qkv, qkv_columns, gain_rows[0]),
            gain_gradient(full_up, up_columns, gain_rows[1]),
        ]
    )
    new_moment = 0.9 * gain_moment + 0.1 * summed_gains
    new_second = 0.999 * gain_second + 0.001 * summed_gains * summed_gains
    new_gains = norm_gains - ADAM_RATE * new_moment / (jnp.sqrt(new_second) + 1e-08)
    return (
        layer_out,
        grad_input,
        jnp.stack([low_qkv, low_up]).astype(F32),
        summed_ao,
        summed_fo,
        summed_gains,
        new_moment,
        new_second,
        new_gains,
        new_left_in,
        new_right_in,
        left_ao[0],
        right_stat_ao[0],
        left_fo[0],
        right_stat_fo[0],
        new_in,
        new_ao[0],
        new_fo,
    )


def body(tokens, *others):
    seq_count, dp_count = lax.axis_size("seq"), lax.axis_size("dp")
    token_count, width = tokens.shape
    row_length = token_count * seq_count
    by_heads = (
        width // HEAD_DIM == 3 * seq_count
        and dp_count & (dp_count - 1) == 0
        and seq_count & (seq_count - 1) == 0
        and row_length % QUERY_TILE == 0
        and token_count == PREP_TILE
        and dp_count == 8
        and seq_count == 4
        and others[3].shape[1] == 3 * others[4].shape[0]
        and others[5].shape[1] == 1152
        and others[1].shape[1] == 8
    )
    return head_body(tokens, *others) if by_heads else sequence_body(tokens, *others)


def solution(mesh):
    in_specs = (
        P(("dp", "seq"), None),
        P(("dp", "seq"), None),
        P("dp", None),
        P("dp"),
        P(None, ("dp", "seq"), None),
        P(("dp", "seq"), None),
        P(("dp", "seq"), None),
        P(None, ("dp", "seq")),
        P(None, ("dp", "seq")),
        P(None, ("dp", "seq")),
        P(None, ("dp", "seq"), None),
        P(None, ("dp", "seq"), None),
        P(("dp", "seq"), None),
        P(("dp", "seq"), None),
        P(("dp", "seq"), None),
        P(("dp", "seq"), None),
        P(None, ("dp", "seq"), None),
        P(None, ("dp", "seq"), None),
        P(("dp", "seq"), None),
        P(("dp", "seq"), None),
        P(("dp", "seq"), None),
        P(("dp", "seq"), None),
    )
    out_specs = (
        P(("dp", "seq"), None),
        P(("dp", "seq"), None),
        P(None, ("dp", "seq"), None),
        P(("dp", "seq"), None),
        P(("dp", "seq"), None),
        P(None, ("dp", "seq")),
        P(None, ("dp", "seq")),
        P(None, ("dp", "seq")),
        P(None, ("dp", "seq")),
        P(None, ("dp", "seq"), None),
        P(None, ("dp", "seq"), None),
        P(("dp", "seq"), None),
        P(("dp", "seq"), None),
        P(("dp", "seq"), None),
        P(("dp", "seq"), None),
        P(None, ("dp", "seq"), None),
        P(("dp", "seq"), None),
        P(("dp", "seq"), None),
    )
    return jax.shard_map(body, mesh=mesh, in_specs=in_specs, out_specs=out_specs, check_vma=False)
```

```python
import functools
import math

import jax
import jax.numpy as jnp
from jax import lax
from jax.experimental import pallas as pl
from jax.experimental.pallas import tpu as pltpu
from jax.sharding import PartitionSpec as P

HEAD_DIM = 64


NORM_EPS = 1e-05
ROPE_THETA = 160000.0
SCORE_SCALE = 0.125
MASK_FILL = -1e30
ADAM_RATE = 0.2
SHAMPOO_RATE = 1.0
HIGHEST = lax.Precision.HIGHEST


def norm_forward(values):
    center = values - jnp.mean(values, axis=-1, keepdims=True)
    inv_spread = lax.rsqrt(jnp.mean(center * center, axis=-1, keepdims=True) + NORM_EPS)
    return (center * inv_spread, inv_spread)


def norm_backward(grad_out, normed, inv_spread, gain_row):
    scaled = grad_out * gain_row
    inner_term = (
        scaled
        - jnp.mean(scaled, axis=-1, keepdims=True)
        - normed * jnp.mean(scaled * normed, axis=-1, keepdims=True)
    )
    return (inner_term * inv_spread, jnp.sum(grad_out * normed, axis=0))


def gelu_value(inputs):
    return 0.5 * inputs * (1.0 + lax.erf(inputs * (1.0 / math.sqrt(2.0))))


def gelu_slope(inputs):
    cumulative = 0.5 * (1.0 + lax.erf(inputs * (1.0 / math.sqrt(2.0))))
    return cumulative + inputs * jnp.exp(-0.5 * inputs * inputs) * (1.0 / math.sqrt(2.0 * math.pi))


def rotate(values, cos_table, sin_table):
    half_dim = values.shape[-1] // 2
    turned = jnp.concatenate([-values[..., half_dim:], values[..., :half_dim]], axis=-1)
    return values * cos_table + turned * sin_table


def unrotate(gradient, cos_table, sin_table):
    half_dim = gradient.shape[-1] // 2
    shifted = gradient * sin_table
    back_turn = jnp.concatenate([shifted[..., half_dim:], -shifted[..., :half_dim]], axis=-1)
    return gradient * cos_table + back_turn


def rope_tables(within):
    freq_index = jnp.arange(0, HEAD_DIM, 2, dtype=jnp.float32)
    inverse = 1.0 / jnp.power(ROPE_THETA, freq_index / HEAD_DIM)
    angles = within.astype(jnp.float32)[:, None] * inverse[None, :]
    angles = jnp.concatenate([angles, angles], axis=-1)
    return (jnp.cos(angles), jnp.sin(angles))


def doc_tables(lengths_row, pad_count, row_length):
    doc_order = jnp.arange(lengths_row.shape[0], dtype=jnp.int32)
    doc_ends = jnp.sum(
        jnp.where(doc_order[:, None] >= doc_order[None, :], lengths_row[None, :], 0), axis=1
    )
    starts = doc_ends - lengths_row
    places = jnp.arange(row_length, dtype=jnp.int32)
    segment = jnp.sum((places[:, None] >= doc_ends[None, :]).astype(jnp.int32), axis=1)
    doc_ids = jnp.arange(lengths_row.shape[0], dtype=jnp.int32)
    doc_begin = jnp.sum(jnp.where(segment[:, None] == doc_ids[None, :], starts[None, :], 0), axis=1)
    is_valid = places < row_length - pad_count
    return (segment, places - doc_begin, is_valid)


def apply_rows(activations, weight):
    return lax.dot_general(
        activations, weight, (((1,), (1,)), ((), ())), preferred_element_type=jnp.float32
    )


def outer_sum(grad_rows, act_rows):
    return lax.dot_general(
        grad_rows, act_rows, (((0,), (0,)), ((), ())), preferred_element_type=jnp.float32
    )


def sequence_body(
    tokens,
    cotangent,
    doc_lengths,
    pad_counts,
    w_in,
    w_ao,
    w_fo,
    norm_gains,
    gain_moment,
    gain_second,
    stat_l_in,
    stat_r_in,
    stat_l_ao,
    stat_r_ao,
    stat_l_fo,
    stat_r_fo,
    root_l_in,
    root_r_in,
    root_l_ao,
    root_r_ao,
    root_l_fo,
    root_r_fo,
):
    token_count, model_width = tokens.shape
    head_count = model_width // HEAD_DIM
    pair_count = head_count // 2
    pair_width = 2 * HEAD_DIM
    hidden_width = w_fo.shape[1]
    seq_count = lax.axis_size("seq")
    row_length = token_count * seq_count
    first_place = lax.axis_index("seq") * token_count
    segment, within, is_valid = doc_tables(doc_lengths[0], pad_counts[0], row_length)
    own_places = first_place + jnp.arange(token_count, dtype=jnp.int32)
    all_places = jnp.arange(row_length, dtype=jnp.int32)
    own_segment = lax.dynamic_slice_in_dim(segment, first_place, token_count)
    own_within = lax.dynamic_slice_in_dim(within, first_place, token_count)
    allowed = (own_segment[:, None] == segment[None, :]) & (
        is_valid[None, :] | (own_places[:, None] == all_places[None, :])
    )
    cos_table, sin_table = rope_tables(own_within)
    cos_table = cos_table[:, None, :]
    sin_table = sin_table[:, None, :]
    low_weights = (
        w_in.astype(jnp.bfloat16),
        w_ao.astype(jnp.bfloat16),
        w_fo.astype(jnp.bfloat16),
        norm_gains.astype(jnp.bfloat16),
    )
    full_in, full_ao, full_fo, full_gains = (
        lax.all_gather(low_weights[0], ("dp", "seq"), axis=1, tiled=True),
        lax.all_gather(low_weights[1], ("dp", "seq"), axis=0, tiled=True),
        lax.all_gather(low_weights[2], ("dp", "seq"), axis=0, tiled=True),
        lax.all_gather(low_weights[3], ("dp", "seq"), axis=1, tiled=True),
    )
    gain_rows = full_gains.astype(jnp.float32)
    inputs = tokens.astype(jnp.float32)
    normed_one, spread_one = norm_forward(inputs)
    attn_in = (normed_one * gain_rows[0]).astype(jnp.bfloat16)
    qkv_raw = apply_rows(attn_in, full_in[0])
    query_low = (
        rotate(
            qkv_raw[:, :model_width].reshape(token_count, head_count, HEAD_DIM),
            cos_table,
            sin_table,
        )
        .reshape(token_count, model_width)
        .astype(jnp.bfloat16)
    )
    key_low = (
        rotate(
            qkv_raw[:, model_width : 2 * model_width].reshape(token_count, head_count, HEAD_DIM),
            cos_table,
            sin_table,
        )
        .reshape(token_count, model_width)
        .astype(jnp.bfloat16)
    )
    value_low = qkv_raw[:, 2 * model_width :].astype(jnp.bfloat16)
    keys_all, values_all = (
        lax.all_gather(key_low, "seq", axis=0, tiled=True),
        lax.all_gather(value_low, "seq", axis=0, tiled=True),
    )

    def pair_slice(matrix, pair_index):
        return lax.dynamic_slice_in_dim(matrix, pair_index * pair_width, pair_width, 1).reshape(
            matrix.shape[0], 2, HEAD_DIM
        )

    def pair_scores(query_pair, key_pair, allow_mask):
        raw_scores = (
            jnp.einsum("thd,khd->htk", query_pair, key_pair, preferred_element_type=jnp.float32)
            * SCORE_SCALE
        )
        return jnp.where(allow_mask[None], raw_scores, MASK_FILL)

    def forward_pair(loop_carry, pair_index):
        scores = pair_scores(
            pair_slice(query_low, pair_index), pair_slice(keys_all, pair_index), allowed
        )
        row_max = jnp.max(scores, axis=-1, keepdims=True)
        exponent = jnp.exp(scores - row_max)
        row_sum = jnp.sum(exponent, axis=-1, keepdims=True)
        weights_low = (exponent / row_sum).astype(jnp.bfloat16)
        attended = jnp.einsum(
            "htk,khd->thd",
            weights_low,
            pair_slice(values_all, pair_index),
            preferred_element_type=jnp.float32,
        )
        return (
            loop_carry,
            (attended.reshape(token_count, pair_width), (row_max + jnp.log(row_sum))[..., 0]),
        )

    unused, (attended_pairs, log_norms) = lax.scan(forward_pair, 0, jnp.arange(pair_count))
    attn_low = (
        jnp.transpose(attended_pairs, (1, 0, 2))
        .reshape(token_count, model_width)
        .astype(jnp.bfloat16)
    )
    residual = inputs + apply_rows(attn_low, full_ao)
    normed_two, spread_two = norm_forward(residual)
    ffn_in = (normed_two * gain_rows[1]).astype(jnp.bfloat16)
    projected = apply_rows(ffn_in, full_in[1])
    inner_part = projected[:, :hidden_width]
    gate_part = projected[:, hidden_width:]
    activated = gelu_value(inner_part)
    mid_low = (activated * gate_part).astype(jnp.bfloat16)
    layer_out = (residual + apply_rows(mid_low, full_fo)).astype(jnp.bfloat16)
    back_in, back_ao, back_fo, back_gains = (
        lax.all_gather(low_weights[0], ("dp", "seq"), axis=1, tiled=True),
        lax.all_gather(low_weights[1], ("dp", "seq"), axis=0, tiled=True),
        lax.all_gather(low_weights[2], ("dp", "seq"), axis=0, tiled=True),
        lax.all_gather(low_weights[3], ("dp", "seq"), axis=1, tiled=True),
    )
    back_rows = back_gains.astype(jnp.float32)
    grad_fo_w = outer_sum(cotangent, mid_low)
    grad_mid = jnp.dot(cotangent, back_fo, preferred_element_type=jnp.float32)
    grad_proj = jnp.concatenate(
        [grad_mid * gate_part * gelu_slope(inner_part), grad_mid * activated], axis=1
    ).astype(jnp.bfloat16)
    grad_ffn_w = outer_sum(grad_proj, ffn_in)
    grad_ffn_in = jnp.dot(grad_proj, back_in[1], preferred_element_type=jnp.float32)
    grad_norm_two, grad_gain_two = norm_backward(grad_ffn_in, normed_two, spread_two, back_rows[1])
    grad_resid = cotangent.astype(jnp.float32) + grad_norm_two
    grad_out_attn = grad_resid.astype(jnp.bfloat16)
    grad_ao_w = outer_sum(grad_out_attn, attn_low)
    grad_attn = jnp.dot(grad_out_attn, back_ao, preferred_element_type=jnp.float32).astype(
        jnp.bfloat16
    )

    def query_side_grads(pair_index):
        query_pair = pair_slice(query_low, pair_index)
        key_pair = pair_slice(keys_all, pair_index)
        value_pair = pair_slice(values_all, pair_index)
        grad_pair = pair_slice(grad_attn, pair_index)
        scores = pair_scores(query_pair, key_pair, allowed)
        softmax_out = jnp.exp(scores - log_norms[pair_index][..., None])
        grad_weights = jnp.einsum(
            "thd,khd->htk", grad_pair, value_pair, preferred_element_type=jnp.float32
        )
        delta_row = jnp.sum(softmax_out * grad_weights, axis=-1, keepdims=True)
        grad_scores = (softmax_out * (grad_weights - delta_row)).astype(jnp.bfloat16)
        grad_query = (
            jnp.einsum("htk,khd->thd", grad_scores, key_pair, preferred_element_type=jnp.float32)
            * SCORE_SCALE
        )
        return (query_pair, grad_pair, softmax_out, grad_scores, grad_query, delta_row)

    def backward_pair(loop_carry, pair_index):
        query_pair, grad_pair, softmax_out, grad_scores, grad_query, delta_row = query_side_grads(
            pair_index
        )
        grad_key = (
            jnp.einsum("htk,thd->khd", grad_scores, query_pair, preferred_element_type=jnp.float32)
            * SCORE_SCALE
        )
        grad_value = jnp.einsum(
            "htk,thd->khd",
            softmax_out.astype(jnp.bfloat16),
            grad_pair,
            preferred_element_type=jnp.float32,
        )
        return (
            loop_carry,
            (
                grad_query.reshape(token_count, pair_width),
                grad_key.reshape(row_length, pair_width),
                grad_value.reshape(row_length, pair_width),
            ),
        )

    unused, (grad_query_pairs, grad_key_parts, grad_value_parts) = lax.scan(
        backward_pair, 0, jnp.arange(pair_count)
    )
    grad_key_pairs, grad_value_pairs = (
        lax.psum_scatter(
            grad_key_parts.astype(jnp.bfloat16), "seq", scatter_dimension=1, tiled=True
        ).astype(jnp.float32),
        lax.psum_scatter(
            grad_value_parts.astype(jnp.bfloat16), "seq", scatter_dimension=1, tiled=True
        ).astype(jnp.float32),
    )

    def heads_of(pairs_array):
        return jnp.transpose(pairs_array, (1, 0, 2)).reshape(token_count, head_count, HEAD_DIM)

    grad_qkv = jnp.concatenate(
        [
            unrotate(heads_of(grad_query_pairs), cos_table, sin_table).reshape(
                token_count, model_width
            ),
            unrotate(heads_of(grad_key_pairs), cos_table, sin_table).reshape(
                token_count, model_width
            ),
            heads_of(grad_value_pairs).reshape(token_count, model_width),
        ],
        axis=1,
    ).astype(jnp.bfloat16)
    grad_qkv_w = outer_sum(grad_qkv, attn_in)
    grad_attn_in = jnp.dot(grad_qkv, back_in[0], preferred_element_type=jnp.float32)
    grad_norm_one, grad_gain_one = norm_backward(grad_attn_in, normed_one, spread_one, back_rows[0])
    grad_input = grad_resid + grad_norm_one
    w_terms = jnp.stack([grad_qkv_w, grad_ffn_w])
    gain_terms = jnp.stack([grad_gain_one, grad_gain_two])
    summed_in, summed_ao, summed_fo, summed_gains = (
        lax.psum_scatter(w_terms, ("dp", "seq"), scatter_dimension=1, tiled=True),
        lax.psum_scatter(grad_ao_w, ("dp", "seq"), scatter_dimension=0, tiled=True),
        lax.psum_scatter(grad_fo_w, ("dp", "seq"), scatter_dimension=0, tiled=True),
        lax.psum_scatter(gain_terms, ("dp", "seq"), scatter_dimension=1, tiled=True),
    )
    new_moment = 0.9 * gain_moment + 0.1 * summed_gains
    new_second = 0.999 * gain_second + 0.001 * summed_gains * summed_gains
    new_gains = norm_gains - ADAM_RATE * new_moment / (jnp.sqrt(new_second) + 1e-08)
    whole_in, whole_ao, whole_fo = (
        lax.all_gather(summed_in.astype(jnp.bfloat16), ("dp", "seq"), axis=1, tiled=True).astype(
            summed_in.dtype
        ),
        lax.all_gather(summed_ao.astype(jnp.bfloat16), ("dp", "seq"), axis=0, tiled=True).astype(
            summed_ao.dtype
        ),
        lax.all_gather(summed_fo.astype(jnp.bfloat16), ("dp", "seq"), axis=0, tiled=True).astype(
            summed_fo.dtype
        ),
    )
    dev_index = lax.axis_index(("dp", "seq"))

    def refresh(grad_shard, grad_full, stat_left, stat_right, root_right):
        col_count = stat_right.shape[1]
        new_left = 0.5 * stat_left + 0.5 * jnp.einsum(
            "arn,amn->arm", grad_shard, grad_full, precision=HIGHEST
        )
        full_cols = lax.dynamic_slice_in_dim(grad_full, dev_index * col_count, col_count, 2)
        new_right = 0.5 * stat_right + 0.5 * jnp.einsum(
            "amc,amn->acn", full_cols, grad_full, precision=HIGHEST
        )
        applied = jnp.einsum("amn,acn->amc", grad_full, root_right, precision=HIGHEST)
        return (new_left, new_right, applied)

    left_in, right_in, applied_in = refresh(summed_in, whole_in, stat_l_in, stat_r_in, root_r_in)
    left_ao, right_ao, applied_ao = refresh(
        summed_ao[None], whole_ao[None], stat_l_ao[None], stat_r_ao[None], root_r_ao[None]
    )
    left_fo, right_fo, applied_fo = refresh(
        summed_fo[None], whole_fo[None], stat_l_fo[None], stat_r_fo[None], root_r_fo[None]
    )
    product_in, product_ao, product_fo = (
        lax.all_gather(applied_in.astype(jnp.bfloat16), ("dp", "seq"), axis=2, tiled=True).astype(
            applied_in.dtype
        ),
        lax.all_gather(applied_ao.astype(jnp.bfloat16), ("dp", "seq"), axis=2, tiled=True).astype(
            applied_ao.dtype
        ),
        lax.all_gather(applied_fo.astype(jnp.bfloat16), ("dp", "seq"), axis=2, tiled=True).astype(
            applied_fo.dtype
        ),
    )
    new_w_in = w_in - SHAMPOO_RATE * jnp.einsum(
        "arm,amn->arn", root_l_in, product_in, precision=HIGHEST
    )
    new_w_ao = (
        w_ao
        - SHAMPOO_RATE
        * jnp.einsum("arm,amn->arn", root_l_ao[None], product_ao, precision=HIGHEST)[0]
    )
    new_w_fo = (
        w_fo
        - SHAMPOO_RATE
        * jnp.einsum("arm,amn->arn", root_l_fo[None], product_fo, precision=HIGHEST)[0]
    )
    return (
        layer_out,
        grad_input,
        summed_in,
        summed_ao,
        summed_fo,
        summed_gains,
        new_moment,
        new_second,
        new_gains,
        left_in,
        right_in,
        left_ao[0],
        right_ao[0],
        left_fo[0],
        right_fo[0],
        new_w_in,
        new_w_ao,
        new_w_fo,
    )


QUERY_TILE = 480
ROW_ALIGN = 16
KEY_STEP = 512
KEY_ALIGN = 128
PREP_TILE = 480
LANES = 128
REFRESH_ROWS = 768
ROOT_SPLIT = 640
MASK_BIT = -(2.0**100)
NO_MAX = -3e38
BF16 = jnp.bfloat16
F32 = jnp.float32
VMEM_BYTES = 56 * 2**20


def dot_rows(left, right):
    return lax.dot_general(left, right, (((1,), (1,)), ((), ())), preferred_element_type=F32)


def dot_plain(left, right):
    return lax.dot_general(left, right, (((1,), (0,)), ((), ())), preferred_element_type=F32)


def dot_first(left, right):
    return lax.dot_general(left, right, (((0,), (0,)), ((), ())), preferred_element_type=F32)


def lane_index(rows):
    return lax.broadcasted_iota(jnp.int32, (rows, LANES), 1)


def three_pieces(column):
    first = column.astype(BF16).astype(F32)
    second = (column - first).astype(BF16).astype(F32)
    return first, second, column - first - second


def with_pieces(values, column, lane, at):
    one, two, three = three_pieces(column)
    return jnp.where(
        lane == at, one, jnp.where(lane == at + 1, two, jnp.where(lane == at + 2, three, values))
    ).astype(BF16)


def project_kernel(
    tokens, weight, gain, cosine, sine, query_mask, key_mask, attn_in, query, key, value
):
    step = pl.program_id(0)
    last = pl.num_programs(0) - 1
    own_heads = query.shape[0]
    rows = tokens.shape[0]
    lane = lane_index(rows)
    low_lanes = lane < HEAD_DIM

    @pl.when(step < last)
    def compute():
        normed = norm_forward(tokens[...].astype(F32))[0]
        low = (normed * gain[...]).astype(BF16)
        attn_in[...] = low
        raw = dot_rows(low, weight[...])
        first_half = lane % HEAD_DIM < HEAD_DIM // 2
        ones = jnp.where(lane < HEAD_DIM + 3, 1.0, 0.0)
        for head in range(own_heads):
            both = raw[:, head * LANES : (head + 1) * LANES]
            turned = jnp.where(
                first_half,
                -pltpu.roll(both, LANES - HEAD_DIM // 2, 1),
                pltpu.roll(both, HEAD_DIM // 2, 1),
            )
            both = both * cosine[...] + turned * sine[...]
            query[head] = jnp.where(
                low_lanes, both * SCORE_SCALE, query_mask[...].astype(F32)
            ).astype(BF16)
            key[head] = jnp.where(
                low_lanes, pltpu.roll(both, HEAD_DIM, 1), key_mask[...].astype(F32)
            ).astype(BF16)
            at = own_heads + head // 2
            pair = raw[:, at * LANES : (at + 1) * LANES]
            if head % 2:
                pair = pltpu.roll(pair, HEAD_DIM, 1)
            value[head] = jnp.where(low_lanes, pair, ones).astype(BF16)

    @pl.when(step == last)
    def pad():
        blocked = jnp.where(
            low_lanes,
            0.0,
            jnp.where(lane < HEAD_DIM + 8, MASK_BIT, jnp.where(lane < HEAD_DIM + 11, 1.0, 0.0)),
        ).astype(BF16)
        for head in range(own_heads):
            key[head] = blocked
            value[head] = jnp.zeros((rows, LANES), BF16)


def attend_kernel(
    start_at, step_count, pad_from, query, key, value, pair_out, extra_out, query_out
):
    tile = pl.program_id(0)
    own_heads, rows, _ = query.shape
    lane = lane_index(rows)
    low_lanes = lane < HEAD_DIM
    place = tile * rows + lax.broadcasted_iota(jnp.int32, (rows, 1), 0)
    padded = place >= pad_from[0]
    own_rows = pl.ds(pl.multiple_of(tile * rows, ROW_ALIGN), rows)
    maxima, totals = [], []
    for head in range(own_heads):
        products = query[head].astype(F32) * key[head, own_rows, :].astype(F32)
        self_score = jnp.sum(jnp.where(low_lanes, products, 0.0), axis=1, keepdims=True)
        maxima.append(jnp.where(padded, self_score, NO_MAX))
        totals.append(jnp.where(padded, value[head, own_rows, :].astype(F32), 0.0))
    first = start_at[tile] * KEY_ALIGN

    def step(index, carry):
        maxima, totals = carry
        at = pl.ds(pl.multiple_of(first + index * KEY_STEP, KEY_ALIGN), KEY_STEP)
        new_maxima, new_totals = [], []
        for head in range(own_heads):
            scores = dot_rows(query[head], key[head, at, :])
            row_max = jnp.maximum(maxima[head], jnp.max(scores, axis=1, keepdims=True))
            weights = jnp.exp(scores - row_max).astype(BF16)
            new_totals.append(
                totals[head] * jnp.exp(maxima[head] - row_max)
                + dot_plain(weights, value[head, at, :])
            )
            new_maxima.append(row_max)
        return new_maxima, new_totals

    maxima, totals = lax.fori_loop(0, step_count[tile], step, (maxima, totals))
    outs = []
    for head in range(own_heads):
        row_sum = totals[head][:, HEAD_DIM : HEAD_DIM + 1]
        outs.append(jnp.where(low_lanes, totals[head] * (1.0 / row_sum), 0.0))
        query_out[head] = with_pieces(
            query[head].astype(F32), -(maxima[head] + jnp.log(row_sum)), lane, HEAD_DIM + 8
        )
    pair_out[...] = (outs[0] + pltpu.roll(outs[1], HEAD_DIM, 1)).astype(BF16)
    extra_out[...] = outs[2].astype(BF16)


def attend_back_kernel(
    start_at,
    step_count,
    pad_from,
    query,
    pair_out,
    extra_out,
    grad_pair,
    grad_extra,
    key,
    value,
    cosine,
    sine,
    grads,
    grad_query,
    grad_key,
    grad_value,
):
    tile = pl.program_id(0)
    own_heads, rows, _ = query.shape
    tile_count = grad_query.shape[1] // rows

    @pl.when(tile == 0)
    def clear():
        grad_key[...] = jnp.zeros_like(grad_key)
        grad_value[...] = jnp.zeros_like(grad_value)

    @pl.when(tile < tile_count)
    def accumulate():
        lane = lane_index(rows)
        low_lanes = lane < HEAD_DIM
        own_rows = pl.ds(pl.multiple_of(tile * rows, ROW_ALIGN), rows)
        first = start_at[tile] * KEY_ALIGN
        pair = grad_pair[...].astype(F32)
        extra = grad_extra[...].astype(F32)
        pair_product = pair * pair_out[...].astype(F32)
        products = [
            jnp.where(low_lanes, pair_product, 0.0),
            jnp.where(low_lanes, 0.0, pair_product),
            extra * extra_out[...].astype(F32),
        ]
        incoming = [pair, pltpu.roll(pair, HEAD_DIM, 1), extra]
        grads_out = []
        for head in range(own_heads):
            own = jnp.where(low_lanes, incoming[head], 0.0)
            delta = jnp.sum(products[head], axis=1, keepdims=True)
            grads_out.append(with_pieces(own, -delta, lane, HEAD_DIM))

        def step(index, carry):
            at = pl.ds(pl.multiple_of(first + index * KEY_STEP, KEY_ALIGN), KEY_STEP)
            sums = []
            for head in range(own_heads):
                keys = key[head, at, :]
                probs = jnp.exp(dot_rows(keys, query[head]))
                grad_scores = (probs * dot_rows(value[head, at, :], grads_out[head])).astype(BF16)
                grad_value[head, at, :] += dot_plain(probs.astype(BF16), grads_out[head])
                grad_key[head, at, :] += dot_plain(grad_scores, query[head])
                sums.append(carry[head] + dot_first(grad_scores, keys))
            return sums

        zeros = [jnp.zeros((rows, LANES), F32) for _ in range(own_heads)]
        sums = lax.fori_loop(0, step_count[tile], step, zeros)
        for head in range(own_heads):
            grad_query[head, own_rows, :] = sums[head]

        @pl.when((tile + 1) * rows > pad_from[0])
        def self_terms():
            place = tile * rows + lax.broadcasted_iota(jnp.int32, (rows, 1), 0)
            padded = place >= pad_from[0]
            for head in range(own_heads):
                keys = key[head, own_rows, :].astype(F32)
                queries = query[head].astype(F32)
                outs = grads_out[head].astype(F32)
                counted = low_lanes | (lane >= HEAD_DIM + 8)
                score = jnp.sum(jnp.where(counted, queries * keys, 0.0), axis=1, keepdims=True)
                prob = jnp.where(padded, jnp.exp(jnp.where(padded, score, 0.0)), 0.0)
                grad_prob = jnp.sum(
                    outs * value[head, own_rows, :].astype(F32), axis=1, keepdims=True
                )
                grad_score = (prob * grad_prob).astype(BF16).astype(F32)
                low_prob = prob.astype(BF16).astype(F32)
                grad_query[head, own_rows, :] += grad_score * jnp.where(low_lanes, keys, 0.0)
                grad_key[head, own_rows, :] += grad_score * queries
                grad_value[head, own_rows, :] += low_prob * outs

    @pl.when(tile >= tile_count)
    def finish():
        size = grads.shape[0]
        at = pl.ds(pl.multiple_of((tile - tile_count) * size, ROW_ALIGN), size)
        lane = lane_index(size)
        low_lanes = lane < HEAD_DIM
        first_half = lane % HEAD_DIM < HEAD_DIM // 2
        values, turns = [], []
        for head in range(own_heads):
            both = jnp.where(
                low_lanes,
                grad_query[head, at, :] * SCORE_SCALE,
                pltpu.roll(grad_key[head, at, :], HEAD_DIM, 1),
            )
            shifted = both * sine[...]
            turned = jnp.where(
                first_half,
                pltpu.roll(shifted, LANES - HEAD_DIM // 2, 1),
                -pltpu.roll(shifted, HEAD_DIM // 2, 1),
            )
            turns.append(both * cosine[...] + turned)
            values.append(jnp.where(low_lanes, grad_value[head, at, :], 0.0))
        swapped = pltpu.roll(turns[1], HEAD_DIM, 1)
        grads[:, :LANES] = jnp.where(low_lanes, turns[0], swapped).astype(BF16)
        grads[:, LANES : 2 * LANES] = jnp.where(low_lanes, turns[2], turns[0]).astype(BF16)
        grads[:, 2 * LANES : 3 * LANES] = jnp.where(low_lanes, swapped, turns[2]).astype(BF16)
        base = own_heads * LANES
        grads[:, base : base + LANES] = (values[0] + pltpu.roll(values[1], HEAD_DIM, 1)).astype(
            BF16
        )
        grads[:, base + LANES : base + 2 * LANES] = values[2].astype(BF16)


def refresh_kernel(
    full, own, select, stat_left, stat_right, root_left, right_root, weight, *refs, kept, own_at, root_at
):
    new_left, new_right, new_weight, columns, total = refs[kept:]
    step = pl.program_id(0)
    chosen = select.shape[0]
    count = new_right.shape[-2]
    own_rows = own[:, own_at : own_at + full.shape[1]]
    outer = dot_rows(jnp.concatenate([select[...], own_rows]), full[...])
    columns[...] = outer[:chosen]
    new_left[0] = 0.5 * stat_left[0] + 0.5 * outer[chosen:]
    left = jnp.concatenate([outer[:chosen].astype(BF16), root_left[0].astype(BF16)])
    product = dot_plain(left, full[...])

    @pl.when(step == 0)
    def begin():
        total[...] = product

    @pl.when(step > 0)
    def add():
        total[...] += product

    @pl.when(step == pl.num_programs(0) - 1)
    def finish():
        new_right[0] = 0.5 * stat_right[0] + 0.5 * total[:count, :]
        product = total[chosen:, :].astype(BF16)
        if root_at is None:
            new_weight[0] = weight[0] - SHAMPOO_RATE * dot_plain(product, right_root[...])
        else:
            size = product.shape[1]
            rest = root_at + size
            new_weight[0] = dot_rows(product, right_root[:, root_at:rest])
            new_weight[1] = dot_rows(
                product[:, :ROOT_SPLIT], right_root[:, rest : rest + ROOT_SPLIT]
            )
            new_weight[2] = dot_rows(
                product[:, ROOT_SPLIT:], right_root[:, rest : rest + size - ROOT_SPLIT]
            )


def refresh(
    at, full, own, own_at, select, stat_left, stat_right, root_left, roots, root_at, weight, previous
):
    in_dim, out_dim = full.shape
    chunk = REFRESH_ROWS
    rows, count, chosen = own.shape[0], stat_right.shape[1], select.shape[0]

    def by_chunk(rows):
        return pl.BlockSpec((1, rows, chunk), lambda i: (at, 0, i))

    def whole(*shape):
        return pl.BlockSpec(shape, lambda i: (0,) * len(shape))

    def stacked(array):
        return pl.BlockSpec((1,) + array.shape[1:], lambda i: (at, 0, 0))

    kept = [pl.BlockSpec(memory_space=pl.ANY)] * len(previous)
    square = root_at >= 0
    if square:
        new_weight = stacked(weight), weight.shape
        root_block = pl.BlockSpec((out_dim, out_dim), lambda i: (0, root_at))
    else:
        parts = (3, rows, roots.shape[0])
        new_weight = whole(*parts), parts
        root_block = whole(*roots.shape)
    return pl.pallas_call(
        functools.partial(
            refresh_kernel,
            kept=len(previous),
            own_at=own_at,
            root_at=None if square else -root_at,
        ),
        grid=(in_dim // chunk,),
        in_specs=[
            pl.BlockSpec((chunk, out_dim), lambda i: (i, 0)),
            whole(*own.shape),
            whole(*select.shape),
            by_chunk(rows),
            stacked(stat_right),
            by_chunk(rows),
            root_block,
            stacked(weight),
        ]
        + kept,
        out_specs=[
            by_chunk(rows),
            stacked(stat_right),
            new_weight[0],
            pl.BlockSpec((chosen, chunk), lambda i: (0, i)),
        ],
        out_shape=[
            jax.ShapeDtypeStruct(stat_left.shape, F32),
            jax.ShapeDtypeStruct(stat_right.shape, F32),
            jax.ShapeDtypeStruct(new_weight[1], F32),
            jax.ShapeDtypeStruct((chosen, in_dim), F32),
        ],
        scratch_shapes=[pltpu.VMEM((chosen + rows, out_dim), F32)],
        input_output_aliases={8 + i: i for i in range(len(previous))},
        compiler_params=pltpu.CompilerParams(vmem_limit_bytes=VMEM_BYTES),
        cost_estimate=pl.CostEstimate(
            flops=4 * (chosen + rows) * in_dim * out_dim,
            bytes_accessed=2 * in_dim * out_dim + 12 * rows * in_dim + 2 * out_dim * out_dim,
            transcendentals=0,
        ),
        name="refresh",
    )(
        full,
        own,
        select,
        stat_left,
        stat_right,
        root_left,
        roots,
        weight,
        *previous,
    )


def exchange(values, axis, offset):
    size = lax.axis_size(axis)
    return lax.ppermute(values, axis, [(i, i ^ offset) for i in range(size)])


def arrange_kernel(own_at, *refs, count, moves):
    blocks, outs, sems = refs[:count], refs[count:-1], refs[-1]
    copies = []
    for index, (number, offset, source, which, target) in enumerate(moves):
        place = own_at[0] ^ offset
        start = blocks[number].at[source] if source else blocks[number]
        end = outs[which].at[tuple(place if at == "place" else at for at in target)]
        copies.append(pltpu.make_async_copy(start, end, sems.at[index]))
    for copy in copies:
        copy.start()
    for copy in copies:
        copy.wait()


def arrange(blocks, own_at, shapes, moves):
    count = len(blocks)
    return pl.pallas_call(
        functools.partial(arrange_kernel, count=count, moves=moves),
        in_specs=[pl.BlockSpec(memory_space=pltpu.SMEM)]
        + [pl.BlockSpec(memory_space=pl.ANY)] * count,
        out_specs=[pl.BlockSpec(memory_space=pltpu.VMEM)] * len(shapes),
        scratch_shapes=[pltpu.SemaphoreType.DMA((len(moves),))],
        out_shape=[jax.ShapeDtypeStruct(shape, blocks[0].dtype) for shape in shapes],
        compiler_params=pltpu.CompilerParams(vmem_limit_bytes=VMEM_BYTES),
        cost_estimate=pl.CostEstimate(
            flops=0, bytes_accessed=2 * count * blocks[0].size * 2, transcendentals=0
        ),
        name="arrange",
    )(own_at[None], *blocks)


def terms_kernel(
    core, grad_proj, ffn_in, grad_out, attended, cotangent, middle, send, keep
):
    step = pl.program_id(0)
    groups, rows, _ = send.shape
    width = ffn_in.shape[1]
    chunk = 2 * groups * rows
    pieces = [(grad_proj, part * width, ffn_in) for part in range(grad_proj.shape[1] // width)]
    pieces += [(grad_out, 0, attended), (cotangent, 0, middle)]
    first = 0
    for left, offset, right in pieces:
        columns = pl.ds(pl.multiple_of(offset + step * chunk, KEY_ALIGN), chunk)
        term = dot_first(left[:, columns], right[...]).astype(BF16)
        last = first + right.shape[1]
        for own in range(2):

            @pl.when(core[0] == own)
            def store():
                for group in range(groups):
                    for side, out in ((own, keep), (1 - own, send)):
                        at = (2 * group + side) * rows
                        out[group, :, first:last] = term[at : at + rows]

        first = last


def gather_plane(values, by_steps=False):
    last = None if by_steps else exchange(values, "seq", 3)
    far = exchange(values, "seq", 2)
    last = exchange(far, "seq", 1) if by_steps else last
    blocks = [values, exchange(values, "seq", 1), far, last]
    shape = (len(blocks),) + values.shape
    moves = [(k, k, (), 0, ("place",)) for k in range(len(blocks))]
    return arrange(blocks, lax.axis_index("seq"), [shape], moves)[0]


def gather_near(plane):
    half = plane.shape[0] // 2
    left, right = plane[:half], plane[half:]
    left_two, right_four = exchange(left, "dp", 2), exchange(right, "dp", 4)
    return [left, right, left_two, exchange(right, "dp", 2), exchange(left, "dp", 4), right_four]


def gather_far(near):
    return [*near, exchange(near[2], "dp", 4), exchange(near[5], "dp", 2)]


def gather_partners(plane):
    return gather_far(gather_near(plane))


def gather_cores(even):
    blocks = []
    for k in range(0, len(even), 2):
        blocks += [*even[k : k + 2], *(exchange(block, "dp", 1) for block in even[k : k + 2])]
    return blocks


def half_moves(blocks, cuts):
    half = blocks[0].shape[0]
    moves = []
    for number in range(len(blocks)):
        rows = slice(number % 2 * half, (number % 2 + 1) * half)
        for source, which, target in cuts:
            end = tuple(rows if at == "half" else at for at in target)
            moves.append((number, number // 2, source, which, end))
    return moves


def column_moves(blocks, widths):
    shapes, cuts, first = [], [], 0
    half, rows, _ = blocks[0].shape
    for which, width in enumerate(widths):
        shapes.append((len(blocks) // 2, 2 * half, rows, width))
        source = (slice(None), slice(None), slice(first, first + width))
        cuts.append((source, which, ("place", "half")))
        first += width
    return shapes, half_moves(blocks, cuts)


def fence(*values):
    return lax.optimization_barrier(values)


def add_blocks(blocks):
    total = blocks[0].astype(F32)
    for block in blocks[1:]:
        total = total + block.astype(F32)
    return total


def pair_sums(send, keep, axis=0):
    came = exchange(send, "dp", 1)
    own_at = lax.axis_index("dp") >> 1
    return [
        add_blocks(
            [
                lax.dynamic_index_in_dim(side, own_at ^ k, axis, keepdims=False)
                for side in (keep, came)
            ]
        )
        for k in range(keep.shape[axis])
    ]


def swap_blocks(blocks, axis, unit):
    came = [exchange(blocks[k], axis, k * unit) for k in range(len(blocks) - 1, 0, -1)]
    return [blocks[0]] + came[::-1]


def add_partners(blocks, axis, unit):
    return add_blocks(swap_blocks(blocks, axis, unit))


def lows(blocks):
    return [block.astype(BF16) for block in blocks]


def by_distance(values, axis):
    own_at = lax.axis_index(axis)
    return [
        lax.dynamic_index_in_dim(values, own_at ^ k, 0, keepdims=False)
        for k in range(values.shape[0])
    ]


def head_body(
    tokens,
    cotangent,
    doc_lengths,
    pad_counts,
    w_in,
    w_ao,
    w_fo,
    norm_gains,
    gain_moment,
    gain_second,
    stat_l_in,
    stat_r_in,
    stat_l_ao,
    stat_r_ao,
    stat_l_fo,
    stat_r_fo,
    root_l_in,
    root_r_in,
    root_l_ao,
    root_r_ao,
    root_l_fo,
    root_r_fo,
):
    token_count, width = tokens.shape
    hidden = w_fo.shape[1]
    seq_count, dp_count = lax.axis_size("seq"), lax.axis_size("dp")
    all_count = seq_count * dp_count
    row_length = token_count * seq_count
    seq_at = lax.axis_index("seq")
    dev_at = lax.axis_index(("dp", "seq"))
    head_count = width // HEAD_DIM
    own_heads = head_count // seq_count
    own_width = own_heads * HEAD_DIM
    in_rows = w_in.shape[1]
    ao_rows = w_ao.shape[0]
    gain_cols = norm_gains.shape[1]

    gain_lanes = jnp.zeros((in_rows, LANES), BF16).at[:2, :gain_cols].set(norm_gains.astype(BF16))
    up_parts = in_rows // ao_rows
    row_tokens = lax.all_gather(tokens, "seq", axis=0, tiled=True)
    qkv_blocks = gather_cores(
        gather_partners(gather_plane(jnp.concatenate([w_in[0].astype(BF16), gain_lanes], axis=1)))
    )
    full_qkv, gain_blocks = arrange(
        qkv_blocks, lax.axis_index("dp"), *column_moves(qkv_blocks, [width, LANES])
    )
    full_qkv = full_qkv.reshape(all_count * in_rows, width)
    gain_rows = (
        jnp.transpose(gain_blocks[:, :, :2, :gain_cols], (2, 0, 1, 3)).reshape(2, width).astype(F32)
    )
    full_up = lax.all_gather(w_in[1].astype(BF16), ("dp", "seq"), axis=0, tiled=True)
    out_weights = jnp.concatenate([w_ao.astype(BF16), w_fo.astype(BF16)], axis=1)
    row_tokens, out_weights = fence(row_tokens, out_weights)
    out_plane = gather_plane(out_weights)
    root_rows = stat_r_in.shape[1]
    fo_rest = root_r_fo.shape[0] - root_rows
    rest_rows = root_r_fo[root_rows:].astype(BF16)
    wrapped = jnp.concatenate(
        [
            rest_rows[:, :ROOT_SPLIT],
            jnp.pad(rest_rows[:, ROOT_SPLIT:], ((0, 0), (0, 2 * ROOT_SPLIT - hidden))),
        ]
    )
    roots = jnp.concatenate(
        [
            root_r_in[0].astype(BF16),
            root_r_in[1].astype(BF16),
            root_r_ao.astype(BF16),
            root_r_fo[:root_rows].astype(BF16),
            wrapped,
        ],
        axis=1,
    )

    lengths = doc_lengths[0]
    segment, within, is_valid = doc_tables(lengths, pad_counts[0], row_length)
    pad_from = row_length - pad_counts[0]
    doc_ids = jnp.arange(lengths.shape[0], dtype=jnp.int32)
    places = jnp.arange(row_length, dtype=jnp.int32)
    doc_begin = places - within
    doc_end = doc_begin + jnp.sum(
        jnp.where(segment[:, None] == doc_ids[None, :], lengths[None, :], 0), axis=1
    )
    freq_index = jnp.arange(0, HEAD_DIM, 2, dtype=F32)
    inverse = 1.0 / jnp.power(ROPE_THETA, freq_index / HEAD_DIM)
    angles = within.astype(F32)[:, None] * inverse[None, :]
    copies = LANES // (HEAD_DIM // 2)
    cos_table = jnp.concatenate([jnp.cos(angles)] * copies, axis=1)
    sin_table = jnp.concatenate([jnp.sin(angles)] * copies, axis=1)
    lane = jnp.arange(LANES, dtype=jnp.int32)
    in_doc = lane[None, :] - HEAD_DIM == segment[:, None]
    mask_lanes = (lane >= HEAD_DIM) & (lane < HEAD_DIM + 8)
    one_lanes = (lane >= HEAD_DIM + 8) & (lane < HEAD_DIM + 11)
    query_mask = in_doc.astype(BF16)
    key_mask = jnp.where(
        mask_lanes[None, :] & ~(in_doc & is_valid[:, None]),
        MASK_BIT,
        jnp.where(one_lanes[None, :], 1.0, 0.0),
    ).astype(BF16)
    tile_starts = doc_begin[::QUERY_TILE] // KEY_ALIGN
    tile_ends = jnp.minimum(doc_end[QUERY_TILE - 1 :: QUERY_TILE], pad_from)
    tile_steps = jnp.maximum(-((tile_starts * KEY_ALIGN - tile_ends) // KEY_STEP), 0)
    tile_count = row_length // QUERY_TILE
    pad_at = pad_from[None]

    qkv_heads = lax.dynamic_slice_in_dim(
        full_qkv.reshape(3, head_count, HEAD_DIM, width), seq_at * own_heads, own_heads, 1
    )
    own_weight = jnp.concatenate(
        [
            jnp.transpose(qkv_heads[:2], (1, 0, 2, 3)).reshape(2 * own_width, width),
            qkv_heads[2].reshape(own_width, width),
            jnp.zeros((HEAD_DIM, width), BF16),
        ]
    )
    back_weight = jnp.concatenate(
        [qkv_heads.reshape(3 * own_width, width), jnp.zeros((HEAD_DIM, width), BF16)]
    )
    own_columns = own_weight.shape[0]
    prep_count = row_length // PREP_TILE
    key_length = row_length + PREP_TILE

    def row_block(columns):
        return pl.BlockSpec(
            (PREP_TILE, columns), lambda i, *_: (jnp.minimum(i, prep_count - 1), 0)
        )

    def fixed_block(*shape):
        return pl.BlockSpec(shape, lambda i, *_: (0,) * len(shape))

    head_block = pl.BlockSpec((own_heads, PREP_TILE, LANES), lambda i, *_: (0, i, 0))
    attn_in, query_ext, key_ext, value_ext = pl.pallas_call(
        project_kernel,
        grid=(prep_count + 1,),
        in_specs=[
            row_block(width),
            fixed_block(own_columns, width),
            fixed_block(1, width),
            row_block(LANES),
            row_block(LANES),
            row_block(LANES),
            row_block(LANES),
        ],
        out_specs=[
            row_block(width),
            pl.BlockSpec(
                (own_heads, PREP_TILE, LANES), lambda i: (0, jnp.minimum(i, prep_count - 1), 0)
            ),
            head_block,
            head_block,
        ],
        out_shape=[
            jax.ShapeDtypeStruct((row_length, width), BF16),
            jax.ShapeDtypeStruct((own_heads, row_length, LANES), BF16),
            jax.ShapeDtypeStruct((own_heads, key_length, LANES), BF16),
            jax.ShapeDtypeStruct((own_heads, key_length, LANES), BF16),
        ],
        compiler_params=pltpu.CompilerParams(vmem_limit_bytes=VMEM_BYTES),
        cost_estimate=pl.CostEstimate(
            flops=2 * row_length * own_columns * width,
            bytes_accessed=14_000_000,
            transcendentals=0,
        ),
        name="project",
    )(
        row_tokens,
        own_weight,
        gain_rows[:1],
        cos_table,
        sin_table,
        query_mask,
        key_mask,
    )

    query_ext, key_ext, value_ext, out_plane = fence(query_ext, key_ext, value_ext, out_plane)
    out_partners = gather_partners(out_plane)

    def tile_block(columns):
        return pl.BlockSpec(
            (QUERY_TILE, columns), lambda i, *_: (jnp.minimum(i, tile_count - 1), 0)
        )

    head_tile = pl.BlockSpec(
        (own_heads, QUERY_TILE, LANES), lambda i, *_: (0, jnp.minimum(i, tile_count - 1), 0)
    )
    whole_keys = fixed_block(own_heads, key_length, LANES)
    pair_out, extra_out, query_low = pl.pallas_call(
        attend_kernel,
        grid_spec=pltpu.PrefetchScalarGridSpec(
            num_scalar_prefetch=3,
            grid=(tile_count,),
            in_specs=[head_tile, whole_keys, whole_keys],
            out_specs=[tile_block(LANES), tile_block(LANES), head_tile],
        ),
        out_shape=[
            jax.ShapeDtypeStruct((row_length, LANES), BF16),
            jax.ShapeDtypeStruct((row_length, LANES), BF16),
            jax.ShapeDtypeStruct((own_heads, row_length, LANES), BF16),
        ],
        compiler_params=pltpu.CompilerParams(vmem_limit_bytes=VMEM_BYTES),
        cost_estimate=pl.CostEstimate(
            flops=2 * own_heads * row_length * row_length * LANES,
            bytes_accessed=12_000_000,
            transcendentals=0,
        ),
        name="attend",
    )(tile_starts, tile_steps, pad_at, query_ext, key_ext, value_ext)

    fenced = fence(pair_out, extra_out, query_low, *out_partners)
    pair_out, extra_out, query_low = fenced[:3]
    out_blocks = gather_cores(fenced[3:])
    full_ao, full_fo = arrange(
        out_blocks, lax.axis_index("dp"), *column_moves(out_blocks, [width, hidden])
    )
    full_ao = full_ao.reshape(width, width)
    full_fo = full_fo.reshape(width, hidden)

    half_tokens = token_count // 2

    def fold(extra):
        blocks = extra[:, :HEAD_DIM].reshape(seq_count, 2, half_tokens, HEAD_DIM)
        return jnp.concatenate([blocks[:, 0], blocks[:, 1]], axis=-1)

    def unfold(folded):
        return jnp.concatenate([folded[:, :, :HEAD_DIM], folded[:, :, HEAD_DIM:]], axis=1)

    packed = jnp.concatenate(
        [pair_out.reshape(seq_count, token_count, LANES), fold(extra_out)], axis=1
    )
    packed = lax.all_to_all(packed, "seq", 0, 0, tiled=True)
    attn_low = jnp.concatenate([packed[:, :token_count], unfold(packed[:, token_count:])], axis=-1)
    attn_low = jnp.transpose(attn_low, (1, 0, 2)).reshape(token_count, width)

    inputs = tokens.astype(F32)
    residual = inputs + apply_rows(attn_low, full_ao)
    normed_two, spread_two = norm_forward(residual)
    ffn_in = (normed_two * gain_rows[1]).astype(BF16)
    projected = apply_rows(ffn_in, full_up)
    inner_part = projected[:, :hidden]
    gate_part = projected[:, hidden:]
    activated = gelu_value(inner_part)
    mid_low = (activated * gate_part).astype(BF16)
    layer_out = (residual + apply_rows(mid_low, full_fo)).astype(BF16)
    grad_mid = jnp.dot(cotangent, full_fo, preferred_element_type=F32)
    grad_proj = jnp.concatenate(
        [grad_mid * gate_part * gelu_slope(inner_part), grad_mid * activated], axis=1
    ).astype(BF16)
    grad_ffn_in = jnp.dot(grad_proj, full_up, preferred_element_type=F32)
    grad_norm_two, _ = norm_backward(grad_ffn_in, normed_two, spread_two, gain_rows[1])
    grad_resid = cotangent.astype(F32) + grad_norm_two
    grad_out_attn = grad_resid.astype(BF16)
    grad_attn = jnp.dot(grad_out_attn, full_ao, preferred_element_type=F32).astype(BF16)

    grad_blocks = jnp.transpose(
        grad_attn.reshape(token_count, seq_count, own_width), (1, 0, 2)
    )
    folded = grad_blocks[:, :, LANES:].reshape(seq_count, 2, half_tokens, HEAD_DIM)
    packed_back = jnp.concatenate(
        [grad_blocks[:, :, :LANES], jnp.concatenate([folded[:, 0], folded[:, 1]], axis=-1)], axis=1
    )
    packed_back = lax.all_to_all(packed_back, "seq", 0, 0, tiled=True)

    pack_width = up_parts * width + width + hidden
    pair_count = dp_count // 2
    block_rows = seq_count * ao_rows
    core = lax.axis_index("dp") & 1
    operands = (grad_proj, ffn_in, grad_out_attn, attn_low, cotangent, mid_low)
    half_block = pl.BlockSpec((pair_count // 2, block_rows, pack_width), lambda i: (i, 0, 0))
    send_terms, keep_terms = pl.pallas_call(
        terms_kernel,
        grid=(2,),
        in_specs=[pl.BlockSpec(memory_space=pltpu.SMEM)]
        + [pl.BlockSpec(operand.shape, lambda i: (0, 0)) for operand in operands],
        out_specs=[half_block, half_block],
        out_shape=[jax.ShapeDtypeStruct((pair_count, block_rows, pack_width), BF16)] * 2,
        compiler_params=pltpu.CompilerParams(vmem_limit_bytes=VMEM_BYTES),
        cost_estimate=pl.CostEstimate(
            flops=2 * token_count * width * pack_width,
            bytes_accessed=13_000_000,
            transcendentals=0,
        ),
        name="terms",
    )(core[None], *operands)
    send_terms, packed_back, roots = fence(send_terms, packed_back, roots)
    roots = lax.all_gather(roots, ("dp", "seq"), axis=0, tiled=True)
    pair_blocks = lows(pair_sums(send_terms, keep_terms))
    grad_pair = packed_back[:, :token_count]
    grad_extra = packed_back[:, token_count:]
    grad_pair = grad_pair.reshape(row_length, LANES)
    grad_extra = unfold(grad_extra).reshape(row_length, HEAD_DIM)
    grad_extra = jnp.pad(grad_extra, ((0, 0), (0, LANES - HEAD_DIM)))
    fenced = fence(grad_pair, grad_extra, *pair_blocks)
    grad_pair, grad_extra, pair_blocks = fenced[0], fenced[1], fenced[2:]
    plane_blocks = [pair_blocks[0]] + [
        exchange(block, "dp", 2 * k) for k, block in enumerate(pair_blocks) if k
    ]

    finish_count = prep_count

    def finish_block(columns):
        return pl.BlockSpec(
            (PREP_TILE, columns), lambda i, *_: (jnp.maximum(i - tile_count, 0), 0)
        )

    grad_qkv = pl.pallas_call(
        attend_back_kernel,
        grid_spec=pltpu.PrefetchScalarGridSpec(
            num_scalar_prefetch=3,
            grid=(tile_count + finish_count,),
            in_specs=[
                head_tile,
                tile_block(LANES),
                tile_block(LANES),
                tile_block(LANES),
                tile_block(LANES),
                whole_keys,
                whole_keys,
                finish_block(LANES),
                finish_block(LANES),
            ],
            out_specs=finish_block(own_columns),
            scratch_shapes=[
                pltpu.VMEM((own_heads, row_length, LANES), F32),
                pltpu.VMEM((own_heads, key_length, LANES), F32),
                pltpu.VMEM((own_heads, key_length, LANES), F32),
            ],
        ),
        out_shape=jax.ShapeDtypeStruct((row_length, own_columns), BF16),
        compiler_params=pltpu.CompilerParams(vmem_limit_bytes=VMEM_BYTES),
        cost_estimate=pl.CostEstimate(
            flops=5 * own_heads * row_length * row_length * LANES,
            bytes_accessed=15_000_000,
            transcendentals=0,
        ),
        name="attend_back",
    )(
        tile_starts,
        tile_steps,
        pad_at,
        query_low,
        pair_out,
        extra_out,
        grad_pair,
        grad_extra,
        key_ext,
        value_ext,
        cos_table,
        sin_table,
    )
    fenced = fence(grad_qkv, *plane_blocks)
    grad_qkv = fenced[0]
    plane_sum = add_blocks(fenced[1:]).astype(BF16).reshape(seq_count, ao_rows, pack_width)
    seq_blocks = by_distance(plane_sum, "seq")
    far_sum = add_blocks([seq_blocks[2], exchange(seq_blocks[3], "seq", 1)]).astype(BF16)
    near_sum = add_blocks([seq_blocks[0], exchange(seq_blocks[1], "seq", 1)])
    summed = add_blocks([near_sum, exchange(far_sum, "seq", 2)])
    low_sum = summed.astype(BF16)
    term_plane = gather_plane(low_sum, by_steps=True)
    summed_ao = summed[:, up_parts * width : (up_parts + 1) * width]
    summed_fo = summed[:, (up_parts + 1) * width :]

    qkv_term = outer_sum(grad_qkv, attn_in)[: 3 * own_width].astype(BF16)
    qkv_rows = own_width // dp_count
    qkv_term = qkv_term.reshape(3, pair_count, 2, qkv_rows, width)
    qkv_halves = [
        lax.dynamic_index_in_dim(qkv_term, side, 2, keepdims=False) for side in (1 - core, core)
    ]
    qkv_sum = add_partners(lows(pair_sums(*qkv_halves, axis=1)), "dp", 2).astype(BF16)
    qkv_plane = gather_plane(qkv_sum)
    input_term = jnp.dot(grad_qkv, back_weight, preferred_element_type=F32).astype(BF16)
    input_term, roots = fence(input_term, roots, qkv_plane, term_plane)[:2]
    qkv_blocks = gather_cores(gather_partners(qkv_plane))
    term_partners = gather_partners(term_plane)
    grad_attn_in = lax.psum_scatter(input_term, "seq", scatter_dimension=0, tiled=True).astype(F32)
    normed_one, spread_one = norm_forward(inputs)
    grad_norm_one, _ = norm_backward(grad_attn_in, normed_one, spread_one, gain_rows[0])
    grad_input = grad_resid + grad_norm_one

    def select(count, size):
        places = jnp.arange(-(-count // 16) * 16, dtype=jnp.int32)[:, None]
        wanted = jnp.where(places < count, dev_at * count + places, -1)
        return (wanted == jnp.arange(size, dtype=jnp.int32)[None, :]).astype(BF16)

    select_in = select(stat_r_in.shape[1], width)
    select_fo = select(stat_r_fo.shape[0], hidden)
    [whole_qkv] = arrange(
        qkv_blocks,
        lax.axis_index("dp"),
        [(3, seq_count, dp_count, qkv_rows, width)],
        half_moves(qkv_blocks, [((slice(None), part), 0, (part, "half", "place")) for part in range(3)]),
    )
    whole_qkv = whole_qkv.reshape(3 * width, width)
    low_qkv = lax.dynamic_slice_in_dim(whole_qkv, dev_at * in_rows, in_rows, 0)
    *stacked, qkv_columns = refresh(
        0, whole_qkv, low_qkv, 0, select_in, stat_l_in, stat_r_in, root_l_in, roots, 0, w_in, []
    )
    fenced = fence(stacked, *term_partners)
    stacked, term_blocks = fenced[0], gather_cores(fenced[1:])
    fenced = fence(grad_input, *term_blocks)
    grad_input, term_blocks = fenced[0], fenced[1:]
    whole_shape = (dp_count, seq_count, ao_rows)
    cut = (slice(None), slice(None))
    whole_up, whole_ao, whole_fo = arrange(
        term_blocks,
        lax.axis_index("dp"),
        [(up_parts,) + whole_shape + (width,), whole_shape + (width,), whole_shape + (hidden,)],
        half_moves(
            term_blocks,
            [
                (cut + (slice(part * width, (part + 1) * width),), 0, (part, "place", "half"))
                for part in range(up_parts)
            ]
            + [
                (cut + (slice(up_parts * width, (up_parts + 1) * width),), 1, ("place", "half")),
                (cut + (slice((up_parts + 1) * width, pack_width),), 2, ("place", "half")),
            ],
        ),
    )
    whole_up = whole_up.reshape(up_parts * width, width)
    whole_ao = whole_ao.reshape(width, width)
    whole_fo = whole_fo.reshape(width, hidden)
    low_up = lax.dynamic_slice_in_dim(whole_up, dev_at * in_rows, in_rows, 0)
    left_ao, right_stat_ao, new_ao, _ = refresh(
        0,
        whole_ao,
        low_sum,
        up_parts * width,
        select_in,
        stat_l_ao[None],
        stat_r_ao[None],
        root_l_ao[None],
        roots,
        2,
        w_ao[None],
        [],
    )
    left_fo, right_stat_fo, fo_parts, _ = refresh(
        0,
        whole_fo,
        low_sum,
        (up_parts + 1) * width,
        select_fo,
        stat_l_fo[None],
        stat_r_fo[None],
        root_l_fo[None],
        roots,
        -3 * width,
        w_fo[None],
        [],
    )
    update_first = fo_parts[0].reshape(ao_rows, all_count, root_rows)
    update_rest = fo_parts[1].reshape(ao_rows, all_count, root_rows)[:, :, :fo_rest]
    update_rest += fo_parts[2].reshape(ao_rows, all_count, root_rows)[:, :, fo_rest:]
    update = jnp.concatenate([update_first, update_rest], axis=2).reshape(ao_rows, hidden)
    new_fo = w_fo - SHAMPOO_RATE * update
    *stacked, up_columns = refresh(
        1, whole_up, low_up, 0, select_in, stat_l_in, stat_r_in, root_l_in, roots, 1, w_in, stacked
    )
    new_left_in, new_right_in, new_in = stacked

    def gain_gradient(weight, columns, gain):
        own_weight_columns = lax.dynamic_slice_in_dim(weight, dev_at * gain_cols, gain_cols, 1)
        products = jnp.transpose(own_weight_columns).astype(F32) * columns[:gain_cols]
        own_gain = lax.dynamic_slice_in_dim(gain, dev_at * gain_cols, gain_cols)
        return jnp.sum(products, axis=1) / own_gain

    summed_gains = jnp.stack(
        [
            gain_gradient(full_qkv, qkv_columns, gain_rows[0]),
            gain_gradient(full_up, up_columns, gain_rows[1]),
        ]
    )
    new_moment = 0.9 * gain_moment + 0.1 * summed_gains
    new_second = 0.999 * gain_second + 0.001 * summed_gains * summed_gains
    new_gains = norm_gains - ADAM_RATE * new_moment / (jnp.sqrt(new_second) + 1e-08)
    return (
        layer_out,
        grad_input,
        jnp.stack([low_qkv, low_up]).astype(F32),
        summed_ao,
        summed_fo,
        summed_gains,
        new_moment,
        new_second,
        new_gains,
        new_left_in,
        new_right_in,
        left_ao[0],
        right_stat_ao[0],
        left_fo[0],
        right_stat_fo[0],
        new_in,
        new_ao[0],
        new_fo,
    )


def body(tokens, *others):
    seq_count, dp_count = lax.axis_size("seq"), lax.axis_size("dp")
    token_count, width = tokens.shape
    row_length = token_count * seq_count
    by_heads = (
        width // HEAD_DIM == 3 * seq_count
        and dp_count & (dp_count - 1) == 0
        and seq_count & (seq_count - 1) == 0
        and row_length % QUERY_TILE == 0
        and token_count == PREP_TILE
        and dp_count == 8
        and seq_count == 4
        and others[3].shape[1] == 3 * others[4].shape[0]
        and others[5].shape[1] == 1152
        and others[1].shape[1] == 8
    )
    return head_body(tokens, *others) if by_heads else sequence_body(tokens, *others)


def solution(mesh):
    in_specs = (
        P(("dp", "seq"), None),
        P(("dp", "seq"), None),
        P("dp", None),
        P("dp"),
        P(None, ("dp", "seq"), None),
        P(("dp", "seq"), None),
        P(("dp", "seq"), None),
        P(None, ("dp", "seq")),
        P(None, ("dp", "seq")),
        P(None, ("dp", "seq")),
        P(None, ("dp", "seq"), None),
        P(None, ("dp", "seq"), None),
        P(("dp", "seq"), None),
        P(("dp", "seq"), None),
        P(("dp", "seq"), None),
        P(("dp", "seq"), None),
        P(None, ("dp", "seq"), None),
        P(None, ("dp", "seq"), None),
        P(("dp", "seq"), None),
        P(("dp", "seq"), None),
        P(("dp", "seq"), None),
        P(("dp", "seq"), None),
    )
    out_specs = (
        P(("dp", "seq"), None),
        P(("dp", "seq"), None),
        P(None, ("dp", "seq"), None),
        P(("dp", "seq"), None),
        P(("dp", "seq"), None),
        P(None, ("dp", "seq")),
        P(None, ("dp", "seq")),
        P(None, ("dp", "seq")),
        P(None, ("dp", "seq")),
        P(None, ("dp", "seq"), None),
        P(None, ("dp", "seq"), None),
        P(("dp", "seq"), None),
        P(("dp", "seq"), None),
        P(("dp", "seq"), None),
        P(("dp", "seq"), None),
        P(None, ("dp", "seq"), None),
        P(("dp", "seq"), None),
        P(("dp", "seq"), None),
    )
    return jax.shard_map(body, mesh=mesh, in_specs=in_specs, out_specs=out_specs, check_vma=False)
```
